256 devices in a mesh: seq: 32 (over x, z), head: 8 (over y, core).
Axes of the slice: x: 4, y: 4, z: 8, core: 2. Of those that a mesh axis runs over, the one named last changes fastest.
Arguments:
- x_values: bfloat16 [32768, 8192], P('seq', 'head'), may hold values from -6 to 6
- b_values: bfloat16 [32768, 1024], P('seq', 'head'), may hold values from -6 to 6
- c_values: bfloat16 [32768, 1024], P('seq', 'head'), may hold values from -6 to 6
- z_values: bfloat16 [32768, 8192], P('seq', 'head'), may hold values from -6 to 6
- time_steps: float32 [32768, 128], P('seq', 'head'), may hold values from 0 to 0.35, as said below
- decay_rate: float32 [128], P('head'), may hold values from 0.5 to 2
- skip_gain: float32 [128], P('head'), may hold values from 0.5 to 1.5
- conv_x: bfloat16 [4, 8192], P(None, 'head'), may hold values from -3 to 3
- conv_bc: bfloat16 [2, 4, 1024], P(None, None, 'head'), may hold values from -3 to 3
- norm_gain: float32 [8192], P('head'), may hold values from 0.5 to 13, as said below
- rollout: bfloat16 [32768, 8192], P('seq', 'head'), may hold values from -6 to 6
- seq_spans: int32 [4], replicated, may hold values from 1 to 64, 128 in all
Outputs:
- normed: bfloat16 [32768, 8192], P('seq', 'head')
- rel_error: float32 [32768], P('seq')
The draws below stay inside these ranges and needn't reach their ends.
Inputs may be any that keep to these rules, and one draw needn't show every extreme that they name: `time_steps`: positive step sizes. `norm_gain`: positive gains. `seq_spans`: the spans of all sequences sum to 128.
All inputs are finite; a program needn't handle non-finite values.
Results may differ from the reference program's by a relative error of at most 0.0046.
Values may be sent and summed in bfloat16 or wider, within the bound.
No kernel may reach another device: no remote copies, remote signals or barrier semaphores. Data moves between devices by JAX's collectives and lax.ppermute only.
A program may use at most 128 MiB of HBM per device.

```python
import math
import jax
import jax.numpy as jnp
import numpy as np
from jax import lax

HEADS = 128
HEAD_DIM = 64
STATE = 128
GROUPS = 8
CONV_K = 4
SPAN = 256
INNER_CHANNELS = 8192
SPANS = 128
TOKENS = 32768
SEQS = 4
MOST = 64


def draw_time_steps(key, part):
    key = jax.random.fold_in(key, 11)
    keys = jax.random.split(key, 6)
    length = MOST * SPAN
    fast_share = 0.5
    selector_index = jax.random.uniform(keys[0], (HEADS,))
    slow_base = jnp.exp(jax.random.uniform(keys[1], (HEADS,), minval=jnp.log(0.2), maxval=jnp.log(0.5))) / length
    fast_base = jnp.exp(jax.random.uniform(keys[2], (HEADS,), minval=jnp.log(0.02), maxval=jnp.log(0.06)))
    base = jnp.where(selector_index < fast_share, fast_base, slow_base)
    blocks = jnp.exp(jax.random.uniform(keys[3], (SPANS, 1, HEADS), minval=jnp.log(0.5), maxval=jnp.log(2.0)))
    rough = jax.random.uniform(keys[4], (SPANS, SPAN, HEADS), minval=0.5, maxval=1.5)
    flagged_spots = jax.random.randint(keys[5], (2,), 0, TOKENS)
    slot_offset_within_sequence = jnp.arange(TOKENS)
    element_run_length = jnp.any(slot_offset_within_sequence[:, None] == flagged_spots[None, :], axis=1)
    payload_vector_items = (base[None, None, :] * blocks * rough).reshape(TOKENS, HEADS)
    return jnp.where(element_run_length[:, None], 0.35, payload_vector_items).astype(jnp.float32)


def draw_norm_gain(key, part):
    key = jax.random.fold_in(key, 23)
    head_ids = (jnp.arange(INNER_CHANNELS) // HEAD_DIM).astype(jnp.float32)
    rising = 1.0 + 2.0 * head_ids / (HEADS - 1)
    rough = jax.random.uniform(key, (INNER_CHANNELS,), minval=0.6, maxval=1.4)
    return (rising * rough).astype(jnp.float32)


def block_scale(rng, dims, cuts, smallest, top_value):
    def one(dim, parts):
        draws = jax.random.uniform(jax.random.fold_in(jax.random.fold_in(rng, 6), dim), (parts,), jnp.float32, smallest / len(cuts), top_value / len(cuts))
        return jnp.repeat(jnp.exp(draws), dims[dim] // parts).reshape((-1,) + (1,) * (len(dims) - dim - 1))

    gain = one(*cuts[0])
    for cut in cuts[1:]:
        gain = gain * one(*cut)
    return gain


def split_up(amount, total, most, lean):
    portions = [(1 << 20) // math.isqrt(standing ** lean) + 1 for standing in range(2, amount + 1)]
    surplus, counts = total - most - (amount - 1), [1] * (amount - 1)
    while surplus > 0:
        free = [i for i in range(amount - 1) if counts[i] < most]
        whole, remaining = sum([portions[i] for i in free]), surplus
        for i in free:
            addition = min(most - counts[i], max(1, remaining * portions[i] // whole), surplus)
            counts[i] = counts[i] + addition
            surplus = surplus - addition
    return np.array([most] + counts)


def ragged_sizes(stream_key, amount, total, bound, lean):
    if amount == 2:
        one = jax.random.randint(stream_key, (), max(1, total - bound), min(bound, total - 1) + 1)
        return jnp.stack([one, total - one])
    tallies = jnp.asarray(split_up(amount, total, bound, lean), jnp.int32)
    twos = (amount - 1) // 2
    giver, taker = tallies[1:1 + 2 * twos:2], tallies[2:2 + 2 * twos:2]
    margin = jnp.minimum(giver - 1, bound - taker)
    moved = jax.random.randint(jax.random.fold_in(stream_key, 1), (twos,), 0, 1 << 20) % (margin + 1)
    tallies = tallies.at[1:1 + 2 * twos:2].set(giver - moved).at[2:2 + 2 * twos:2].set(taker + moved)
    return tallies[jax.random.permutation(jax.random.fold_in(stream_key, 2), amount)]


def scatter_about(stream_key, extent, width, most, pieces=(), kind=jnp.bfloat16):
    values = jax.random.normal(stream_key, extent, jnp.float32) * width
    if len(pieces) > 0:
        values = block_scale(stream_key, extent, pieces, -0.22, 0.18) * values
    return jnp.clip(values, min=-most, max=most).astype(kind)


def setup_inputs(seed: int = 0) -> dict:
    streams_of = jax.random.split(jax.random.key(seed), 13)
    x_values = scatter_about(streams_of[0], (TOKENS, INNER_CHANNELS), 1.0, 6.0, ((0, 32), (1, 8)))
    b_values = scatter_about(streams_of[1], (TOKENS, GROUPS * STATE), 1.0, 6.0, ((0, 32), (1, 8)))
    c_values = scatter_about(streams_of[2], (TOKENS, GROUPS * STATE), 1.0, 6.0, ((0, 32), (1, 8)))
    z_values = scatter_about(streams_of[3], (TOKENS, INNER_CHANNELS), 1.0, 6.0, ((0, 32), (1, 8)))
    time_steps = draw_time_steps(jax.random.fold_in(streams_of[12], 71), 0)
    decay_rate = jnp.clip(jnp.exp(math.log(2.0) - 1.3862944 * jax.random.uniform(streams_of[5], (HEADS,), jnp.float32) ** block_scale(streams_of[5], (HEADS,), ((0, 8),), -0.2, 0.2)), 0.5, 2.0)
    skip_gain = jnp.clip(0.5 + 1.0 * jax.random.uniform(streams_of[6], (HEADS,), jnp.float32) ** block_scale(streams_of[6], (HEADS,), ((0, 8),), -0.2, 0.2), 0.5, 1.5)
    conv_x = scatter_about(streams_of[7], (CONV_K, INNER_CHANNELS), CONV_K ** -0.5, 3.0, ((1, 8),))
    conv_bc = scatter_about(streams_of[8], (2, CONV_K, GROUPS * STATE), CONV_K ** -0.5, 3.0, ((2, 8),))
    norm_gain = draw_norm_gain(jax.random.fold_in(streams_of[12], 71), 0)
    rollout = scatter_about(streams_of[10], (TOKENS, INNER_CHANNELS), 1.0, 6.0, ((0, 32), (1, 8)))
    seq_spans = ragged_sizes(streams_of[11], SEQS, SPANS, MOST, 2).astype(jnp.int32)
    return {"x_values": x_values, "b_values": b_values, "c_values": c_values, "z_values": z_values, "time_steps": time_steps, "decay_rate": decay_rate, "skip_gain": skip_gain, "conv_x": conv_x, "conv_bc": conv_bc, "norm_gain": norm_gain, "rollout": rollout, "seq_spans": seq_spans}


def span_tables(seq_spans):
    span_ids = jnp.arange(SPANS, dtype=jnp.int32)
    starts = jnp.cumsum(seq_spans, dtype=jnp.int32) - seq_spans
    first_flags = jnp.any(span_ids[:, None] == starts[None, :], axis=1)
    begin_span = lax.optimization_barrier(jnp.max(jnp.where(span_ids[:, None] >= starts[None, :], starts[None, :], 0), axis=1)).astype(jnp.int32)
    return (first_flags, begin_span)

def causal_conv(payload_vector_items, boundary_rows, weight, slot_offset_within_sequence, begin_token):
    reach = CONV_K - 1
    extended = jnp.concatenate([boundary_rows, payload_vector_items], axis=0)
    count = payload_vector_items.shape[0]
    summed = jnp.zeros(payload_vector_items.shape, jnp.float32)
    for offset in range(CONV_K):
        shifted = extended[reach - offset:reach - offset + count]
        inside = (slot_offset_within_sequence - offset >= begin_token)[:, None]
        summed = summed + jnp.where(inside, shifted.astype(jnp.float32), 0.0) * weight[CONV_K - 1 - offset].astype(jnp.float32)
    return lax.optimization_barrier(jax.nn.silu(summed).astype(jnp.bfloat16))

def edges_of(payload_vector_items):
    blocks = payload_vector_items.reshape(SPANS, SPAN, payload_vector_items.shape[1])
    reach = CONV_K - 1
    return (jnp.concatenate([jnp.zeros((1, reach, payload_vector_items.shape[1]), payload_vector_items.dtype), blocks[:-1, SPAN - reach:]], axis=0), blocks)

def reference(x_values, b_values, c_values, z_values, time_steps, decay_rate, skip_gain, conv_x, conv_bc, norm_gain, rollout, seq_spans):
    first_flags, begin_span = span_tables(seq_spans)
    group_heads = HEADS // GROUPS
    past_only_filter = jnp.arange(SPAN)[:, None] >= jnp.arange(SPAN)[None, :]
    x_edges, x_blocks = edges_of(x_values)
    b_edges, b_blocks = edges_of(b_values)
    c_edges, c_blocks = edges_of(c_values)

    def one_span(state_carry, inputs):
        span_index, x_span, x_edge, b_span, b_edge, c_span, c_edge, z_span, step_span, roll_span = inputs
        slot_offset_within_sequence = span_index * SPAN + jnp.arange(SPAN, dtype=jnp.int32)
        begin_token = begin_span[span_index] * SPAN
        x_conv = causal_conv(x_span, x_edge, conv_x, slot_offset_within_sequence, begin_token)
        b_conv = causal_conv(b_span, b_edge, conv_bc[0], slot_offset_within_sequence, begin_token)
        readout_filter_output = causal_conv(c_span, c_edge, conv_bc[1], slot_offset_within_sequence, begin_token)
        x_heads = x_conv.reshape(SPAN, HEADS, HEAD_DIM).astype(jnp.float32)
        b_groups = b_conv.reshape(SPAN, GROUPS, STATE).astype(jnp.float32)
        readout_groups = readout_filter_output.reshape(SPAN, GROUPS, STATE).astype(jnp.float32)
        rates = -step_span * decay_rate[None, :]
        cumulated = jnp.cumsum(rates, axis=0)
        attention_weights_matrix = jnp.repeat(jnp.einsum('tgn,ugn->gtu', readout_groups, b_groups), group_heads, axis=0)
        spread_log = cumulated.T[:, :, None] - cumulated.T[:, None, :]
        mixing = jnp.where(past_only_filter[None], attention_weights_matrix * jnp.exp(jnp.where(past_only_filter[None], spread_log, 0.0)) * step_span.T[:, None, :], 0.0)
        mixing = lax.optimization_barrier(mixing.astype(jnp.bfloat16)).astype(jnp.float32)
        mixed = jnp.einsum('htu,uhp->thp', mixing, x_heads)
        incoming_sequence_flag = jnp.where(first_flags[span_index], 0.0, state_carry)
        state_read = lax.optimization_barrier(incoming_sequence_flag.astype(jnp.bfloat16)).astype(jnp.float32)
        c_heads = jnp.repeat(readout_groups, group_heads, axis=1)
        mixed = mixed + jnp.exp(cumulated)[:, :, None] * jnp.einsum('thn,hnp->thp', c_heads, state_read)
        b_heads = jnp.repeat(b_groups, group_heads, axis=1)
        weights = jnp.exp(cumulated[-1][None, :] - cumulated) * step_span
        decayed = lax.optimization_barrier((b_heads * weights[:, :, None]).astype(jnp.bfloat16)).astype(jnp.float32)
        span_state = jnp.einsum('uhn,uhp->hnp', decayed, x_heads)
        state_next = jnp.exp(cumulated[-1])[:, None, None] * incoming_sequence_flag + span_state
        mixed = mixed + skip_gain[None, :, None] * x_heads
        gated = mixed * jax.nn.silu(z_span.reshape(SPAN, HEADS, HEAD_DIM).astype(jnp.float32))
        grouped = gated.reshape(SPAN, GROUPS, group_heads * HEAD_DIM)
        square_mean = lax.optimization_barrier(jnp.mean(grouped * grouped, axis=-1, keepdims=True))
        normed = ((grouped * lax.rsqrt(square_mean + 1e-05)).reshape(SPAN, INNER_CHANNELS) * norm_gain[None, :]).astype(jnp.bfloat16)
        roll_float = roll_span.astype(jnp.float32)
        deviation = normed.astype(jnp.float32) - roll_float
        relative = jnp.sqrt(lax.optimization_barrier(jnp.sum(deviation * deviation, axis=1)) / (lax.optimization_barrier(jnp.sum(roll_float * roll_float, axis=1)) + 1e-06))
        return (state_next, (normed, relative))
    inputs = (jnp.arange(SPANS, dtype=jnp.int32), x_blocks, x_edges, b_blocks, b_edges, c_blocks, c_edges, z_values.reshape(SPANS, SPAN, INNER_CHANNELS), time_steps.reshape(SPANS, SPAN, HEADS), rollout.reshape(SPANS, SPAN, INNER_CHANNELS))
    start_state = jnp.zeros((HEADS, STATE, HEAD_DIM), jnp.float32)
    final_state, outputs = lax.scan(one_span, start_state, inputs)
    return (outputs[0].reshape(TOKENS, INNER_CHANNELS), outputs[1].reshape(TOKENS))
```

```python
import functools

import jax
import jax.numpy as jnp
from jax import lax
from jax.experimental import pallas as pl
from jax.experimental.pallas import tpu as pltpu
from jax.sharding import PartitionSpec as P

HEADS = 128
HEAD_DIM = 64
STATE = 128
GROUPS = 8
CONV_K = 4
SPAN = 256
CHUNK = 128
LANES = 256
HALO = 16

F32 = jnp.float32
BF16 = jnp.bfloat16


def parts3(v):
    hi = v.astype(BF16)
    rest = v - hi.astype(F32)
    mid = rest.astype(BF16)
    low = (rest - mid.astype(F32)).astype(BF16)
    return hi, mid, low


def silu_half(h):
    return h + h * jnp.tanh(h)


def mm(a, b):
    return jnp.dot(a, b, preferred_element_type=F32)


def one_hot(lane0, width=LANES):
    r = lax.broadcasted_iota(jnp.int32, (256, width), 0)
    c = lax.broadcasted_iota(jnp.int32, (256, width), 1)
    return jnp.where((r & 127) == (c + lane0) // HEAD_DIM, 1.0, 0.0).astype(BF16)


def span_keep(seq_ref, span):
    start = seq_ref[0] * 0
    fresh = span == start
    for i in range(seq_ref.shape[0] - 1):
        start = start + seq_ref[i]
        fresh = fresh | (span == start)
    return jnp.where(fresh, 0.0, 1.0).astype(F32)


def conv_block(padded_ref, taps):
    rows = padded_ref.shape[0] - 8
    total = padded_ref[pl.ds(5, rows), :] * taps[0:1]
    for k in range(1, CONV_K):
        total = total + padded_ref[pl.ds(5 + k, rows), :] * taps[k : k + 1]
    return silu_half(total)


def conv_ordered(padded_ref, taps):
    per = CHUNK // 8
    shifted = {m: padded_ref[pl.ds(8 + m, 8, stride=per), :] for m in range(1 - CONV_K, per)}
    rows = []
    for j in range(per):
        total = shifted[j + 1 - CONV_K] * taps[0:1]
        for k in range(1, CONV_K):
            total = total + shifted[j + 1 - CONV_K + k] * taps[k : k + 1]
        rows.append(silu_half(total))
    return jnp.concatenate(rows, axis=0)


def turned(v, heads, chunk):
    turn = (128 - heads * chunk) % 128
    return pltpu.roll(v, turn, 1) if turn else v


def split2(v):
    hi = v.astype(BF16)
    return hi, (v - hi.astype(F32)).astype(BF16)


def stack_scales(source, heads, chunks, target):
    for k in range(chunks):
        hi, low = split2(turned(source, heads, k))
        target[k * CHUNK : (k + 1) * CHUNK, 0:128] = hi
        target[k * CHUNK : (k + 1) * CHUNK, 128:256] = low


def chunk_rates(ts_ref, rate_ref, chunks):
    steps = jnp.concatenate([ts_ref[:, k * CHUNK : (k + 1) * CHUNK] for k in range(chunks)], axis=0).T
    return steps, -steps * jnp.concatenate([rate_ref[...]] * chunks, axis=1)


def sum_rates(picks, rates):
    picks = picks.astype(BF16)
    r1, r2, r3 = parts3(rates)
    return mm(picks, r1) + (mm(picks, r2) + mm(picks, r3))


def spread_rows(v, e):
    n = v.shape[0]
    out = mm(jnp.concatenate(parts3(v), axis=0), e[0:128])
    return out[0:n] + (out[n : 2 * n] + out[2 * n : 3 * n])


def chunk_keeps(chunks, seq_ref, rank_ref):
    per_span = SPAN // CHUNK
    first = rank_ref[0] * (chunks // per_span)
    return [None if k % per_span else span_keep(seq_ref, first + k // per_span) for k in range(chunks)]


def fill_padded(padded_ref, src_ref, edge, k, lanes, keep):
    if k == 0:
        halo = edge
    else:
        halo = src_ref[k * CHUNK - HALO : k * CHUNK, lanes].astype(F32)[HALO - 8 :]
    padded_ref[0:8, :] = halo if keep is None else halo * keep
    padded_ref[8 : 8 + CHUNK, :] = src_ref[k * CHUNK : (k + 1) * CHUNK, lanes].astype(F32)


def tail_kernel(x_ref, b_ref, c_ref, out_ref):
    width = x_ref.shape[1]
    out_ref[:, 0:width] = x_ref[...]
    out_ref[:, width : width + STATE] = b_ref[...]
    out_ref[:, width + STATE : width + 2 * STATE] = c_ref[...]


def state_kernel(
    chunks, seq_ref, rank_ref, x_hbm, b_ref, ts_ref, rate_ref, wx_ref, wb_ref,
    end_ref, head_scale_ref, chain_ref, head_ref,
    x_all, padded, order, lhsu, wide, bt, xs, x_sems,
):
    blocks = x_all.shape[0]
    width = blocks * LANES
    heads = ts_ref.shape[0]

    def x_copy(i):
        lanes = pl.ds(pl.multiple_of(i * LANES, LANES), LANES)
        return pltpu.make_async_copy(x_hbm.at[:, lanes], x_all.at[i], x_sems.at[i])

    def start(i, carry):
        x_copy(i).start()
        return carry

    lax.fori_loop(0, blocks, start, 0)
    steps, rates = chunk_rates(ts_ref, rate_ref, chunks)
    t = lax.broadcasted_iota(jnp.int32, (CHUNK + 16, CHUNK), 0)
    u = lax.broadcasted_iota(jnp.int32, (CHUNK + 16, CHUNK), 1)
    after = sum_rates(jnp.where((u > t) | (t >= CHUNK), 1.0, 0.0), rates)
    totals = after[CHUNK : CHUNK + 16]
    j = lax.broadcasted_iota(jnp.int32, (CHUNK, CHUNK), 0)
    k = lax.broadcasted_iota(jnp.int32, (CHUNK, CHUNK), 1)
    later = jnp.where((lax.rem(j, heads) == lax.rem(k, heads)) & (j > k), 1.0, 0.0).astype(BF16)
    t1, t2, t3 = parts3(totals)
    later = mm(t1, later) + (mm(t2, later) + mm(t3, later))
    lane = lax.broadcasted_iota(jnp.int32, (16, 128), 1)
    reached = jnp.ones((16, 128), F32)
    whole = jnp.exp(later + totals)
    for n in range(0, chunks, SPAN // CHUNK):
        keep = span_keep(seq_ref, rank_ref[0] * (chunks * CHUNK // SPAN) + n * CHUNK // SPAN)
        reached = jnp.where(lane < n * heads, reached * keep, reached)
        whole = whole * keep
    scale = jnp.exp(after[0:CHUNK] + later[0:1]) * steps * reached[0:1]
    order[...] = scale
    per = CHUNK // 8
    stack_scales(jnp.concatenate([order[pl.ds(n, 8, stride=per), :] for n in range(per)], axis=0), heads, chunks, lhsu)
    e = one_hot(0, width)
    wide_all = mm(lhsu[...], e)
    for i in range(blocks):
        wide[i] = wide_all[:, i * LANES : (i + 1) * LANES]
    head_scale_ref[...] = mm(jnp.concatenate(split2(scale[0:HALO]), axis=1), e)
    row = lax.broadcasted_iota(jnp.int32, (16, 1), 0)
    p1, p2, p3 = parts3(whole)
    p = jnp.where(row == 0, p1.astype(F32), jnp.where(row == 1, p2.astype(F32), p3.astype(F32)))
    chain_ref[...] = mm(jnp.where(row < 3, p, 0.0).astype(BF16), e[0:128])[0:8]
    taps = wb_ref[0].astype(F32) * 0.5
    none = jnp.zeros((8, 128), F32)

    keeps = chunk_keeps(chunks, seq_ref, rank_ref)
    for k in range(chunks):
        pad = padded.at[k % 4]
        fill_padded(pad, b_ref, none, k, slice(0, STATE), keeps[k])
        v = conv_ordered(pad, taps)
        if k == 0:
            v = jnp.where((lax.broadcasted_iota(jnp.int32, v.shape, 0) & 7) == 0, 0.0, v)
        bt[:, k * CHUNK : (k + 1) * CHUNK] = v.T.astype(BF16)
    head_ref[:, width : width + STATE] = b_ref[0:HALO, :]

    def block(i, carry):
        lane0 = pl.multiple_of(i * LANES, LANES)
        lanes = pl.ds(lane0, LANES)
        x_ref = x_all.at[i]
        weights = wx_ref[:, lanes].astype(F32) * 0.5
        x_copy(i).wait()
        head_ref[:, lanes] = x_ref[0:HALO, :]

        for k in range(chunks):
            toks = slice(k * CHUNK, (k + 1) * CHUNK)
            for part in range(LANES // 128):
                cols = slice(part * 128, (part + 1) * 128)
                pad = padded.at[(2 * k + part) % 4]
                fill_padded(pad, x_ref, none, k, cols, keeps[k])
                v = conv_ordered(pad, weights[:, cols])
                xs[toks, cols] = (v * wide[i, toks, cols]).astype(BF16)
        end_ref[:, lanes] = mm(bt[...], xs[...])
        return carry

    lax.fori_loop(0, blocks, block, 0)


def edge_kernel(
    chunks, seq_ref, rank_ref, edge_ref, head_ref, wx_ref, wbc_ref, scale_ref, end_ref, chain_ref,
    msg_ref, edge_out_ref,
):
    keep = span_keep(seq_ref, rank_ref[0] * (chunks * CHUNK // SPAN))
    width = wx_ref.shape[1]
    b_cols = slice(width, width + STATE)
    edge_out_ref[...] = edge_ref[...]

    def conv(before, block, taps):
        taps = taps.astype(F32) * 0.5
        joined = jnp.concatenate([before.astype(F32)[HALO - 8 :] * keep, block.astype(F32)], axis=0)
        total = joined[5 : 5 + HALO] * taps[0:1]
        for k in range(1, CONV_K):
            total = total + joined[5 + k : 5 + k + HALO] * taps[k : k + 1]
        return silu_half(total)

    bc = conv(edge_ref[:, b_cols], head_ref[:, b_cols], wbc_ref[0])
    bt = jnp.concatenate([bc, jnp.zeros((STATE - HALO, STATE), F32)], axis=0).T[:, 0:HALO].astype(BF16)

    for i in range(width // LANES):
        cols = slice(i * LANES, (i + 1) * LANES)
        v = conv(edge_ref[:, cols], head_ref[:, cols], wx_ref[:, cols])
        xs = (v * scale_ref[:, cols]).astype(BF16)
        state = end_ref[:, cols] + mm(bt, xs)
        both = jnp.concatenate([state, chain_ref[:, cols]], axis=0)
        for part in range(LANES // 128):
            piece = both[:, part * 128 : (part + 1) * 128]
            for nb in range(4):
                own = jnp.concatenate([piece[nb * 32 : (nb + 1) * 32], piece[STATE:]], axis=0)
                msg_ref[(i * (LANES // 128) + part) * 4 + nb] = own.astype(BF16)


def scan_kernel(in_ref, after_ref, out_ref):
    def some(m, carried):
        for n in range(8):
            i = 8 * m + n
            out_ref[i] = carried.astype(BF16)
            block = in_ref[i].astype(F32)
            decay = block[32:33] + (block[33:34] + block[34:35])
            carried = carried * decay + block[0:32]
        return carried

    lax.fori_loop(0, in_ref.shape[0] // 8, some, jnp.zeros((32, 128), F32))


def mix_first(chunks, seq_ref, rank_ref, b_ref, c_ref, edge_ref, wbc_ref, left, bt, cc_ref, padded):
    t = lax.broadcasted_iota(jnp.int32, (CHUNK, CHUNK), 0)
    u = lax.broadcasted_iota(jnp.int32, (CHUNK, CHUNK), 1)
    edges = edge_ref[...].astype(F32)[HALO - 8 :]

    keeps = chunk_keeps(chunks, seq_ref, rank_ref)
    for k in range(chunks):
        toks = slice(k * CHUNK, (k + 1) * CHUNK)
        pair = []
        for i, ref in enumerate((b_ref, c_ref)):
            pad = padded.at[(2 * k + i) % 4]
            fill_padded(pad, ref, edges[:, i * STATE : (i + 1) * STATE], k, slice(0, STATE), keeps[k])
            pair.append(conv_block(pad, wbc_ref[i].astype(F32) * 0.5))
        b, c = pair
        bt[k] = b.T.astype(BF16)
        c = c.astype(BF16)
        cc_ref[toks, :] = c
        left[toks, 128:256] = c
        g = lax.dot_general(c, b.astype(BF16), (((1,), (1,)), ((), ())), preferred_element_type=F32)
        left[toks, 0:128] = jnp.where(u <= t, g, 0.0).astype(BF16)


def mix_kernel(
    chunks, lane_first, seq_ref, rank_ref, x_ref, edge_ref, ts_ref, rate_ref, z_ref, roll_ref, wx_ref, skip_ref, *refs
):
    if lane_first == 0:
        b_ref, c_ref, bc_edge_ref, wbc_ref, a_ref, f_ref, roll_sum_ref, left, bt, cc_ref = refs[:10]
    else:
        left, bt, a_ref, f_ref, roll_sum_ref = refs[:5]
    padded, wide_u, wide_t, part, state, lhsu, lhst, ends_all, rows = refs[-9:]
    heads = skip_ref.shape[1]

    @pl.when(pl.program_id(0) == 0)
    def _():
        if lane_first == 0:
            mix_first(chunks, seq_ref, rank_ref, b_ref, c_ref, bc_edge_ref, wbc_ref, left, bt, cc_ref, padded)
        steps, rates = chunk_rates(ts_ref, rate_ref, chunks)
        t = lax.broadcasted_iota(jnp.int32, (CHUNK + 16, CHUNK), 0)
        u = lax.broadcasted_iota(jnp.int32, (CHUNK + 16, CHUNK), 1)
        half = jnp.where(u < CHUNK // 2, 1.0, 0.0)
        tri = jnp.where(u <= t, 1.0, 0.0) - half
        cum = sum_rates(jnp.where(t < CHUNK, tri, jnp.where(t == CHUNK, half, 1.0)), rates)
        rel = cum[:CHUNK]
        stack_scales(jnp.exp(-rel) * steps, heads, chunks, lhsu)
        stack_scales(jnp.exp(rel), heads, chunks, lhst)
        ends = jnp.exp(jnp.concatenate([rel[CHUNK - 8 :], cum[CHUNK : CHUNK + 8]], axis=0))
        for k in range(chunks):
            ends_all[k] = turned(ends, heads, k)
        part[...] = jnp.zeros_like(part)

    e = one_hot(lane_first + pl.program_id(0) * LANES)
    rows[...] = spread_rows(ends_all[...].reshape(16 * chunks, 128), e).reshape(chunks, 16, LANES)
    wide_u[...] = mm(lhsu[...], e)
    wide_t[...] = mm(lhst[...], e)
    s1, s2, s3 = parts3(skip_ref[...])
    skip = mm(jnp.concatenate([s1.astype(F32), s2.astype(F32), s3.astype(F32)], axis=0).astype(BF16), e[0:heads])
    skip = skip[0:1] + (skip[1:2] + skip[2:3])
    state[...] = jnp.zeros_like(state)
    edges = edge_ref[...].astype(F32)[HALO - 8 :]
    weights = wx_ref[...].astype(F32) * 0.5

    keeps = chunk_keeps(chunks, seq_ref, rank_ref)
    reach = jnp.ones((1, LANES), F32)
    for k in range(chunks):
        toks = slice(k * CHUNK, (k + 1) * CHUNK)
        to_end, to_mid, whole = rows[k, 7:8, :], rows[k, 8:9, :], rows[k, 9:10, :]
        xs, direct = [], []
        for lane in range(0, LANES, 128):
            cols = slice(lane, lane + 128)
            pad = padded.at[(2 * k + lane // 128) % 4]
            fill_padded(pad, x_ref, edges[:, cols], k, cols, keeps[k])
            v = conv_block(pad, weights[:, cols])
            xs.append((v * wide_u[toks, cols]).astype(BF16))
            direct.append(v.astype(BF16).astype(F32) * skip[:, cols])
        xs, direct = jnp.concatenate(xs, axis=1), jnp.concatenate(direct, axis=1)
        before = state[...]
        if keeps[k] is not None:
            before = before * keeps[k]
            reach = reach * keeps[k]
        state[...] = before * whole + mm(bt[k], xs) * to_end
        right = jnp.concatenate([xs, (before * to_mid).astype(BF16)], axis=0)
        inner = mm(left[toks, :], right)
        scale = wide_t[toks, :]
        gate = silu_half(z_ref[toks, :].astype(F32) * 0.5)
        a_ref[toks, :] = ((inner * scale + direct) * gate).astype(BF16)
        f_ref[toks, :] = (scale * gate * (reach * to_mid)).astype(BF16)
        r = roll_ref[toks, :].astype(F32)
        r = r * r
        part[toks, :] += r[:, 0:128] + r[:, 128:256]
        reach = reach * whole

    @pl.when(pl.program_id(0) == pl.num_programs(0) - 1)
    def _():
        for k in range(chunks):
            roll_sum_ref[k : k + 1, :] = jnp.sum(part[k * CHUNK : (k + 1) * CHUNK, :].T, axis=0, keepdims=True)


def norm_kernel(
    in_ref, a1_all, f1_all, cc_hbm, a0_hbm, f0_hbm, roll_hbm, gain_hbm, roll0_hbm, roll1_hbm, out_hbm, sums_ref,
    entering, gated, a0_all, f0_all, roll_all, out_all, cc_ref, gain_ref, roll0_ref, roll1_ref, sums,
    in_sems, out_sems, small_sems,
):
    width = out_all.shape[1]
    chunks, half = out_all.shape[0] // CHUNK, a0_all.shape[1]
    pairs = [(cc_hbm, cc_ref), (a0_hbm, a0_all), (f0_hbm, f0_all), (roll_hbm, roll_all)]
    smalls = [(gain_hbm, gain_ref), (roll0_hbm, roll0_ref), (roll1_hbm, roll1_ref)]
    size = 2 * CHUNK

    def copy_in(i, m):
        here = pl.ds(pl.multiple_of(m * size, size), size)
        return pltpu.make_async_copy(pairs[i][0].at[here], pairs[i][1].at[here], in_sems.at[i, m])

    def copy_out(m):
        here = pl.ds(pl.multiple_of(m * size, size), size)
        return pltpu.make_async_copy(out_all.at[here], out_hbm.at[here], out_sems.at[m])

    def copy_small(i):
        return pltpu.make_async_copy(*smalls[i], small_sems.at[i])

    for m in range(chunks // 2):
        for i in range(len(pairs)):
            copy_in(i, m).start()
        if m == 0:
            for i in range(len(smalls)):
                copy_small(i).start()
    for lb in range(width // 128):
        for nb in range(4):
            entering[nb * 32 : (nb + 1) * 32, lb * 128 : (lb + 1) * 128] = in_ref[lb * 4 + nb]
    for i in range(len(smalls)):
        copy_small(i).wait()

    def two(m, carry):
        for i in range(len(pairs)):
            copy_in(i, m).wait()
        scales = []
        for n in range(2):
            toks = pl.ds(pl.multiple_of(m * size + n * CHUNK, CHUNK), CHUNK)
            squares = jnp.zeros((CHUNK, 128), F32)
            for lane in range(0, width, LANES):
                cols = slice(lane, lane + LANES)
                a_ref, f_ref = (a0_all, f0_all) if lane < half else (a1_all, f1_all)
                own = slice(lane % half, lane % half + LANES)
                g = a_ref[toks, own].astype(F32) + f_ref[toks, own].astype(F32) * mm(cc_ref[toks, :], entering[:, cols])
                gated[n, :, cols] = g
                g = g * g
                squares = squares + (g[:, 0:128] + g[:, 128:256])
            mean = jnp.sum(squares, axis=1, keepdims=True) * (1.0 / width)
            scales.append(lax.rsqrt(mean + 1e-05))
        for n in range(2):
            toks = pl.ds(pl.multiple_of(m * size + n * CHUNK, CHUNK), CHUNK)
            squares = jnp.zeros((CHUNK, 128), F32)
            for lane in range(0, width, 128):
                cols = slice(lane, lane + 128)
                v = (gated[n, :, cols] * scales[n] * gain_ref[:, cols]).astype(BF16)
                out_all[toks, cols] = v
                d = v.astype(F32) - roll_all[toks, cols].astype(F32)
                squares = squares + d * d
            sums[pl.ds(2 * m + n, 1), :] = jnp.sum(squares.T, axis=0, keepdims=True)
        copy_out(m).start()
        return carry

    lax.fori_loop(0, chunks // 2, two, 0)
    both = jnp.concatenate([sums[...], roll0_ref[...] + roll1_ref[...]], axis=0)
    for i in range(sums_ref.shape[0]):
        sums_ref[i] = both
    for m in range(chunks // 2):
        copy_out(m).wait()


def shards(
    x_values, b_values, c_values, z_values, time_steps, decay_rate, skip_gain,
    conv_x, conv_bc, norm_gain, rollout, seq_spans,
):
    ring = lax.axis_size("seq")
    rows, width = x_values.shape
    heads = decay_rate.shape[0]
    chunks = rows // CHUNK
    blocks = width // LANES
    rank = lax.axis_index("seq").astype(jnp.int32).reshape(1)

    ends = width + 2 * STATE
    smem = pl.BlockSpec(memory_space=pltpu.SMEM)

    def whole(*shape):
        return pl.BlockSpec(shape, lambda i: (0,) * len(shape))

    def lane_block(r, first=0):
        return pl.BlockSpec((r, LANES), lambda i: (0, first + i))

    def grant(mib):
        return pltpu.CompilerParams(vmem_limit_bytes=mib * 1024 * 1024)

    def in_hbm(*arrays):
        return [pltpu.with_memory_space_constraint(v, pltpu.HBM) for v in arrays]

    x_values, b_values, c_values, z_values, rollout = in_hbm(x_values, b_values, c_values, z_values, rollout)
    (seq_spans,) = in_hbm(seq_spans)
    steps_row, rate_row, skip_row, gain_row, conv_x, conv_bc = in_hbm(
        time_steps.T, decay_rate.reshape(1, heads), skip_gain.reshape(1, heads), norm_gain.reshape(1, width), conv_x, conv_bc
    )
    last = rows // HALO - 1
    edge = pl.pallas_call(
        tail_kernel,
        grid=(1,),
        in_specs=[pl.BlockSpec((HALO, n), lambda i: (last, 0)) for n in (width, STATE, STATE)],
        out_specs=whole(HALO, ends),
        out_shape=jax.ShapeDtypeStruct((HALO, ends), BF16),
        compiler_params=grant(8),
        name="tails",
    )(x_values, b_values, c_values)
    edge = lax.ppermute(edge, "seq", [(i, i + 1) for i in range(ring - 1)])
    conv_scratch = pltpu.VMEM((4, 8 + CHUNK, 128), F32)
    wide_scratch = pltpu.VMEM((rows, LANES), F32)

    vmem = pl.BlockSpec(memory_space=pltpu.VMEM)
    hbm = pl.BlockSpec(memory_space=pl.ANY)
    end, head_scale, chain, head = pl.pallas_call(
        functools.partial(state_kernel, chunks),
        in_specs=[smem, smem, hbm] + [vmem] * 5,
        out_specs=[vmem] * 4,
        out_shape=[
            jax.ShapeDtypeStruct((STATE, width), F32),
            jax.ShapeDtypeStruct((HALO, width), F32),
            jax.ShapeDtypeStruct((8, width), F32),
            jax.ShapeDtypeStruct((HALO, width + STATE), BF16),
        ],
        scratch_shapes=[
            pltpu.VMEM((blocks, rows, LANES), BF16),
            conv_scratch,
            pltpu.VMEM((CHUNK, 128), F32),
            pltpu.VMEM((rows, 256), BF16),
            pltpu.VMEM((blocks, rows, LANES), F32),
            pltpu.VMEM((STATE, rows), BF16),
            pltpu.VMEM((rows, LANES), BF16),
            pltpu.SemaphoreType.DMA((blocks,)),
        ],
        compiler_params=grant(16),
        cost_estimate=pl.CostEstimate(flops=1 << 29, bytes_accessed=4 << 20, transcendentals=1 << 20),
        name="states",
    )(seq_spans, rank, x_values, b_values, steps_row, rate_row, conv_x, conv_bc)

    msg, edge = pl.pallas_call(
        functools.partial(edge_kernel, chunks),
        grid=(1,),
        in_specs=[
            smem, smem, whole(HALO, ends), whole(HALO, width + STATE), whole(CONV_K, width),
            whole(2, CONV_K, STATE), whole(HALO, width), whole(STATE, width), whole(8, width),
        ],
        out_specs=[whole(ring, 40, 128), whole(HALO, ends)],
        out_shape=[jax.ShapeDtypeStruct((ring, 40, 128), BF16), pltpu.HBM((HALO, ends), BF16)],
        compiler_params=grant(8),
        name="edge_states",
    )(seq_spans, rank, edge, head, conv_x, conv_bc, head_scale, end, chain)
    (edge,) = in_hbm(edge)

    spread = lax.all_to_all(msg, "seq", split_axis=0, concat_axis=0, tiled=True)

    def mix(first, specs, operands, more_specs, more_shapes):
        half = blocks // 2
        place = pltpu.HBM if first == 0 else pltpu.VMEM
        return pl.pallas_call(
            functools.partial(mix_kernel, chunks, first * LANES),
            grid=(half,),
            in_specs=[
                smem, smem, lane_block(rows, first), lane_block(HALO, first), whole(heads, rows), whole(1, heads),
                lane_block(rows, first), lane_block(rows, first), lane_block(CONV_K, first), whole(1, heads),
            ]
            + specs,
            out_specs=[lane_block(rows), lane_block(rows), whole(chunks, CHUNK)] + more_specs,
            out_shape=[
                place((rows, half * LANES), BF16),
                place((rows, half * LANES), BF16),
                pltpu.HBM((chunks, CHUNK), F32),
            ]
            + more_shapes,
            scratch_shapes=[
                conv_scratch, wide_scratch, wide_scratch, pltpu.VMEM((rows, 128), F32), pltpu.VMEM((STATE, LANES), F32),
                pltpu.VMEM((rows, 256), BF16), pltpu.VMEM((rows, 256), BF16), pltpu.VMEM((chunks, 16, 128), F32),
                pltpu.VMEM((chunks, 16, LANES), F32),
            ],
            compiler_params=grant(32),
            cost_estimate=pl.CostEstimate(flops=1 << 30, bytes_accessed=9 << 20, transcendentals=1 << 20),
            name="mix_first" if first == 0 else "mix_second",
        )(
            seq_spans, rank, x_values, edge, steps_row, rate_row, z_values, rollout, conv_x,
            skip_row, *operands,
        )

    shared_specs = [whole(rows, 256), whole(chunks, STATE, CHUNK)]
    a0, f0, roll0, left, bt, cc = mix(
        0,
        [
            whole(rows, STATE), whole(rows, STATE), pl.BlockSpec((HALO, 2 * STATE), lambda i: (0, width // (2 * STATE))),
            whole(2, CONV_K, STATE),
        ],
        [b_values, c_values, edge, conv_bc],
        shared_specs + [whole(rows, STATE)],
        [
            pltpu.HBM((rows, 256), BF16),
            pltpu.HBM((chunks, STATE, CHUNK), BF16),
            pltpu.HBM((rows, STATE), BF16),
        ],
    )
    a0, f0, roll0, left, bt, cc = in_hbm(a0, f0, roll0, left, bt, cc)
    a1, f1, roll1 = mix(blocks // 2, shared_specs, [left, bt], [], [])
    a1, f1 = (pltpu.with_memory_space_constraint(v, pltpu.VMEM) for v in (a1, f1))
    (roll1,) = in_hbm(roll1)

    entering = pl.pallas_call(
        scan_kernel,
        in_specs=[pl.BlockSpec(memory_space=pltpu.VMEM), pl.BlockSpec(memory_space=pl.ANY)],
        out_shape=jax.ShapeDtypeStruct((ring, 32, 128), BF16),
        compiler_params=grant(8),
        name="scan",
    )(spread, roll0)
    entering = lax.all_to_all(entering, "seq", split_axis=0, concat_axis=0, tiled=True)

    group = lax.axis_size("head")
    normed, sums = pl.pallas_call(
        norm_kernel,
        in_specs=[vmem] * 3 + [hbm] * 7,
        out_specs=[hbm, vmem],
        out_shape=[pltpu.HBM((rows, width), BF16), jax.ShapeDtypeStruct((group, 2 * chunks, CHUNK), F32)],
        scratch_shapes=[pltpu.VMEM((STATE, width), BF16), pltpu.VMEM((2, CHUNK, width), F32)]
        + [pltpu.VMEM((rows, width // 2), BF16)] * 2
        + [pltpu.VMEM((rows, width), BF16)] * 2
        + [pltpu.VMEM((rows, STATE), BF16), pltpu.VMEM((1, width), F32)]
        + [pltpu.VMEM((chunks, CHUNK), F32)] * 3
        + [pltpu.SemaphoreType.DMA((n, chunks // 2)) for n in (4,)]
        + [pltpu.SemaphoreType.DMA((chunks // 2,)), pltpu.SemaphoreType.DMA((3,))],
        compiler_params=grant(24),
        cost_estimate=pl.CostEstimate(flops=1 << 28, bytes_accessed=8 << 20, transcendentals=1 << 10),
        name="norms",
    )(entering, a1, f1, cc, a0, f0, rollout, gain_row, roll0, roll1)

    sums = jnp.sum(lax.all_to_all(sums, "head", split_axis=0, concat_axis=0, tiled=True), axis=0)
    relative = jnp.sqrt(sums[:chunks] / (sums[chunks:] + 1e-06))
    return normed, relative.reshape(rows)


def solution(mesh):
    placed = (
        P("seq", "head"), P("seq", "head"), P("seq", "head"), P("seq", "head"), P("seq", "head"),
        P("head"), P("head"), P(None, "head"), P(None, None, "head"), P("head"), P("seq", "head"), P(),
    )
    return jax.shard_map(
        shards, mesh=mesh, in_specs=placed, out_specs=(P("seq", "head"), P("seq")), check_vma=False
    )
```

```python
import functools

import jax
import jax.numpy as jnp
from jax import lax
from jax.experimental import pallas as pl
from jax.experimental.pallas import tpu as pltpu
from jax.sharding import PartitionSpec as P

HEADS = 128
HEAD_DIM = 64
STATE = 128
GROUPS = 8
CONV_K = 4
SPAN = 256
CHUNK = 128
LANES = 256
HALO = 16

F32 = jnp.float32
BF16 = jnp.bfloat16


def parts3(v):
    hi = v.astype(BF16)
    rest = v - hi.astype(F32)
    mid = rest.astype(BF16)
    low = (rest - mid.astype(F32)).astype(BF16)
    return hi, mid, low


def silu_half(h):
    return h + h * jnp.tanh(h)


def mm(a, b):
    return jnp.dot(a, b, preferred_element_type=F32)


def one_hot(lane0, width=LANES):
    r = lax.broadcasted_iota(jnp.int32, (256, width), 0)
    c = lax.broadcasted_iota(jnp.int32, (256, width), 1)
    return jnp.where((r & 127) == (c + lane0) // HEAD_DIM, 1.0, 0.0).astype(BF16)


def span_keep(seq_ref, span):
    start = seq_ref[0] * 0
    fresh = span == start
    for i in range(seq_ref.shape[0] - 1):
        start = start + seq_ref[i]
        fresh = fresh | (span == start)
    return jnp.where(fresh, 0.0, 1.0).astype(F32)


def conv_block(padded_ref, taps):
    rows = padded_ref.shape[0] - 8
    total = padded_ref[pl.ds(5, rows), :] * taps[0:1]
    for k in range(1, CONV_K):
        total = total + padded_ref[pl.ds(5 + k, rows), :] * taps[k : k + 1]
    return silu_half(total)


def conv_ordered(padded_ref, taps):
    per = CHUNK // 8
    shifted = {m: padded_ref[pl.ds(8 + m, 8, stride=per), :] for m in range(1 - CONV_K, per)}
    rows = []
    for j in range(per):
        total = shifted[j + 1 - CONV_K] * taps[0:1]
        for k in range(1, CONV_K):
            total = total + shifted[j + 1 - CONV_K + k] * taps[k : k + 1]
        rows.append(silu_half(total))
    return jnp.concatenate(rows, axis=0)


def turned(v, heads, chunk):
    turn = (128 - heads * chunk) % 128
    return pltpu.roll(v, turn, 1) if turn else v


def split2(v):
    hi = v.astype(BF16)
    return hi, (v - hi.astype(F32)).astype(BF16)


def stack_scales(source, heads, chunks, target):
    for k in range(chunks):
        hi, low = split2(turned(source, heads, k))
        target[k * CHUNK : (k + 1) * CHUNK, 0:128] = hi
        target[k * CHUNK : (k + 1) * CHUNK, 128:256] = low


def chunk_rates(ts_ref, rate_ref, chunks):
    steps = jnp.concatenate([ts_ref[:, k * CHUNK : (k + 1) * CHUNK] for k in range(chunks)], axis=0).T
    return steps, -steps * jnp.concatenate([rate_ref[...]] * chunks, axis=1)


def sum_rates(picks, rates):
    picks = picks.astype(BF16)
    r1, r2, r3 = parts3(rates)
    return mm(picks, r1) + (mm(picks, r2) + mm(picks, r3))


def spread_rows(v, e):
    n = v.shape[0]
    out = mm(jnp.concatenate(parts3(v), axis=0), e[0:128])
    return out[0:n] + (out[n : 2 * n] + out[2 * n : 3 * n])


def chunk_keeps(chunks, seq_ref, rank_ref):
    per_span = SPAN // CHUNK
    first = rank_ref[0] * (chunks // per_span)
    return [None if k % per_span else span_keep(seq_ref, first + k // per_span) for k in range(chunks)]


def fill_padded(padded_ref, src_ref, edge, k, lanes, keep):
    if k == 0:
        halo = edge
    else:
        halo = src_ref[k * CHUNK - HALO : k * CHUNK, lanes].astype(F32)[HALO - 8 :]
    padded_ref[0:8, :] = halo if keep is None else halo * keep
    padded_ref[8 : 8 + CHUNK, :] = src_ref[k * CHUNK : (k + 1) * CHUNK, lanes].astype(F32)


def tail_kernel(x_ref, b_ref, c_ref, out_ref):
    width = x_ref.shape[1]
    out_ref[:, 0:width] = x_ref[...]
    out_ref[:, width : width + STATE] = b_ref[...]
    out_ref[:, width + STATE : width + 2 * STATE] = c_ref[...]


def state_kernel(
    chunks, seq_ref, rank_ref, x_hbm, b_ref, ts_ref, rate_ref, wx_ref, wb_ref,
    end_ref, head_scale_ref, chain_ref, head_ref, taps_ref,
    x_all, padded, order, lhsu, wide, bt, xs, x_sems,
):
    blocks = x_all.shape[0]
    width = blocks * LANES
    heads = ts_ref.shape[0]

    def x_copy(i):
        lanes = pl.ds(pl.multiple_of(i * LANES, LANES), LANES)
        return pltpu.make_async_copy(x_hbm.at[:, lanes], x_all.at[i], x_sems.at[i])

    def start(i, carry):
        x_copy(i).start()
        return carry

    lax.fori_loop(0, blocks, start, 0)
    steps, rates = chunk_rates(ts_ref, rate_ref, chunks)
    t = lax.broadcasted_iota(jnp.int32, (CHUNK + 16, CHUNK), 0)
    u = lax.broadcasted_iota(jnp.int32, (CHUNK + 16, CHUNK), 1)
    after = sum_rates(jnp.where((u > t) | (t >= CHUNK), 1.0, 0.0), rates)
    totals = after[CHUNK : CHUNK + 16]
    j = lax.broadcasted_iota(jnp.int32, (CHUNK, CHUNK), 0)
    k = lax.broadcasted_iota(jnp.int32, (CHUNK, CHUNK), 1)
    later = jnp.where((lax.rem(j, heads) == lax.rem(k, heads)) & (j > k), 1.0, 0.0).astype(BF16)
    t1, t2, t3 = parts3(totals)
    later = mm(t1, later) + (mm(t2, later) + mm(t3, later))
    lane = lax.broadcasted_iota(jnp.int32, (16, 128), 1)
    reached = jnp.ones((16, 128), F32)
    whole = jnp.exp(later + totals)
    for n in range(0, chunks, SPAN // CHUNK):
        keep = span_keep(seq_ref, rank_ref[0] * (chunks * CHUNK // SPAN) + n * CHUNK // SPAN)
        reached = jnp.where(lane < n * heads, reached * keep, reached)
        whole = whole * keep
    scale = jnp.exp(after[0:CHUNK] + later[0:1]) * steps * reached[0:1]
    order[...] = scale
    per = CHUNK // 8
    stack_scales(jnp.concatenate([order[pl.ds(n, 8, stride=per), :] for n in range(per)], axis=0), heads, chunks, lhsu)
    e = one_hot(0, width)
    wide_all = mm(lhsu[...], e)
    for i in range(blocks):
        wide[i] = wide_all[:, i * LANES : (i + 1) * LANES]
    head_scale_ref[...] = mm(jnp.concatenate(split2(scale[0:HALO]), axis=1), e)
    row = lax.broadcasted_iota(jnp.int32, (16, 1), 0)
    p1, p2, p3 = parts3(whole)
    p = jnp.where(row == 0, p1.astype(F32), jnp.where(row == 1, p2.astype(F32), p3.astype(F32)))
    chain_ref[...] = mm(jnp.where(row < 3, p, 0.0).astype(BF16), e[0:128])[0:8]
    taps = wb_ref[0].astype(F32) * 0.5
    none = jnp.zeros((8, 128), F32)

    keeps = chunk_keeps(chunks, seq_ref, rank_ref)
    for k in range(chunks):
        pad = padded.at[k % 4]
        fill_padded(pad, b_ref, none, k, slice(0, STATE), keeps[k])
        v = conv_ordered(pad, taps)
        if k == 0:
            v = jnp.where((lax.broadcasted_iota(jnp.int32, v.shape, 0) & 7) == 0, 0.0, v)
        bt[:, k * CHUNK : (k + 1) * CHUNK] = v.T.astype(BF16)
    head_ref[:, width : width + STATE] = b_ref[0:HALO, :]
    taps_ref[0:CONV_K, 0:width] = wx_ref[...].astype(F32) * 0.5
    taps_ref[0:CONV_K, width : width + STATE] = taps
    taps_ref[CONV_K : CONV_K + 1, :] = jnp.ones((1, width + STATE), F32) * keeps[0]

    def block(i, carry):
        lane0 = pl.multiple_of(i * LANES, LANES)
        lanes = pl.ds(lane0, LANES)
        x_ref = x_all.at[i]
        weights = wx_ref[:, lanes].astype(F32) * 0.5
        x_copy(i).wait()
        head_ref[:, lanes] = x_ref[0:HALO, :]

        for k in range(chunks):
            toks = slice(k * CHUNK, (k + 1) * CHUNK)
            for part in range(LANES // 128):
                cols = slice(part * 128, (part + 1) * 128)
                pad = padded.at[(2 * k + part) % 4]
                fill_padded(pad, x_ref, none, k, cols, keeps[k])
                v = conv_ordered(pad, weights[:, cols])
                xs[i, toks, cols] = (v * wide[i, toks, cols]).astype(BF16)
        return carry

    lax.fori_loop(0, blocks, block, 0)
    for i in range(blocks):
        end_ref[:, i * LANES : (i + 1) * LANES] = mm(bt[...], xs[i])


def edge_kernel(edge_ref, head_ref, taps_ref, scale_ref, end_ref, chain_ref, msg_ref):
    width = end_ref.shape[1]
    b_cols = slice(width, width + STATE)

    def conv(cols):
        taps = taps_ref[:, cols]
        before = edge_ref[:, cols].astype(F32)[HALO - 8 :] * taps[CONV_K : CONV_K + 1]
        joined = jnp.concatenate([before, head_ref[:, cols].astype(F32)], axis=0)
        total = joined[5 : 5 + HALO] * taps[0:1]
        for k in range(1, CONV_K):
            total = total + joined[5 + k : 5 + k + HALO] * taps[k : k + 1]
        return silu_half(total)

    bc = conv(b_cols)
    bt = jnp.concatenate([bc, jnp.zeros((STATE - HALO, STATE), F32)], axis=0).T[:, 0:HALO].astype(BF16)

    for i in range(width // LANES):
        cols = slice(i * LANES, (i + 1) * LANES)
        v = conv(cols)
        xs = (v * scale_ref[:, cols]).astype(BF16)
        state = end_ref[:, cols] + mm(bt, xs)
        both = jnp.concatenate([state, chain_ref[:, cols]], axis=0)
        for part in range(LANES // 128):
            piece = both[:, part * 128 : (part + 1) * 128]
            for nb in range(4):
                own = jnp.concatenate([piece[nb * 32 : (nb + 1) * 32], piece[STATE:]], axis=0)
                msg_ref[(i * (LANES // 128) + part) * 4 + nb] = own.astype(BF16)


def scan_kernel(in_ref, after_ref, out_ref):
    def some(m, carried):
        for n in range(8):
            i = 8 * m + n
            out_ref[i] = carried.astype(BF16)
            block = in_ref[i].astype(F32)
            decay = block[32:33] + (block[33:34] + block[34:35])
            carried = carried * decay + block[0:32]
        return carried

    lax.fori_loop(0, in_ref.shape[0] // 8, some, jnp.zeros((32, 128), F32))


def mix_first(chunks, seq_ref, rank_ref, b_ref, c_ref, edge_ref, wbc_ref, left, bt, cc_ref, padded):
    t = lax.broadcasted_iota(jnp.int32, (CHUNK, CHUNK), 0)
    u = lax.broadcasted_iota(jnp.int32, (CHUNK, CHUNK), 1)
    edges = edge_ref[...].astype(F32)[HALO - 8 :]

    keeps = chunk_keeps(chunks, seq_ref, rank_ref)
    for k in range(chunks):
        toks = slice(k * CHUNK, (k + 1) * CHUNK)
        pair = []
        for i, ref in enumerate((b_ref, c_ref)):
            pad = padded.at[(2 * k + i) % 4]
            fill_padded(pad, ref, edges[:, i * STATE : (i + 1) * STATE], k, slice(0, STATE), keeps[k])
            pair.append(conv_block(pad, wbc_ref[i].astype(F32) * 0.5))
        b, c = pair
        bt[k] = b.T.astype(BF16)
        c = c.astype(BF16)
        cc_ref[toks, :] = c
        left[toks, 128:256] = c
        g = lax.dot_general(c, b.astype(BF16), (((1,), (1,)), ((), ())), preferred_element_type=F32)
        left[toks, 0:128] = jnp.where(u <= t, g, 0.0).astype(BF16)


def mix_kernel(
    chunks, lane_first, seq_ref, rank_ref, x_ref, edge_ref, ts_ref, rate_ref, z_ref, roll_ref, wx_ref, skip_ref, *refs
):
    if lane_first == 0:
        b_ref, c_ref, bc_edge_ref, wbc_ref, a_ref, f_ref, roll_sum_ref, left, bt, cc_ref = refs[:10]
    else:
        left, bt, a_ref, f_ref, roll_sum_ref = refs[:5]
    padded, wide_u, wide_t, part, state, lhsu, lhst, ends_all, rows = refs[-9:]
    heads = skip_ref.shape[1]

    @pl.when(pl.program_id(0) == 0)
    def _():
        if lane_first == 0:
            mix_first(chunks, seq_ref, rank_ref, b_ref, c_ref, bc_edge_ref, wbc_ref, left, bt, cc_ref, padded)
        steps, rates = chunk_rates(ts_ref, rate_ref, chunks)
        t = lax.broadcasted_iota(jnp.int32, (CHUNK + 16, CHUNK), 0)
        u = lax.broadcasted_iota(jnp.int32, (CHUNK + 16, CHUNK), 1)
        half = jnp.where(u < CHUNK // 2, 1.0, 0.0)
        tri = jnp.where(u <= t, 1.0, 0.0) - half
        cum = sum_rates(jnp.where(t < CHUNK, tri, jnp.where(t == CHUNK, half, 1.0)), rates)
        rel = cum[:CHUNK]
        stack_scales(jnp.exp(-rel) * steps, heads, chunks, lhsu)
        stack_scales(jnp.exp(rel), heads, chunks, lhst)
        ends = jnp.exp(jnp.concatenate([rel[CHUNK - 8 :], cum[CHUNK : CHUNK + 8]], axis=0))
        for k in range(chunks):
            ends_all[k] = turned(ends, heads, k)
        part[...] = jnp.zeros_like(part)

    e = one_hot(lane_first + pl.program_id(0) * LANES)
    rows[...] = spread_rows(ends_all[...].reshape(16 * chunks, 128), e).reshape(chunks, 16, LANES)
    wide_u[...] = mm(lhsu[...], e)
    wide_t[...] = mm(lhst[...], e)
    s1, s2, s3 = parts3(skip_ref[...])
    skip = mm(jnp.concatenate([s1.astype(F32), s2.astype(F32), s3.astype(F32)], axis=0).astype(BF16), e[0:heads])
    skip = skip[0:1] + (skip[1:2] + skip[2:3])
    state[...] = jnp.zeros_like(state)
    edges = edge_ref[...].astype(F32)[HALO - 8 :]
    weights = wx_ref[...].astype(F32) * 0.5

    keeps = chunk_keeps(chunks, seq_ref, rank_ref)
    reach = jnp.ones((1, LANES), F32)
    for k in range(chunks):
        toks = slice(k * CHUNK, (k + 1) * CHUNK)
        to_end, to_mid, whole = rows[k, 7:8, :], rows[k, 8:9, :], rows[k, 9:10, :]
        xs, direct = [], []
        for lane in range(0, LANES, 128):
            cols = slice(lane, lane + 128)
            pad = padded.at[(2 * k + lane // 128) % 4]
            fill_padded(pad, x_ref, edges[:, cols], k, cols, keeps[k])
            v = conv_block(pad, weights[:, cols])
            xs.append((v * wide_u[toks, cols]).astype(BF16))
            direct.append(v.astype(BF16).astype(F32) * skip[:, cols])
        xs, direct = jnp.concatenate(xs, axis=1), jnp.concatenate(direct, axis=1)
        before = state[...]
        if keeps[k] is not None:
            before = before * keeps[k]
            reach = reach * keeps[k]
        state[...] = before * whole + mm(bt[k], xs) * to_end
        right = jnp.concatenate([xs, (before * to_mid).astype(BF16)], axis=0)
        inner = mm(left[toks, :], right)
        scale = wide_t[toks, :]
        gate = silu_half(z_ref[toks, :].astype(F32) * 0.5)
        a_ref[toks, :] = ((inner * scale + direct) * gate).astype(BF16)
        f_ref[toks, :] = (scale * gate * (reach * to_mid)).astype(BF16)
        r = roll_ref[toks, :].astype(F32)
        r = r * r
        part[toks, :] += r[:, 0:128] + r[:, 128:256]
        reach = reach * whole

    @pl.when(pl.program_id(0) == pl.num_programs(0) - 1)
    def _():
        for k in range(chunks):
            roll_sum_ref[k : k + 1, :] = jnp.sum(part[k * CHUNK : (k + 1) * CHUNK, :].T, axis=0, keepdims=True)


def norm_kernel(
    in_ref, a1_all, f1_all, cc_ref, a0_hbm, f0_hbm, roll_hbm, gain_hbm, roll0_hbm, roll1_hbm, out_hbm, sums_ref,
    entering, gated, a0_all, f0_all, roll_all, out_all, gain_ref, roll0_ref, roll1_ref, sums,
    in_sems, out_sems, small_sems,
):
    width = out_all.shape[1]
    chunks, half = out_all.shape[0] // CHUNK, a0_all.shape[1]
    pairs = [(a0_hbm, a0_all), (f0_hbm, f0_all), (roll_hbm, roll_all)]
    smalls = [(gain_hbm, gain_ref), (roll0_hbm, roll0_ref), (roll1_hbm, roll1_ref)]
    size = 2 * CHUNK

    def copy_in(i, m):
        here = pl.ds(pl.multiple_of(m * size, size), size)
        return pltpu.make_async_copy(pairs[i][0].at[here], pairs[i][1].at[here], in_sems.at[i, m])

    def copy_out(m):
        here = pl.ds(pl.multiple_of(m * size, size), size)
        return pltpu.make_async_copy(out_all.at[here], out_hbm.at[here], out_sems.at[m])

    def copy_small(i):
        return pltpu.make_async_copy(*smalls[i], small_sems.at[i])

    for m in range(chunks // 2):
        for i in range(len(pairs)):
            copy_in(i, m).start()
        if m == 0:
            for i in range(len(smalls)):
                copy_small(i).start()
    for lb in range(width // 128):
        for nb in range(4):
            entering[nb * 32 : (nb + 1) * 32, lb * 128 : (lb + 1) * 128] = in_ref[lb * 4 + nb]
    for i in range(len(smalls)):
        copy_small(i).wait()

    def two(m, carry):
        for i in range(len(pairs)):
            copy_in(i, m).wait()
        scales = []
        for n in range(2):
            toks = pl.ds(pl.multiple_of(m * size + n * CHUNK, CHUNK), CHUNK)
            squares = jnp.zeros((CHUNK, 128), F32)
            for lane in range(0, width, LANES):
                cols = slice(lane, lane + LANES)
                a_ref, f_ref = (a0_all, f0_all) if lane < half else (a1_all, f1_all)
                own = slice(lane % half, lane % half + LANES)
                g = a_ref[toks, own].astype(F32) + f_ref[toks, own].astype(F32) * mm(cc_ref[toks, :], entering[:, cols])
                gated[n, :, cols] = g
                g = g * g
                squares = squares + (g[:, 0:128] + g[:, 128:256])
            mean = jnp.sum(squares, axis=1, keepdims=True) * (1.0 / width)
            scales.append(lax.rsqrt(mean + 1e-05))
        for n in range(2):
            toks = pl.ds(pl.multiple_of(m * size + n * CHUNK, CHUNK), CHUNK)
            squares = jnp.zeros((CHUNK, 128), F32)
            for lane in range(0, width, 128):
                cols = slice(lane, lane + 128)
                v = (gated[n, :, cols] * scales[n] * gain_ref[:, cols]).astype(BF16)
                out_all[toks, cols] = v
                d = v.astype(F32) - roll_all[toks, cols].astype(F32)
                squares = squares + d * d
            sums[pl.ds(2 * m + n, 1), :] = jnp.sum(squares.T, axis=0, keepdims=True)
        copy_out(m).start()
        return carry

    lax.fori_loop(0, chunks // 2, two, 0)
    both = jnp.concatenate([sums[...], roll0_ref[...] + roll1_ref[...]], axis=0)
    for i in range(sums_ref.shape[0]):
        sums_ref[i] = both
    for m in range(chunks // 2):
        copy_out(m).wait()


def shards(
    x_values, b_values, c_values, z_values, time_steps, decay_rate, skip_gain,
    conv_x, conv_bc, norm_gain, rollout, seq_spans,
):
    ring = lax.axis_size("seq")
    rows, width = x_values.shape
    heads = decay_rate.shape[0]
    chunks = rows // CHUNK
    blocks = width // LANES
    rank = lax.axis_index("seq").astype(jnp.int32).reshape(1)

    ends = width + 2 * STATE
    smem = pl.BlockSpec(memory_space=pltpu.SMEM)

    def whole(*shape):
        return pl.BlockSpec(shape, lambda i: (0,) * len(shape))

    def lane_block(r, first=0):
        return pl.BlockSpec((r, LANES), lambda i: (0, first + i))

    def grant(mib):
        return pltpu.CompilerParams(vmem_limit_bytes=mib * 1024 * 1024)

    def in_hbm(*arrays):
        return [pltpu.with_memory_space_constraint(v, pltpu.HBM) for v in arrays]

    x_values, b_values, c_values, z_values, rollout = in_hbm(x_values, b_values, c_values, z_values, rollout)
    (seq_spans,) = in_hbm(seq_spans)
    steps_row, rate_row, skip_row, gain_row, conv_x, conv_bc = in_hbm(
        time_steps.T, decay_rate.reshape(1, heads), skip_gain.reshape(1, heads), norm_gain.reshape(1, width), conv_x, conv_bc
    )
    last = rows // HALO - 1
    edge = pl.pallas_call(
        tail_kernel,
        grid=(1,),
        in_specs=[pl.BlockSpec((HALO, n), lambda i: (last, 0)) for n in (width, STATE, STATE)],
        out_specs=whole(HALO, ends),
        out_shape=jax.ShapeDtypeStruct((HALO, ends), BF16),
        compiler_params=grant(8),
        name="tails",
    )(x_values, b_values, c_values)
    edge = lax.ppermute(edge, "seq", [(i, i + 1) for i in range(ring - 1)])
    conv_scratch = pltpu.VMEM((4, 8 + CHUNK, 128), F32)
    wide_scratch = pltpu.VMEM((rows, LANES), F32)

    vmem = pl.BlockSpec(memory_space=pltpu.VMEM)
    hbm = pl.BlockSpec(memory_space=pl.ANY)
    end, head_scale, chain, head, taps = pl.pallas_call(
        functools.partial(state_kernel, chunks),
        in_specs=[smem, smem, hbm] + [vmem] * 5,
        out_specs=[vmem] * 5,
        out_shape=[
            jax.ShapeDtypeStruct((STATE, width), F32),
            jax.ShapeDtypeStruct((HALO, width), F32),
            jax.ShapeDtypeStruct((8, width), F32),
            jax.ShapeDtypeStruct((HALO, width + STATE), BF16),
            jax.ShapeDtypeStruct((8, width + STATE), F32),
        ],
        scratch_shapes=[
            pltpu.VMEM((blocks, rows, LANES), BF16),
            conv_scratch,
            pltpu.VMEM((CHUNK, 128), F32),
            pltpu.VMEM((rows, 256), BF16),
            pltpu.VMEM((blocks, rows, LANES), F32),
            pltpu.VMEM((STATE, rows), BF16),
            pltpu.VMEM((blocks, rows, LANES), BF16),
            pltpu.SemaphoreType.DMA((blocks,)),
        ],
        compiler_params=grant(16),
        cost_estimate=pl.CostEstimate(flops=1 << 29, bytes_accessed=4 << 20, transcendentals=1 << 20),
        name="states",
    )(seq_spans, rank, x_values, b_values, steps_row, rate_row, conv_x, conv_bc)

    msg = pl.pallas_call(
        edge_kernel,
        out_shape=pltpu.VMEM((ring, 40, 128), BF16),
        compiler_params=grant(8),
        name="edge_states",
    )(edge, head, taps, head_scale, end, chain)
    edge = pltpu.with_memory_space_constraint(edge, pltpu.VMEM)

    spread = lax.all_to_all(msg, "seq", split_axis=0, concat_axis=0, tiled=True)

    def mix(first, specs, operands, more_specs, more_shapes):
        half = blocks // 2
        place = pltpu.HBM if first == 0 else pltpu.VMEM
        return pl.pallas_call(
            functools.partial(mix_kernel, chunks, first * LANES),
            grid=(half,),
            in_specs=[
                smem, smem, lane_block(rows, first), lane_block(HALO, first), whole(heads, rows), whole(1, heads),
                lane_block(rows, first), lane_block(rows, first), lane_block(CONV_K, first), whole(1, heads),
            ]
            + specs,
            out_specs=[lane_block(rows), lane_block(rows), whole(chunks, CHUNK)] + more_specs,
            out_shape=[
                place((rows, half * LANES), BF16),
                place((rows, half * LANES), BF16),
                pltpu.HBM((chunks, CHUNK), F32),
            ]
            + more_shapes,
            scratch_shapes=[
                conv_scratch, wide_scratch, wide_scratch, pltpu.VMEM((rows, 128), F32), pltpu.VMEM((STATE, LANES), F32),
                pltpu.VMEM((rows, 256), BF16), pltpu.VMEM((rows, 256), BF16), pltpu.VMEM((chunks, 16, 128), F32),
                pltpu.VMEM((chunks, 16, LANES), F32),
            ],
            compiler_params=grant(32),
            cost_estimate=pl.CostEstimate(flops=1 << 30, bytes_accessed=9 << 20, transcendentals=1 << 20),
            name="mix_first" if first == 0 else "mix_second",
        )(
            seq_spans, rank, x_values, edge, steps_row, rate_row, z_values, rollout, conv_x,
            skip_row, *operands,
        )

    shared_specs = [whole(rows, 256), whole(chunks, STATE, CHUNK)]
    a0, f0, roll0, left, bt, cc = mix(
        0,
        [
            whole(rows, STATE), whole(rows, STATE), pl.BlockSpec((HALO, 2 * STATE), lambda i: (0, width // (2 * STATE))),
            whole(2, CONV_K, STATE),
        ],
        [b_values, c_values, edge, conv_bc],
        shared_specs + [whole(rows, STATE)],
        [
            pltpu.HBM((rows, 256), BF16),
            pltpu.HBM((chunks, STATE, CHUNK), BF16),
            pltpu.VMEM((rows, STATE), BF16),
        ],
    )
    a0, f0, roll0, left, bt = in_hbm(a0, f0, roll0, left, bt)
    cc = pltpu.with_memory_space_constraint(cc, pltpu.VMEM)
    a1, f1, roll1 = mix(blocks // 2, shared_specs, [left, bt], [], [])
    a1, f1 = (pltpu.with_memory_space_constraint(v, pltpu.VMEM) for v in (a1, f1))
    (roll1,) = in_hbm(roll1)

    entering = pl.pallas_call(
        scan_kernel,
        in_specs=[pl.BlockSpec(memory_space=pltpu.VMEM), pl.BlockSpec(memory_space=pl.ANY)],
        out_shape=pltpu.VMEM((ring, 32, 128), BF16),
        compiler_params=grant(8),
        name="scan",
    )(spread, roll0)
    entering = lax.all_to_all(entering, "seq", split_axis=0, concat_axis=0, tiled=True)

    group = lax.axis_size("head")
    normed, sums = pl.pallas_call(
        norm_kernel,
        in_specs=[vmem] * 4 + [hbm] * 6,
        out_specs=[hbm, vmem],
        out_shape=[pltpu.HBM((rows, width), BF16), jax.ShapeDtypeStruct((group, 2 * chunks, CHUNK), F32)],
        scratch_shapes=[pltpu.VMEM((STATE, width), BF16), pltpu.VMEM((2, CHUNK, width), F32)]
        + [pltpu.VMEM((rows, width // 2), BF16)] * 2
        + [pltpu.VMEM((rows, width), BF16)] * 2
        + [pltpu.VMEM((1, width), F32)]
        + [pltpu.VMEM((chunks, CHUNK), F32)] * 3
        + [pltpu.SemaphoreType.DMA((3, chunks // 2))]
        + [pltpu.SemaphoreType.DMA((chunks // 2,)), pltpu.SemaphoreType.DMA((3,))],
        compiler_params=grant(24),
        cost_estimate=pl.CostEstimate(flops=1 << 28, bytes_accessed=8 << 20, transcendentals=1 << 10),
        name="norms",
    )(entering, a1, f1, cc, a0, f0, rollout, gain_row, roll0, roll1)

    sums = jnp.sum(lax.all_to_all(sums, "head", split_axis=0, concat_axis=0, tiled=True), axis=0)
    relative = jnp.sqrt(sums[:chunks] / (sums[chunks:] + 1e-06))
    return normed, relative.reshape(rows)


def solution(mesh):
    placed = (
        P("seq", "head"), P("seq", "head"), P("seq", "head"), P("seq", "head"), P("seq", "head"),
        P("head"), P("head"), P(None, "head"), P(None, None, "head"), P("head"), P("seq", "head"), P(),
    )
    return jax.shard_map(
        shards, mesh=mesh, in_specs=placed, out_specs=(P("seq", "head"), P("seq")), check_vma=False
    )
```

```python
import functools

import jax
import jax.numpy as jnp
from jax import lax
from jax.experimental import pallas as pl
from jax.experimental.pallas import tpu as pltpu
from jax.sharding import PartitionSpec as P

HEADS = 128
HEAD_DIM = 64
STATE = 128
GROUPS = 8
CONV_K = 4
SPAN = 256
CHUNK = 128
LANES = 256
HALO = 16
MSG = 34

F32 = jnp.float32
BF16 = jnp.bfloat16


def parts3(v):
    hi = v.astype(BF16)
    rest = v - hi.astype(F32)
    mid = rest.astype(BF16)
    low = (rest - mid.astype(F32)).astype(BF16)
    return hi, mid, low


def silu_half(h):
    return h + h * jnp.tanh(h)


def mm(a, b):
    return jnp.dot(a, b, preferred_element_type=F32)


def one_hot(lane0, width=LANES):
    r = lax.broadcasted_iota(jnp.int32, (256, width), 0)
    c = lax.broadcasted_iota(jnp.int32, (256, width), 1)
    return jnp.where((r & 127) == (c + lane0) // HEAD_DIM, 1.0, 0.0).astype(BF16)


def span_keep(seq_ref, span):
    start = seq_ref[0] * 0
    fresh = span == start
    for i in range(seq_ref.shape[0] - 1):
        start = start + seq_ref[i]
        fresh = fresh | (span == start)
    return jnp.where(fresh, 0.0, 1.0).astype(F32)


def conv_block(padded_ref, taps):
    rows = padded_ref.shape[0] - 8
    total = padded_ref[pl.ds(5, rows), :] * taps[0:1]
    for k in range(1, CONV_K):
        total = total + padded_ref[pl.ds(5 + k, rows), :] * taps[k : k + 1]
    return silu_half(total)


def conv_ordered(padded_ref, taps):
    per = CHUNK // 8
    shifted = {m: padded_ref[pl.ds(8 + m, 8, stride=per), :] for m in range(1 - CONV_K, per)}
    rows = []
    for j in range(per):
        total = shifted[j + 1 - CONV_K] * taps[0:1]
        for k in range(1, CONV_K):
            total = total + shifted[j + 1 - CONV_K + k] * taps[k : k + 1]
        rows.append(silu_half(total))
    return jnp.concatenate(rows, axis=0)


def turned(v, heads, chunk):
    turn = (128 - heads * chunk) % 128
    return pltpu.roll(v, turn, 1) if turn else v


def split2(v):
    hi = v.astype(BF16)
    return hi, (v - hi.astype(F32)).astype(BF16)


def stack_scales(source, heads, chunks, target):
    for k in range(chunks):
        hi, low = split2(turned(source, heads, k))
        target[k * CHUNK : (k + 1) * CHUNK, 0:128] = hi
        target[k * CHUNK : (k + 1) * CHUNK, 128:256] = low


def chunk_rates(ts_ref, rate_ref, chunks):
    steps = jnp.concatenate([ts_ref[:, k * CHUNK : (k + 1) * CHUNK] for k in range(chunks)], axis=0).T
    return steps, -steps * jnp.concatenate([rate_ref[...]] * chunks, axis=1)


def sum_rates(picks, rates):
    picks = picks.astype(BF16)
    r1, r2, r3 = parts3(rates)
    return mm(picks, r1) + (mm(picks, r2) + mm(picks, r3))


def spread_rows(v, e):
    n = v.shape[0]
    out = mm(jnp.concatenate(parts3(v), axis=0), e[0:128])
    return out[0:n] + (out[n : 2 * n] + out[2 * n : 3 * n])


def chunk_keeps(chunks, seq_ref, rank_ref):
    per_span = SPAN // CHUNK
    first = rank_ref[0] * (chunks // per_span)
    return [None if k % per_span else span_keep(seq_ref, first + k // per_span) for k in range(chunks)]


def fill_padded(padded_ref, src_ref, edge, k, lanes, keep):
    if k == 0:
        halo = edge
    else:
        halo = src_ref[k * CHUNK - HALO : k * CHUNK, lanes].astype(F32)[HALO - 8 :]
    padded_ref[0:8, :] = halo if keep is None else halo * keep
    padded_ref[8 : 8 + CHUNK, :] = src_ref[k * CHUNK : (k + 1) * CHUNK, lanes].astype(F32)


def tail_kernel(
    chunks, seq_ref, rank_ref, x_ref, b_ref, c_ref, b_all_ref, ts_ref, rate_ref, wx_ref, wbc_ref,
    tail_ref, b_out, ts_out, rate_out, taps_ref, keep_ref,
):
    width = x_ref.shape[1]
    tail_ref[:, 0:width] = x_ref[...]
    tail_ref[:, width : width + STATE] = b_ref[...]
    tail_ref[:, width + STATE : width + 2 * STATE] = c_ref[...]
    b_out[...] = b_all_ref[...]
    ts_out[...] = ts_ref[...]
    rate_out[...] = rate_ref[...]
    taps_ref[...] = jnp.zeros_like(taps_ref)
    taps_ref[0:CONV_K, 0:width] = wx_ref[...].astype(F32) * 0.5
    taps_ref[0:CONV_K, width : width + STATE] = wbc_ref[0].astype(F32) * 0.5
    keeps = [v for v in chunk_keeps(chunks, seq_ref, rank_ref) if v is not None]
    row = lax.broadcasted_iota(jnp.int32, (8, 128), 0)
    flags = jnp.ones((8, 128), F32)
    for i, keep in enumerate(keeps):
        flags = jnp.where(row == i, keep, flags)
    keep_ref[...] = flags


def state_kernel(
    chunks, x_hbm, b_ref, ts_ref, rate_ref, taps_ref, keep_ref,
    end_ref, head_scale_ref, chain_ref, head_ref,
    x_all, padded, order, lhsu, wide, bt, xs, x_sems,
):
    blocks = x_all.shape[0]
    width = blocks * LANES
    heads = ts_ref.shape[0]

    def x_copy(i):
        lanes = pl.ds(pl.multiple_of(i * LANES, LANES), LANES)
        return pltpu.make_async_copy(x_hbm.at[:, lanes], x_all.at[i], x_sems.at[i])

    def start(i, carry):
        x_copy(i).start()
        return carry

    lax.fori_loop(0, blocks, start, 0)
    steps, rates = chunk_rates(ts_ref, rate_ref, chunks)
    t = lax.broadcasted_iota(jnp.int32, (CHUNK + 16, CHUNK), 0)
    u = lax.broadcasted_iota(jnp.int32, (CHUNK + 16, CHUNK), 1)
    after = sum_rates(jnp.where((u > t) | (t >= CHUNK), 1.0, 0.0), rates)
    totals = after[CHUNK : CHUNK + 16]
    j = lax.broadcasted_iota(jnp.int32, (CHUNK, CHUNK), 0)
    k = lax.broadcasted_iota(jnp.int32, (CHUNK, CHUNK), 1)
    later = jnp.where((lax.rem(j, heads) == lax.rem(k, heads)) & (j > k), 1.0, 0.0).astype(BF16)
    t1, t2, t3 = parts3(totals)
    later = mm(t1, later) + (mm(t2, later) + mm(t3, later))
    lane = lax.broadcasted_iota(jnp.int32, (16, 128), 1)
    reached = jnp.ones((16, 128), F32)
    whole = jnp.exp(later + totals)
    for n in range(0, chunks, SPAN // CHUNK):
        keep = keep_ref[n * CHUNK // SPAN : n * CHUNK // SPAN + 1, :]
        reached = jnp.where(lane < n * heads, reached * keep, reached)
        whole = whole * keep
    scale = jnp.exp(after[0:CHUNK] + later[0:1]) * steps * reached[0:1]
    order[...] = scale
    per = CHUNK // 8
    stack_scales(jnp.concatenate([order[pl.ds(n, 8, stride=per), :] for n in range(per)], axis=0), heads, chunks, lhsu)
    e = one_hot(0, width)
    wide_all = mm(lhsu[...], e)
    for i in range(blocks):
        wide[i] = wide_all[:, i * LANES : (i + 1) * LANES]
    head_scale_ref[...] = mm(jnp.concatenate(split2(scale[0:HALO]), axis=1), e)
    row = lax.broadcasted_iota(jnp.int32, (16, 1), 0)
    hi, low = split2(whole)
    p = jnp.where(row == 0, hi.astype(F32), jnp.where(row == 1, low.astype(F32), 0.0))
    chain_ref[...] = mm(p.astype(BF16), e[0:128])[0:8]
    taps = taps_ref[0:CONV_K, width : width + STATE]
    none = jnp.zeros((8, 128), F32)

    per_span = SPAN // CHUNK
    keeps = [None if k % per_span else keep_ref[k // per_span : k // per_span + 1, :] for k in range(chunks)]
    for k in range(chunks):
        pad = padded.at[k % 4]
        fill_padded(pad, b_ref, none, k, slice(0, STATE), keeps[k])
        v = conv_ordered(pad, taps)
        if k == 0:
            v = jnp.where((lax.broadcasted_iota(jnp.int32, v.shape, 0) & 7) == 0, 0.0, v)
        bt[:, k * CHUNK : (k + 1) * CHUNK] = v.T.astype(BF16)
    head_ref[:, width : width + STATE] = b_ref[0:HALO, :]

    def block(i, carry):
        lane0 = pl.multiple_of(i * LANES, LANES)
        lanes = pl.ds(lane0, LANES)
        x_ref = x_all.at[i]
        weights = taps_ref[0:CONV_K, lanes]
        x_copy(i).wait()
        head_ref[:, lanes] = x_ref[0:HALO, :]

        for k in range(chunks):
            toks = slice(k * CHUNK, (k + 1) * CHUNK)
            for part in range(LANES // 128):
                cols = slice(part * 128, (part + 1) * 128)
                pad = padded.at[(2 * k + part) % 4]
                fill_padded(pad, x_ref, none, k, cols, keeps[k])
                v = conv_ordered(pad, weights[:, cols])
                xs[i, toks, cols] = (v * wide[i, toks, cols]).astype(BF16)
        return carry

    lax.fori_loop(0, blocks, block, 0)
    for i in range(blocks):
        end_ref[:, i * LANES : (i + 1) * LANES] = mm(bt[...], xs[i])


def edge_kernel(edge_ref, head_ref, taps_ref, keep_ref, scale_ref, end_ref, chain_ref, msg_ref, flat):
    width = end_ref.shape[1]
    b_cols = slice(width, width + STATE)

    def conv(cols):
        taps = taps_ref[:, cols]
        before = edge_ref[:, cols].astype(F32)[HALO - 8 :] * keep_ref[0:1, 0:1]
        joined = jnp.concatenate([before, head_ref[:, cols].astype(F32)], axis=0)
        total = joined[5 : 5 + HALO] * taps[0:1]
        for k in range(1, CONV_K):
            total = total + joined[5 + k : 5 + k + HALO] * taps[k : k + 1]
        return silu_half(total)

    bc = conv(b_cols)
    bt = jnp.concatenate([bc, jnp.zeros((STATE - HALO, STATE), F32)], axis=0).T[:, 0:HALO].astype(BF16)

    for i in range(width // LANES):
        cols = slice(i * LANES, (i + 1) * LANES)
        v = conv(cols)
        xs = (v * scale_ref[:, cols]).astype(BF16)
        state = end_ref[:, cols] + mm(bt, xs)
        decay = chain_ref[0 : MSG - 32, cols]
        for part in range(LANES // 128):
            block = slice(part * 128, (part + 1) * 128)
            for nb in range(4):
                first = MSG * ((i * (LANES // 128) + part) * 4 + nb)
                flat[first : first + 32, :] = state[nb * 32 : (nb + 1) * 32, block]
                flat[first + 32 : first + MSG, :] = decay[:, block]
    msg_ref[...] = flat[...].astype(BF16)


def scan_kernel(in_ref, after_ref, out_ref, flat):
    flat[...] = in_ref[...].astype(F32)
    carried = jnp.zeros((32, 128), F32)
    for i in range(out_ref.shape[0]):
        first = MSG * i
        out_ref[i] = carried.astype(BF16)
        decay = flat[first + 32 : first + 33, :] + flat[first + 33 : first + 34, :]
        carried = carried * decay + flat[first : first + 32, :]


def mix_first(chunks, seq_ref, rank_ref, b_ref, c_ref, edge_ref, wbc_ref, left, bt, cc_ref, padded):
    t = lax.broadcasted_iota(jnp.int32, (CHUNK, CHUNK), 0)
    u = lax.broadcasted_iota(jnp.int32, (CHUNK, CHUNK), 1)
    edges = edge_ref[...].astype(F32)[HALO - 8 :]

    keeps = chunk_keeps(chunks, seq_ref, rank_ref)
    for k in range(chunks):
        toks = slice(k * CHUNK, (k + 1) * CHUNK)
        pair = []
        for i, ref in enumerate((b_ref, c_ref)):
            pad = padded.at[(2 * k + i) % 4]
            fill_padded(pad, ref, edges[:, i * STATE : (i + 1) * STATE], k, slice(0, STATE), keeps[k])
            pair.append(conv_block(pad, wbc_ref[i].astype(F32) * 0.5))
        b, c = pair
        bt[k] = b.T.astype(BF16)
        c = c.astype(BF16)
        cc_ref[toks, :] = c
        left[toks, 128:256] = c
        g = lax.dot_general(c, b.astype(BF16), (((1,), (1,)), ((), ())), preferred_element_type=F32)
        left[toks, 0:128] = jnp.where(u <= t, g, 0.0).astype(BF16)


def mix_kernel(
    chunks, lane_first, seq_ref, rank_ref, x_ref, edge_ref, ts_ref, rate_ref, z_ref, roll_ref, wx_ref, skip_ref, *refs
):
    if lane_first == 0:
        b_ref, c_ref, bc_edge_ref, wbc_ref, a_ref, f_ref, roll_sum_ref, left, bt, cc_ref = refs[:10]
    else:
        left, bt, a_ref, f_ref, roll_sum_ref = refs[:5]
    padded, wide_u, wide_t, part, state, lhsu, lhst, ends_all, rows = refs[-9:]
    heads = skip_ref.shape[1]

    @pl.when(pl.program_id(0) == 0)
    def _():
        if lane_first == 0:
            mix_first(chunks, seq_ref, rank_ref, b_ref, c_ref, bc_edge_ref, wbc_ref, left, bt, cc_ref, padded)
        steps, rates = chunk_rates(ts_ref, rate_ref, chunks)
        t = lax.broadcasted_iota(jnp.int32, (CHUNK + 16, CHUNK), 0)
        u = lax.broadcasted_iota(jnp.int32, (CHUNK + 16, CHUNK), 1)
        half = jnp.where(u < CHUNK // 2, 1.0, 0.0)
        tri = jnp.where(u <= t, 1.0, 0.0) - half
        cum = sum_rates(jnp.where(t < CHUNK, tri, jnp.where(t == CHUNK, half, 1.0)), rates)
        rel = cum[:CHUNK]
        stack_scales(jnp.exp(-rel) * steps, heads, chunks, lhsu)
        stack_scales(jnp.exp(rel), heads, chunks, lhst)
        ends = jnp.exp(jnp.concatenate([rel[CHUNK - 8 :], cum[CHUNK : CHUNK + 8]], axis=0))
        for k in range(chunks):
            ends_all[k] = turned(ends, heads, k)
        part[...] = jnp.zeros_like(part)

    e = one_hot(lane_first + pl.program_id(0) * LANES)
    rows[...] = spread_rows(ends_all[...].reshape(16 * chunks, 128), e).reshape(chunks, 16, LANES)
    wide_u[...] = mm(lhsu[...], e)
    wide_t[...] = mm(lhst[...], e)
    s1, s2, s3 = parts3(skip_ref[...])
    skip = mm(jnp.concatenate([s1.astype(F32), s2.astype(F32), s3.astype(F32)], axis=0).astype(BF16), e[0:heads])
    skip = skip[0:1] + (skip[1:2] + skip[2:3])
    state[...] = jnp.zeros_like(state)
    edges = edge_ref[...].astype(F32)[HALO - 8 :]
    weights = wx_ref[...].astype(F32) * 0.5

    keeps = chunk_keeps(chunks, seq_ref, rank_ref)
    reach = jnp.ones((1, LANES), F32)
    for k in range(chunks):
        toks = slice(k * CHUNK, (k + 1) * CHUNK)
        to_end, to_mid, whole = rows[k, 7:8, :], rows[k, 8:9, :], rows[k, 9:10, :]
        xs, direct = [], []
        for lane in range(0, LANES, 128):
            cols = slice(lane, lane + 128)
            pad = padded.at[(2 * k + lane // 128) % 4]
            fill_padded(pad, x_ref, edges[:, cols], k, cols, keeps[k])
            v = conv_block(pad, weights[:, cols])
            xs.append((v * wide_u[toks, cols]).astype(BF16))
            direct.append(v.astype(BF16).astype(F32) * skip[:, cols])
        xs, direct = jnp.concatenate(xs, axis=1), jnp.concatenate(direct, axis=1)
        before = state[...]
        if keeps[k] is not None:
            before = before * keeps[k]
            reach = reach * keeps[k]
        state[...] = before * whole + mm(bt[k], xs) * to_end
        right = jnp.concatenate([xs, (before * to_mid).astype(BF16)], axis=0)
        inner = mm(left[toks, :], right)
        scale = wide_t[toks, :]
        gate = silu_half(z_ref[toks, :].astype(F32) * 0.5)
        a_ref[toks, :] = ((inner * scale + direct) * gate).astype(BF16)
        f_ref[toks, :] = (scale * gate * (reach * to_mid)).astype(BF16)
        r = roll_ref[toks, :].astype(F32)
        r = r * r
        part[toks, :] += r[:, 0:128] + r[:, 128:256]
        reach = reach * whole

    @pl.when(pl.program_id(0) == pl.num_programs(0) - 1)
    def _():
        for k in range(chunks):
            roll_sum_ref[k : k + 1, :] = jnp.sum(part[k * CHUNK : (k + 1) * CHUNK, :].T, axis=0, keepdims=True)


def norm_kernel(
    in_ref, a1_all, f1_all, cc_ref, a0_hbm, f0_hbm, roll_hbm, gain_hbm, roll0_hbm, roll1_hbm, out_hbm, sums_ref,
    entering, gated, a0_all, f0_all, roll_all, out_all, gain_ref, roll0_ref, roll1_ref, sums,
    in_sems, out_sems, small_sems,
):
    width = out_all.shape[1]
    chunks, half = out_all.shape[0] // CHUNK, a0_all.shape[1]
    pairs = [(a0_hbm, a0_all), (f0_hbm, f0_all), (roll_hbm, roll_all)]
    smalls = [(gain_hbm, gain_ref), (roll0_hbm, roll0_ref), (roll1_hbm, roll1_ref)]
    size = 2 * CHUNK

    def copy_in(i, m):
        here = pl.ds(pl.multiple_of(m * size, size), size)
        return pltpu.make_async_copy(pairs[i][0].at[here], pairs[i][1].at[here], in_sems.at[i, m])

    def copy_out(m):
        here = pl.ds(pl.multiple_of(m * size, size), size)
        return pltpu.make_async_copy(out_all.at[here], out_hbm.at[here], out_sems.at[m])

    def copy_small(i):
        return pltpu.make_async_copy(*smalls[i], small_sems.at[i])

    for m in range(chunks // 2):
        for i in range(len(pairs)):
            copy_in(i, m).start()
        if m == 0:
            for i in range(len(smalls)):
                copy_small(i).start()
    for lb in range(width // 128):
        for nb in range(4):
            entering[nb * 32 : (nb + 1) * 32, lb * 128 : (lb + 1) * 128] = in_ref[lb * 4 + nb]
    def two(m, carry):
        scales = []
        for n in range(2):
            toks = pl.ds(pl.multiple_of(m * size + n * CHUNK, CHUNK), CHUNK)
            squares = jnp.zeros((CHUNK, 128), F32)
            for lane in [*range(half, width, LANES), *range(0, half, LANES)]:
                cols = slice(lane, lane + LANES)
                if n == 0 and lane == 0:
                    copy_in(0, m).wait()
                    copy_in(1, m).wait()
                a_ref, f_ref = (a0_all, f0_all) if lane < half else (a1_all, f1_all)
                own = slice(lane % half, lane % half + LANES)
                g = a_ref[toks, own].astype(F32) + f_ref[toks, own].astype(F32) * mm(cc_ref[toks, :], entering[:, cols])
                gated[n, :, cols] = g
                g = g * g
                squares = squares + (g[:, 0:128] + g[:, 128:256])
            mean = jnp.sum(squares, axis=1, keepdims=True) * (1.0 / width)
            scales.append(lax.rsqrt(mean + 1e-05))
        copy_in(2, m).wait()

        @pl.when(m == 0)
        def _():
            copy_small(0).wait()

        for n in range(2):
            k = 2 * m + n
            toks = pl.ds(pl.multiple_of(k * CHUNK, CHUNK), CHUNK)
            squares = jnp.zeros((CHUNK, 128), F32)
            for lane in range(0, width, 128):
                cols = slice(lane, lane + 128)
                v = (gated[n, :, cols] * scales[n] * gain_ref[:, cols]).astype(BF16)
                out_all[toks, cols] = v
                d = v.astype(F32) - roll_all[toks, cols].astype(F32)
                squares = squares + d * d
            sums[pl.ds(k, 1), :] = jnp.sum(squares.T, axis=0, keepdims=True)
        copy_out(m).start()
        return carry

    lax.fori_loop(0, chunks // 2, two, 0)
    copy_small(1).wait()
    copy_small(2).wait()
    both = jnp.concatenate([sums[...], roll0_ref[...] + roll1_ref[...]], axis=0)
    for i in range(sums_ref.shape[0]):
        sums_ref[i] = both
    for m in range(chunks // 2):
        copy_out(m).wait()


def shards(
    x_values, b_values, c_values, z_values, time_steps, decay_rate, skip_gain,
    conv_x, conv_bc, norm_gain, rollout, seq_spans,
):
    ring = lax.axis_size("seq")
    rows, width = x_values.shape
    heads = decay_rate.shape[0]
    chunks = rows // CHUNK
    blocks = width // LANES
    rank = lax.axis_index("seq").astype(jnp.int32).reshape(1)

    ends = width + 2 * STATE
    smem = pl.BlockSpec(memory_space=pltpu.SMEM)

    def whole(*shape):
        return pl.BlockSpec(shape, lambda i: (0,) * len(shape))

    def lane_block(r, first=0):
        return pl.BlockSpec((r, LANES), lambda i: (0, first + i))

    def grant(mib):
        return pltpu.CompilerParams(vmem_limit_bytes=mib * 1024 * 1024)

    def in_hbm(*arrays):
        return [pltpu.with_memory_space_constraint(v, pltpu.HBM) for v in arrays]

    x_values, b_values, c_values, z_values, rollout = in_hbm(x_values, b_values, c_values, z_values, rollout)
    (seq_spans,) = in_hbm(seq_spans)
    steps_row, rate_row, skip_row, gain_row, conv_x, conv_bc = in_hbm(
        time_steps.T, decay_rate.reshape(1, heads), skip_gain.reshape(1, heads), norm_gain.reshape(1, width), conv_x, conv_bc
    )
    last = rows // HALO - 1
    vmem = pl.BlockSpec(memory_space=pltpu.VMEM)
    hbm = pl.BlockSpec(memory_space=pl.ANY)
    edge, b_near, steps_near, rate_near, taps, keeps = pl.pallas_call(
        functools.partial(tail_kernel, chunks),
        grid=(1,),
        in_specs=[smem, smem]
        + [pl.BlockSpec((HALO, n), lambda i: (last, 0)) for n in (width, STATE, STATE)]
        + [whole(rows, STATE), whole(heads, rows), whole(1, heads), whole(CONV_K, width), whole(2, CONV_K, STATE)],
        out_specs=[
            whole(HALO, ends), whole(rows, STATE), whole(heads, rows), whole(1, heads), whole(8, width + STATE), whole(8, 128),
        ],
        out_shape=[
            jax.ShapeDtypeStruct((HALO, ends), BF16),
            pltpu.VMEM((rows, STATE), BF16),
            pltpu.VMEM((heads, rows), F32),
            pltpu.VMEM((1, heads), F32),
            pltpu.VMEM((8, width + STATE), F32),
            pltpu.VMEM((8, 128), F32),
        ],
        compiler_params=grant(8),
        name="tails",
    )(seq_spans, rank, x_values, b_values, c_values, b_values, steps_row, rate_row, conv_x, conv_bc)
    edge = lax.ppermute(edge, "seq", [(i, i + 1) for i in range(ring - 1)])
    conv_scratch = pltpu.VMEM((4, 8 + CHUNK, 128), F32)
    wide_scratch = pltpu.VMEM((rows, LANES), F32)

    end, head_scale, chain, head = pl.pallas_call(
        functools.partial(state_kernel, chunks),
        in_specs=[hbm] + [vmem] * 5,
        out_specs=[vmem] * 4,
        out_shape=[
            jax.ShapeDtypeStruct((STATE, width), F32),
            jax.ShapeDtypeStruct((HALO, width), F32),
            jax.ShapeDtypeStruct((8, width), F32),
            jax.ShapeDtypeStruct((HALO, width + STATE), BF16),
        ],
        scratch_shapes=[
            pltpu.VMEM((blocks, rows, LANES), BF16),
            conv_scratch,
            pltpu.VMEM((CHUNK, 128), F32),
            pltpu.VMEM((rows, 256), BF16),
            pltpu.VMEM((blocks, rows, LANES), F32),
            pltpu.VMEM((STATE, rows), BF16),
            pltpu.VMEM((blocks, rows, LANES), BF16),
            pltpu.SemaphoreType.DMA((blocks,)),
        ],
        compiler_params=grant(16),
        cost_estimate=pl.CostEstimate(flops=1 << 29, bytes_accessed=4 << 20, transcendentals=1 << 20),
        name="states",
    )(x_values, b_near, steps_near, rate_near, taps, keeps)

    msg = pl.pallas_call(
        edge_kernel,
        out_shape=jax.ShapeDtypeStruct((ring * MSG, 128), BF16),
        scratch_shapes=[pltpu.VMEM((ring * MSG, 128), F32)],
        compiler_params=grant(8),
        name="edge_states",
    )(edge, head, taps, keeps, head_scale, end, chain)
    edge = pltpu.with_memory_space_constraint(edge, pltpu.VMEM)

    msg = msg.reshape(ring, MSG // 2, 2, 128)
    spread = lax.all_to_all(msg, "seq", split_axis=0, concat_axis=0, tiled=True).reshape(ring * MSG, 128)

    def mix(first, specs, operands, more_specs, more_shapes):
        half = blocks // 2
        place = pltpu.HBM if first == 0 else pltpu.VMEM
        return pl.pallas_call(
            functools.partial(mix_kernel, chunks, first * LANES),
            grid=(half,),
            in_specs=[
                smem, smem, lane_block(rows, first), lane_block(HALO, first), whole(heads, rows), whole(1, heads),
                lane_block(rows, first), lane_block(rows, first), lane_block(CONV_K, first), whole(1, heads),
            ]
            + specs,
            out_specs=[lane_block(rows), lane_block(rows), whole(chunks, CHUNK)] + more_specs,
            out_shape=[
                place((rows, half * LANES), BF16),
                place((rows, half * LANES), BF16),
                pltpu.HBM((chunks, CHUNK), F32),
            ]
            + more_shapes,
            scratch_shapes=[
                conv_scratch, wide_scratch, wide_scratch, pltpu.VMEM((rows, 128), F32), pltpu.VMEM((STATE, LANES), F32),
                pltpu.VMEM((rows, 256), BF16), pltpu.VMEM((rows, 256), BF16), pltpu.VMEM((chunks, 16, 128), F32),
                pltpu.VMEM((chunks, 16, LANES), F32),
            ],
            compiler_params=grant(32),
            cost_estimate=pl.CostEstimate(flops=1 << 30, bytes_accessed=9 << 20, transcendentals=1 << 20),
            name="mix_first" if first == 0 else "mix_second",
        )(
            seq_spans, rank, x_values, edge, steps_row, rate_row, z_values, rollout, conv_x,
            skip_row, *operands,
        )

    shared_specs = [whole(rows, 256), whole(chunks, STATE, CHUNK)]
    a0, f0, roll0, left, bt, cc = mix(
        0,
        [
            whole(rows, STATE), whole(rows, STATE), pl.BlockSpec((HALO, 2 * STATE), lambda i: (0, width // (2 * STATE))),
            whole(2, CONV_K, STATE),
        ],
        [b_values, c_values, edge, conv_bc],
        shared_specs + [whole(rows, STATE)],
        [
            pltpu.HBM((rows, 256), BF16),
            pltpu.HBM((chunks, STATE, CHUNK), BF16),
            pltpu.VMEM((rows, STATE), BF16),
        ],
    )
    a0, f0, roll0, left, bt = in_hbm(a0, f0, roll0, left, bt)
    cc = pltpu.with_memory_space_constraint(cc, pltpu.VMEM)
    a1, f1, roll1 = mix(blocks // 2, shared_specs, [left, bt], [], [])
    a1, f1 = (pltpu.with_memory_space_constraint(v, pltpu.VMEM) for v in (a1, f1))
    (roll1,) = in_hbm(roll1)

    entering = pl.pallas_call(
        scan_kernel,
        in_specs=[pl.BlockSpec(memory_space=pltpu.VMEM), pl.BlockSpec(memory_space=pl.ANY)],
        out_shape=jax.ShapeDtypeStruct((ring, 32, 128), BF16),
        scratch_shapes=[pltpu.VMEM((ring * MSG, 128), F32)],
        compiler_params=grant(8),
        name="scan",
    )(spread, roll0)
    entering = lax.all_to_all(entering, "seq", split_axis=0, concat_axis=0, tiled=True)

    group = lax.axis_size("head")
    normed, sums = pl.pallas_call(
        norm_kernel,
        in_specs=[vmem] * 4 + [hbm] * 6,
        out_specs=[hbm, vmem],
        out_shape=[pltpu.HBM((rows, width), BF16), jax.ShapeDtypeStruct((group, 2 * chunks, CHUNK), F32)],
        scratch_shapes=[pltpu.VMEM((STATE, width), BF16), pltpu.VMEM((2, CHUNK, width), F32)]
        + [pltpu.VMEM((rows, width // 2), BF16)] * 2
        + [pltpu.VMEM((rows, width), BF16)] * 2
        + [pltpu.VMEM((1, width), F32)]
        + [pltpu.VMEM((chunks, CHUNK), F32)] * 3
        + [pltpu.SemaphoreType.DMA((3, chunks // 2))]
        + [pltpu.SemaphoreType.DMA((chunks // 2,)), pltpu.SemaphoreType.DMA((3,))],
        compiler_params=grant(24),
        cost_estimate=pl.CostEstimate(flops=1 << 28, bytes_accessed=8 << 20, transcendentals=1 << 10),
        name="norms",
    )(entering, a1, f1, cc, a0, f0, rollout, gain_row, roll0, roll1)

    sums = jnp.sum(lax.all_to_all(sums, "head", split_axis=0, concat_axis=0, tiled=True), axis=0)
    relative = jnp.sqrt(sums[:chunks] / (sums[chunks:] + 1e-06))
    return normed, relative.reshape(rows)


def solution(mesh):
    placed = (
        P("seq", "head"), P("seq", "head"), P("seq", "head"), P("seq", "head"), P("seq", "head"),
        P("head"), P("head"), P(None, "head"), P(None, None, "head"), P("head"), P("seq", "head"), P(),
    )
    return jax.shard_map(
        shards, mesh=mesh, in_specs=placed, out_specs=(P("seq", "head"), P("seq")), check_vma=False
    )
```

```python
import functools

import jax
import jax.numpy as jnp
from jax import lax
from jax.experimental import pallas as pl
from jax.experimental.pallas import tpu as pltpu
from jax.sharding import PartitionSpec as P

HEADS = 128
HEAD_DIM = 64
STATE = 128
GROUPS = 8
CONV_K = 4
SPAN = 256
CHUNK = 128
LANES = 256
HALO = 16
MSG = 34

F32 = jnp.float32
BF16 = jnp.bfloat16


def parts3(v):
    hi = v.astype(BF16)
    rest = v - hi.astype(F32)
    mid = rest.astype(BF16)
    low = (rest - mid.astype(F32)).astype(BF16)
    return hi, mid, low


def silu_half(h):
    return h + h * jnp.tanh(h)


def mm(a, b):
    return jnp.dot(a, b, preferred_element_type=F32)


def one_hot(lane0, width=LANES):
    r = lax.broadcasted_iota(jnp.int32, (256, width), 0)
    c = lax.broadcasted_iota(jnp.int32, (256, width), 1)
    return jnp.where((r & 127) == (c + lane0) // HEAD_DIM, 1.0, 0.0).astype(BF16)


def span_keep(seq_ref, span):
    start = seq_ref[0] * 0
    fresh = span == start
    for i in range(seq_ref.shape[0] - 1):
        start = start + seq_ref[i]
        fresh = fresh | (span == start)
    return jnp.where(fresh, 0.0, 1.0).astype(F32)


def conv_block(padded_ref, taps):
    rows = padded_ref.shape[0] - 8
    total = padded_ref[pl.ds(5, rows), :] * taps[0:1]
    for k in range(1, CONV_K):
        total = total + padded_ref[pl.ds(5 + k, rows), :] * taps[k : k + 1]
    return silu_half(total)


def conv_ordered(padded_ref, taps):
    per = CHUNK // 8
    shifted = {m: padded_ref[pl.ds(8 + m, 8, stride=per), :] for m in range(1 - CONV_K, per)}
    rows = []
    for j in range(per):
        total = shifted[j + 1 - CONV_K] * taps[0:1]
        for k in range(1, CONV_K):
            total = total + shifted[j + 1 - CONV_K + k] * taps[k : k + 1]
        rows.append(silu_half(total))
    return jnp.concatenate(rows, axis=0)


def turned(v, heads, chunk):
    turn = (128 - heads * chunk) % 128
    return pltpu.roll(v, turn, 1) if turn else v


def split2(v):
    hi = v.astype(BF16)
    return hi, (v - hi.astype(F32)).astype(BF16)


def stack_scales(source, heads, chunks, target):
    for k in range(chunks):
        hi, low = split2(turned(source, heads, k))
        target[k * CHUNK : (k + 1) * CHUNK, 0:128] = hi
        target[k * CHUNK : (k + 1) * CHUNK, 128:256] = low


def chunk_rates(ts_ref, rate_ref, chunks):
    steps = jnp.concatenate([ts_ref[:, k * CHUNK : (k + 1) * CHUNK] for k in range(chunks)], axis=0).T
    return steps, -steps * jnp.concatenate([rate_ref[...]] * chunks, axis=1)


def sum_rates(picks, rates):
    picks = picks.astype(BF16)
    r1, r2, r3 = parts3(rates)
    return mm(picks, r1) + (mm(picks, r2) + mm(picks, r3))


def spread_rows(v, e):
    n = v.shape[0]
    out = mm(jnp.concatenate(parts3(v), axis=0), e[0:128])
    return out[0:n] + (out[n : 2 * n] + out[2 * n : 3 * n])


def chunk_keeps(chunks, seq_ref, rank_ref):
    per_span = SPAN // CHUNK
    first = rank_ref[0] * (chunks // per_span)
    return [None if k % per_span else span_keep(seq_ref, first + k // per_span) for k in range(chunks)]


def fill_padded(padded_ref, src_ref, edge, k, lanes, keep):
    if k == 0:
        halo = edge
    else:
        halo = src_ref[k * CHUNK - HALO : k * CHUNK, lanes].astype(F32)[HALO - 8 :]
    padded_ref[0:8, :] = halo if keep is None else halo * keep
    padded_ref[8 : 8 + CHUNK, :] = src_ref[k * CHUNK : (k + 1) * CHUNK, lanes].astype(F32)


def tail_kernel(
    chunks, seq_ref, rank_ref, x_ref, b_ref, c_ref, b_all_ref, ts_ref, rate_ref, wx_ref, wbc_ref,
    tail_ref, b_out, ts_out, rate_out, taps_ref, keep_ref,
):
    width = x_ref.shape[1]
    tail_ref[:, 0:width] = x_ref[...]
    tail_ref[:, width : width + STATE] = b_ref[...]
    tail_ref[:, width + STATE : width + 2 * STATE] = c_ref[...]
    b_out[...] = b_all_ref[...]
    ts_out[...] = ts_ref[...]
    rate_out[...] = rate_ref[...]
    taps_ref[...] = jnp.zeros_like(taps_ref)
    taps_ref[0:CONV_K, 0:width] = wx_ref[...].astype(F32) * 0.5
    taps_ref[0:CONV_K, width : width + STATE] = wbc_ref[0].astype(F32) * 0.5
    keeps = [v for v in chunk_keeps(chunks, seq_ref, rank_ref) if v is not None]
    row = lax.broadcasted_iota(jnp.int32, (8, 128), 0)
    flags = jnp.ones((8, 128), F32)
    for i, keep in enumerate(keeps):
        flags = jnp.where(row == i, keep, flags)
    keep_ref[...] = flags


def state_kernel(
    chunks, x_hbm, b_ref, ts_ref, rate_ref, taps_ref, keep_ref,
    end_ref, head_scale_ref, chain_ref, head_ref,
    x_all, padded, order, lhsu, wide, bt, xs, x_sems,
):
    blocks = x_all.shape[0]
    width = blocks * LANES
    heads = ts_ref.shape[0]

    def x_copy(i):
        lanes = pl.ds(pl.multiple_of(i * LANES, LANES), LANES)
        return pltpu.make_async_copy(x_hbm.at[:, lanes], x_all.at[i], x_sems.at[i])

    def start(i, carry):
        x_copy(i).start()
        return carry

    lax.fori_loop(0, blocks, start, 0)
    steps, rates = chunk_rates(ts_ref, rate_ref, chunks)
    t = lax.broadcasted_iota(jnp.int32, (CHUNK + 16, CHUNK), 0)
    u = lax.broadcasted_iota(jnp.int32, (CHUNK + 16, CHUNK), 1)
    after = sum_rates(jnp.where((u > t) | (t >= CHUNK), 1.0, 0.0), rates)
    totals = after[CHUNK : CHUNK + 16]
    j = lax.broadcasted_iota(jnp.int32, (CHUNK, CHUNK), 0)
    k = lax.broadcasted_iota(jnp.int32, (CHUNK, CHUNK), 1)
    later = jnp.where((lax.rem(j, heads) == lax.rem(k, heads)) & (j > k), 1.0, 0.0).astype(BF16)
    t1, t2, t3 = parts3(totals)
    later = mm(t1, later) + (mm(t2, later) + mm(t3, later))
    lane = lax.broadcasted_iota(jnp.int32, (16, 128), 1)
    reached = jnp.ones((16, 128), F32)
    whole = jnp.exp(later + totals)
    for n in range(0, chunks, SPAN // CHUNK):
        keep = keep_ref[n * CHUNK // SPAN : n * CHUNK // SPAN + 1, :]
        reached = jnp.where(lane < n * heads, reached * keep, reached)
        whole = whole * keep
    scale = jnp.exp(after[0:CHUNK] + later[0:1]) * steps * reached[0:1]
    order[...] = scale
    per = CHUNK // 8
    stack_scales(jnp.concatenate([order[pl.ds(n, 8, stride=per), :] for n in range(per)], axis=0), heads, chunks, lhsu)
    e = one_hot(0, width)
    wide_all = mm(lhsu[...], e)
    for i in range(blocks):
        wide[i] = wide_all[:, i * LANES : (i + 1) * LANES]
    head_scale_ref[...] = mm(jnp.concatenate(split2(scale[0:HALO]), axis=1), e)
    row = lax.broadcasted_iota(jnp.int32, (16, 1), 0)
    hi, low = split2(whole)
    p = jnp.where(row == 0, hi.astype(F32), jnp.where(row == 1, low.astype(F32), 0.0))
    chain_ref[...] = mm(p.astype(BF16), e[0:128])[0:8]
    taps = taps_ref[0:CONV_K, width : width + STATE]
    none = jnp.zeros((8, 128), F32)

    per_span = SPAN // CHUNK
    keeps = [None if k % per_span else keep_ref[k // per_span : k // per_span + 1, :] for k in range(chunks)]
    for k in range(chunks):
        pad = padded.at[k % 4]
        fill_padded(pad, b_ref, none, k, slice(0, STATE), keeps[k])
        v = conv_ordered(pad, taps)
        if k == 0:
            v = jnp.where((lax.broadcasted_iota(jnp.int32, v.shape, 0) & 7) == 0, 0.0, v)
        bt[:, k * CHUNK : (k + 1) * CHUNK] = v.T.astype(BF16)
    head_ref[:, width : width + STATE] = b_ref[0:HALO, :]

    def block(i, carry):
        lane0 = pl.multiple_of(i * LANES, LANES)
        lanes = pl.ds(lane0, LANES)
        x_ref = x_all.at[i]
        weights = taps_ref[0:CONV_K, lanes]
        x_copy(i).wait()
        head_ref[:, lanes] = x_ref[0:HALO, :]

        for k in range(chunks):
            toks = slice(k * CHUNK, (k + 1) * CHUNK)
            for part in range(LANES // 128):
                cols = slice(part * 128, (part + 1) * 128)
                pad = padded.at[(2 * k + part) % 4]
                fill_padded(pad, x_ref, none, k, cols, keeps[k])
                v = conv_ordered(pad, weights[:, cols])
                xs[i, toks, cols] = (v * wide[i, toks, cols]).astype(BF16)
        return carry

    lax.fori_loop(0, blocks, block, 0)
    for i in range(blocks):
        end_ref[:, i * LANES : (i + 1) * LANES] = mm(bt[...], xs[i])


def edge_kernel(edge_ref, head_ref, taps_ref, keep_ref, scale_ref, end_ref, chain_ref, msg_ref, flat):
    width = end_ref.shape[1]
    b_cols = slice(width, width + STATE)

    def conv(cols):
        taps = taps_ref[:, cols]
        before = edge_ref[:, cols].astype(F32)[HALO - 8 :] * keep_ref[0:1, 0:1]
        joined = jnp.concatenate([before, head_ref[:, cols].astype(F32)], axis=0)
        total = joined[5 : 5 + HALO] * taps[0:1]
        for k in range(1, CONV_K):
            total = total + joined[5 + k : 5 + k + HALO] * taps[k : k + 1]
        return silu_half(total)

    bc = conv(b_cols)
    bt = jnp.concatenate([bc, jnp.zeros((STATE - HALO, STATE), F32)], axis=0).T[:, 0:HALO].astype(BF16)

    for i in range(width // LANES):
        cols = slice(i * LANES, (i + 1) * LANES)
        v = conv(cols)
        xs = (v * scale_ref[:, cols]).astype(BF16)
        state = end_ref[:, cols] + mm(bt, xs)
        decay = chain_ref[0 : MSG - 32, cols]
        for part in range(LANES // 128):
            block = slice(part * 128, (part + 1) * 128)
            for nb in range(4):
                first = MSG * ((i * (LANES // 128) + part) * 4 + nb)
                flat[first : first + 32, :] = state[nb * 32 : (nb + 1) * 32, block]
                flat[first + 32 : first + MSG, :] = decay[:, block]
    msg_ref[...] = flat[...].astype(BF16)


def scan_kernel(in_ref, after_ref, out_ref, flat):
    flat[...] = in_ref[...].astype(F32)
    carried = jnp.zeros((32, 128), F32)
    for i in range(out_ref.shape[0]):
        first = MSG * i
        out_ref[i] = carried.astype(BF16)
        decay = flat[first + 32 : first + 33, :] + flat[first + 33 : first + 34, :]
        carried = carried * decay + flat[first : first + 32, :]


def mix_first(chunks, seq_ref, rank_ref, b_ref, c_ref, edge_ref, wbc_ref, left, bt, cc_ref, padded):
    t = lax.broadcasted_iota(jnp.int32, (CHUNK, CHUNK), 0)
    u = lax.broadcasted_iota(jnp.int32, (CHUNK, CHUNK), 1)
    edges = edge_ref[...].astype(F32)[HALO - 8 :]

    keeps = chunk_keeps(chunks, seq_ref, rank_ref)
    for k in range(chunks):
        toks = slice(k * CHUNK, (k + 1) * CHUNK)
        pair = []
        for i, ref in enumerate((b_ref, c_ref)):
            pad = padded.at[(2 * k + i) % 4]
            fill_padded(pad, ref, edges[:, i * STATE : (i + 1) * STATE], k, slice(0, STATE), keeps[k])
            pair.append(conv_block(pad, wbc_ref[i].astype(F32) * 0.5))
        b, c = pair
        bt[k] = b.T.astype(BF16)
        c = c.astype(BF16)
        cc_ref[toks, :] = c
        left[toks, 128:256] = c
        g = lax.dot_general(c, b.astype(BF16), (((1,), (1,)), ((), ())), preferred_element_type=F32)
        left[toks, 0:128] = jnp.where(u <= t, g, 0.0).astype(BF16)


def mix_kernel(
    chunks, lane_first, seq_ref, rank_ref, x_ref, edge_ref, ts_ref, rate_ref, z_ref, roll_ref, wx_ref, skip_ref, *refs
):
    if lane_first == 0:
        b_ref, c_ref, bc_edge_ref, wbc_ref, a_ref, f_ref, roll_sum_ref, left, bt, cc_ref = refs[:10]
    else:
        left, bt, a_ref, f_ref, roll_sum_ref = refs[:5]
    padded, wide_u, wide_t, part, state, lhsu, lhst, ends_all, rows = refs[-9:]
    heads = skip_ref.shape[1]

    @pl.when(pl.program_id(0) == 0)
    def _():
        if lane_first == 0:
            mix_first(chunks, seq_ref, rank_ref, b_ref, c_ref, bc_edge_ref, wbc_ref, left, bt, cc_ref, padded)
        steps, rates = chunk_rates(ts_ref, rate_ref, chunks)
        t = lax.broadcasted_iota(jnp.int32, (CHUNK + 16, CHUNK), 0)
        u = lax.broadcasted_iota(jnp.int32, (CHUNK + 16, CHUNK), 1)
        half = jnp.where(u < CHUNK // 2, 1.0, 0.0)
        tri = jnp.where(u <= t, 1.0, 0.0) - half
        cum = sum_rates(jnp.where(t < CHUNK, tri, jnp.where(t == CHUNK, half, 1.0)), rates)
        rel = cum[:CHUNK]
        stack_scales(jnp.exp(-rel) * steps, heads, chunks, lhsu)
        stack_scales(jnp.exp(rel), heads, chunks, lhst)
        ends = jnp.exp(jnp.concatenate([rel[CHUNK - 8 :], cum[CHUNK : CHUNK + 8]], axis=0))
        for k in range(chunks):
            ends_all[k] = turned(ends, heads, k)
        part[...] = jnp.zeros_like(part)

    e = one_hot(lane_first + pl.program_id(0) * LANES)
    rows[...] = spread_rows(ends_all[...].reshape(16 * chunks, 128), e).reshape(chunks, 16, LANES)
    wide_u[...] = mm(lhsu[...], e)
    wide_t[...] = mm(lhst[...], e)
    s1, s2, s3 = parts3(skip_ref[...])
    skip = mm(jnp.concatenate([s1.astype(F32), s2.astype(F32), s3.astype(F32)], axis=0).astype(BF16), e[0:heads])
    skip = skip[0:1] + (skip[1:2] + skip[2:3])
    state[...] = jnp.zeros_like(state)
    edges = edge_ref[...].astype(F32)[HALO - 8 :]
    weights = wx_ref[...].astype(F32) * 0.5

    keeps = chunk_keeps(chunks, seq_ref, rank_ref)
    reach = jnp.ones((1, LANES), F32)
    for k in range(chunks):
        toks = slice(k * CHUNK, (k + 1) * CHUNK)
        to_end, to_mid, whole = rows[k, 7:8, :], rows[k, 8:9, :], rows[k, 9:10, :]
        xs, direct = [], []
        for lane in range(0, LANES, 128):
            cols = slice(lane, lane + 128)
            pad = padded.at[(2 * k + lane // 128) % 4]
            fill_padded(pad, x_ref, edges[:, cols], k, cols, keeps[k])
            v = conv_block(pad, weights[:, cols])
            xs.append((v * wide_u[toks, cols]).astype(BF16))
            direct.append(v.astype(BF16).astype(F32) * skip[:, cols])
        xs, direct = jnp.concatenate(xs, axis=1), jnp.concatenate(direct, axis=1)
        before = state[...]
        if keeps[k] is not None:
            before = before * keeps[k]
            reach = reach * keeps[k]
        state[...] = before * whole + mm(bt[k], xs) * to_end
        right = jnp.concatenate([xs, (before * to_mid).astype(BF16)], axis=0)
        inner = mm(left[toks, :], right)
        scale = wide_t[toks, :]
        gate = silu_half(z_ref[toks, :].astype(F32) * 0.5)
        a_ref[toks, :] = ((inner * scale + direct) * gate).astype(BF16)
        f_ref[toks, :] = (scale * gate * (reach * to_mid)).astype(BF16)
        r = roll_ref[toks, :].astype(F32)
        r = r * r
        part[toks, :] += r[:, 0:128] + r[:, 128:256]
        reach = reach * whole

    @pl.when(pl.program_id(0) == pl.num_programs(0) - 1)
    def _():
        for k in range(chunks):
            roll_sum_ref[k : k + 1, :] = jnp.sum(part[k * CHUNK : (k + 1) * CHUNK, :].T, axis=0, keepdims=True)


def norm_kernel(
    in_ref, a1_all, f1_all, cc_ref, a0_hbm, f0_hbm, roll_hbm, gain_hbm, roll0_hbm, roll1_hbm, out_hbm, sums_ref,
    entering, gated, a0_all, f0_all, roll_all, out_all, gain_ref, roll0_ref, roll1_ref, sums,
    in_sems, out_sems, small_sems,
):
    width = out_all.shape[1]
    chunks, half = out_all.shape[0] // CHUNK, a0_all.shape[1]
    pairs = [(a0_hbm, a0_all), (f0_hbm, f0_all), (roll_hbm, roll_all)]
    smalls = [(gain_hbm, gain_ref), (roll0_hbm, roll0_ref), (roll1_hbm, roll1_ref)]
    size = 2 * CHUNK

    def copy_in(i, m):
        here = pl.ds(pl.multiple_of(m * size, size), size)
        return pltpu.make_async_copy(pairs[i][0].at[here], pairs[i][1].at[here], in_sems.at[i, m])

    def copy_out(m):
        here = pl.ds(pl.multiple_of(m * size, size), size)
        return pltpu.make_async_copy(out_all.at[here], out_hbm.at[here], out_sems.at[m])

    def copy_small(i):
        return pltpu.make_async_copy(*smalls[i], small_sems.at[i])

    for m in range(chunks // 2):
        for i in range(len(pairs)):
            copy_in(i, m).start()
        if m == 0:
            for i in range(len(smalls)):
                copy_small(i).start()
    for lb in range(width // 128):
        for nb in range(4):
            entering[nb * 32 : (nb + 1) * 32, lb * 128 : (lb + 1) * 128] = in_ref[lb * 4 + nb]
    for i in range(len(smalls)):
        copy_small(i).wait()

    def two(m, carry):
        for i in range(len(pairs)):
            copy_in(i, m).wait()
        scales = []
        for n in range(2):
            toks = pl.ds(pl.multiple_of(m * size + n * CHUNK, CHUNK), CHUNK)
            squares = jnp.zeros((CHUNK, 128), F32)
            for lane in range(0, width, LANES):
                a_ref, f_ref = (a0_all, f0_all) if lane < half else (a1_all, f1_all)
                q = mm(cc_ref[toks, :], entering[:, lane : lane + LANES])
                for part in range(0, LANES, 128):
                    own = slice(lane % half + part, lane % half + part + 128)
                    g = a_ref[toks, own].astype(F32) + f_ref[toks, own].astype(F32) * q[:, part : part + 128]
                    gated[n, :, lane + part : lane + part + 128] = g
                    squares = squares + g * g
            mean = jnp.sum(squares, axis=1, keepdims=True) * (1.0 / width)
            scales.append(lax.rsqrt(mean + 1e-05))
        for n in range(2):
            k = 2 * m + n
            toks = pl.ds(pl.multiple_of(k * CHUNK, CHUNK), CHUNK)
            squares = jnp.zeros((CHUNK, 128), F32)
            for lane in range(0, width, 128):
                cols = slice(lane, lane + 128)
                v = (gated[n, :, cols] * scales[n] * gain_ref[:, cols]).astype(BF16)
                out_all[toks, cols] = v
                d = v.astype(F32) - roll_all[toks, cols].astype(F32)
                squares = squares + d * d
            sums[pl.ds(k, 1), :] = jnp.sum(squares.T, axis=0, keepdims=True)
        copy_out(m).start()
        return carry

    lax.fori_loop(0, chunks // 2, two, 0)
    both = jnp.concatenate([sums[...], roll0_ref[...] + roll1_ref[...]], axis=0)
    for i in range(sums_ref.shape[0]):
        sums_ref[i] = both
    for m in range(chunks // 2):
        copy_out(m).wait()


def shards(
    x_values, b_values, c_values, z_values, time_steps, decay_rate, skip_gain,
    conv_x, conv_bc, norm_gain, rollout, seq_spans,
):
    ring = lax.axis_size("seq")
    rows, width = x_values.shape
    heads = decay_rate.shape[0]
    chunks = rows // CHUNK
    blocks = width // LANES
    rank = lax.axis_index("seq").astype(jnp.int32).reshape(1)

    ends = width + 2 * STATE
    smem = pl.BlockSpec(memory_space=pltpu.SMEM)

    def whole(*shape):
        return pl.BlockSpec(shape, lambda i: (0,) * len(shape))

    def lane_block(r, first=0):
        return pl.BlockSpec((r, LANES), lambda i: (0, first + i))

    def grant(mib):
        return pltpu.CompilerParams(vmem_limit_bytes=mib * 1024 * 1024)

    def in_hbm(*arrays):
        return [pltpu.with_memory_space_constraint(v, pltpu.HBM) for v in arrays]

    x_values, b_values, c_values, z_values, rollout = in_hbm(x_values, b_values, c_values, z_values, rollout)
    (seq_spans,) = in_hbm(seq_spans)
    steps_row, rate_row, skip_row, gain_row, conv_x, conv_bc = in_hbm(
        time_steps.T, decay_rate.reshape(1, heads), skip_gain.reshape(1, heads), norm_gain.reshape(1, width), conv_x, conv_bc
    )
    last = rows // HALO - 1
    vmem = pl.BlockSpec(memory_space=pltpu.VMEM)
    hbm = pl.BlockSpec(memory_space=pl.ANY)
    edge, b_near, steps_near, rate_near, taps, keeps = pl.pallas_call(
        functools.partial(tail_kernel, chunks),
        grid=(1,),
        in_specs=[smem, smem]
        + [pl.BlockSpec((HALO, n), lambda i: (last, 0)) for n in (width, STATE, STATE)]
        + [whole(rows, STATE), whole(heads, rows), whole(1, heads), whole(CONV_K, width), whole(2, CONV_K, STATE)],
        out_specs=[
            whole(HALO, ends), whole(rows, STATE), whole(heads, rows), whole(1, heads), whole(8, width + STATE), whole(8, 128),
        ],
        out_shape=[
            jax.ShapeDtypeStruct((HALO, ends), BF16),
            pltpu.VMEM((rows, STATE), BF16),
            pltpu.VMEM((heads, rows), F32),
            pltpu.VMEM((1, heads), F32),
            pltpu.VMEM((8, width + STATE), F32),
            pltpu.VMEM((8, 128), F32),
        ],
        compiler_params=grant(8),
        name="tails",
    )(seq_spans, rank, x_values, b_values, c_values, b_values, steps_row, rate_row, conv_x, conv_bc)
    edge = lax.ppermute(edge, "seq", [(i, i + 1) for i in range(ring - 1)])
    conv_scratch = pltpu.VMEM((4, 8 + CHUNK, 128), F32)
    wide_scratch = pltpu.VMEM((rows, LANES), F32)

    end, head_scale, chain, head = pl.pallas_call(
        functools.partial(state_kernel, chunks),
        in_specs=[hbm] + [vmem] * 5,
        out_specs=[vmem] * 4,
        out_shape=[
            jax.ShapeDtypeStruct((STATE, width), F32),
            jax.ShapeDtypeStruct((HALO, width), F32),
            jax.ShapeDtypeStruct((8, width), F32),
            jax.ShapeDtypeStruct((HALO, width + STATE), BF16),
        ],
        scratch_shapes=[
            pltpu.VMEM((blocks, rows, LANES), BF16),
            conv_scratch,
            pltpu.VMEM((CHUNK, 128), F32),
            pltpu.VMEM((rows, 256), BF16),
            pltpu.VMEM((blocks, rows, LANES), F32),
            pltpu.VMEM((STATE, rows), BF16),
            pltpu.VMEM((blocks, rows, LANES), BF16),
            pltpu.SemaphoreType.DMA((blocks,)),
        ],
        compiler_params=grant(16),
        cost_estimate=pl.CostEstimate(flops=1 << 29, bytes_accessed=4 << 20, transcendentals=1 << 20),
        name="states",
    )(x_values, b_near, steps_near, rate_near, taps, keeps)

    msg = pl.pallas_call(
        edge_kernel,
        out_shape=jax.ShapeDtypeStruct((ring * MSG, 128), BF16),
        scratch_shapes=[pltpu.VMEM((ring * MSG, 128), F32)],
        compiler_params=grant(8),
        name="edge_states",
    )(edge, head, taps, keeps, head_scale, end, chain)
    edge = pltpu.with_memory_space_constraint(edge, pltpu.VMEM)

    msg = msg.reshape(ring, MSG // 2, 2, 128)
    spread = lax.all_to_all(msg, "seq", split_axis=0, concat_axis=0, tiled=True).reshape(ring * MSG, 128)

    def mix(first, specs, operands, more_specs, more_shapes):
        half = blocks // 2
        place = pltpu.HBM if first == 0 else pltpu.VMEM
        return pl.pallas_call(
            functools.partial(mix_kernel, chunks, first * LANES),
            grid=(half,),
            in_specs=[
                smem, smem, lane_block(rows, first), lane_block(HALO, first), whole(heads, rows), whole(1, heads),
                lane_block(rows, first), lane_block(rows, first), lane_block(CONV_K, first), whole(1, heads),
            ]
            + specs,
            out_specs=[lane_block(rows), lane_block(rows), whole(chunks, CHUNK)] + more_specs,
            out_shape=[
                place((rows, half * LANES), BF16),
                place((rows, half * LANES), BF16),
                pltpu.HBM((chunks, CHUNK), F32),
            ]
            + more_shapes,
            scratch_shapes=[
                conv_scratch, wide_scratch, wide_scratch, pltpu.VMEM((rows, 128), F32), pltpu.VMEM((STATE, LANES), F32),
                pltpu.VMEM((rows, 256), BF16), pltpu.VMEM((rows, 256), BF16), pltpu.VMEM((chunks, 16, 128), F32),
                pltpu.VMEM((chunks, 16, LANES), F32),
            ],
            compiler_params=grant(32),
            cost_estimate=pl.CostEstimate(flops=1 << 30, bytes_accessed=9 << 20, transcendentals=1 << 20),
            name="mix_first" if first == 0 else "mix_second",
        )(
            seq_spans, rank, x_values, edge, steps_row, rate_row, z_values, rollout, conv_x,
            skip_row, *operands,
        )

    shared_specs = [whole(rows, 256), whole(chunks, STATE, CHUNK)]
    a0, f0, roll0, left, bt, cc = mix(
        0,
        [
            whole(rows, STATE), whole(rows, STATE), pl.BlockSpec((HALO, 2 * STATE), lambda i: (0, width // (2 * STATE))),
            whole(2, CONV_K, STATE),
        ],
        [b_values, c_values, edge, conv_bc],
        shared_specs + [whole(rows, STATE)],
        [
            pltpu.HBM((rows, 256), BF16),
            pltpu.HBM((chunks, STATE, CHUNK), BF16),
            pltpu.VMEM((rows, STATE), BF16),
        ],
    )
    a0, f0, roll0, left, bt = in_hbm(a0, f0, roll0, left, bt)
    cc = pltpu.with_memory_space_constraint(cc, pltpu.VMEM)
    a1, f1, roll1 = mix(blocks // 2, shared_specs, [left, bt], [], [])
    a1, f1 = (pltpu.with_memory_space_constraint(v, pltpu.VMEM) for v in (a1, f1))
    (roll1,) = in_hbm(roll1)

    entering = pl.pallas_call(
        scan_kernel,
        in_specs=[pl.BlockSpec(memory_space=pltpu.VMEM), pl.BlockSpec(memory_space=pl.ANY)],
        out_shape=jax.ShapeDtypeStruct((ring, 32, 128), BF16),
        scratch_shapes=[pltpu.VMEM((ring * MSG, 128), F32)],
        compiler_params=grant(8),
        name="scan",
    )(spread, roll0)
    entering = lax.all_to_all(entering, "seq", split_axis=0, concat_axis=0, tiled=True)

    group = lax.axis_size("head")
    normed, sums = pl.pallas_call(
        norm_kernel,
        in_specs=[vmem] * 4 + [hbm] * 6,
        out_specs=[hbm, vmem],
        out_shape=[pltpu.HBM((rows, width), BF16), jax.ShapeDtypeStruct((group, 2 * chunks, CHUNK), F32)],
        scratch_shapes=[pltpu.VMEM((STATE, width), BF16), pltpu.VMEM((2, CHUNK, width), F32)]
        + [pltpu.VMEM((rows, width // 2), BF16)] * 2
        + [pltpu.VMEM((rows, width), BF16)] * 2
        + [pltpu.VMEM((1, width), F32)]
        + [pltpu.VMEM((chunks, CHUNK), F32)] * 3
        + [pltpu.SemaphoreType.DMA((3, chunks // 2))]
        + [pltpu.SemaphoreType.DMA((chunks // 2,)), pltpu.SemaphoreType.DMA((3,))],
        compiler_params=grant(24),
        cost_estimate=pl.CostEstimate(flops=1 << 28, bytes_accessed=8 << 20, transcendentals=1 << 10),
        name="norms",
    )(entering, a1, f1, cc, a0, f0, rollout, gain_row, roll0, roll1)

    sums = jnp.sum(lax.all_to_all(sums, "head", split_axis=0, concat_axis=0, tiled=True), axis=0)
    relative = jnp.sqrt(sums[:chunks] / (sums[chunks:] + 1e-06))
    return normed, relative.reshape(rows)


def solution(mesh):
    placed = (
        P("seq", "head"), P("seq", "head"), P("seq", "head"), P("seq", "head"), P("seq", "head"),
        P("head"), P("head"), P(None, "head"), P(None, None, "head"), P("head"), P("seq", "head"), P(),
    )
    return jax.shard_map(
        shards, mesh=mesh, in_specs=placed, out_specs=(P("seq", "head"), P("seq")), check_vma=False
    )
```

```python
import functools

import jax
import jax.numpy as jnp
from jax import lax
from jax.experimental import pallas as pl
from jax.experimental.pallas import tpu as pltpu
from jax.sharding import PartitionSpec as P

HEADS = 128
HEAD_DIM = 64
STATE = 128
GROUPS = 8
CONV_K = 4
SPAN = 256
CHUNK = 128
LANES = 256
HALO = 16
MSG = 34

F32 = jnp.float32
BF16 = jnp.bfloat16


def parts3(v):
    hi = v.astype(BF16)
    rest = v - hi.astype(F32)
    mid = rest.astype(BF16)
    low = (rest - mid.astype(F32)).astype(BF16)
    return hi, mid, low


def silu_half(h):
    return h + h * jnp.tanh(h)


def mm(a, b):
    return jnp.dot(a, b, preferred_element_type=F32)


def one_hot(lane0, width=LANES):
    r = lax.broadcasted_iota(jnp.int32, (256, width), 0)
    c = lax.broadcasted_iota(jnp.int32, (256, width), 1)
    return jnp.where((r & 127) == (c + lane0) // HEAD_DIM, 1.0, 0.0).astype(BF16)


def span_keep(seq_ref, span):
    start = seq_ref[0] * 0
    fresh = span == start
    for i in range(seq_ref.shape[0] - 1):
        start = start + seq_ref[i]
        fresh = fresh | (span == start)
    return jnp.where(fresh, 0.0, 1.0).astype(F32)


def conv_block(padded_ref, taps):
    rows = padded_ref.shape[0] - 8
    total = padded_ref[pl.ds(5, rows), :] * taps[0:1]
    for k in range(1, CONV_K):
        total = total + padded_ref[pl.ds(5 + k, rows), :] * taps[k : k + 1]
    return silu_half(total)


def conv_ordered(padded_ref, taps):
    per = CHUNK // 8
    shifted = {m: padded_ref[pl.ds(8 + m, 8, stride=per), :] for m in range(1 - CONV_K, per)}
    rows = []
    for j in range(per):
        total = shifted[j + 1 - CONV_K] * taps[0:1]
        for k in range(1, CONV_K):
            total = total + shifted[j + 1 - CONV_K + k] * taps[k : k + 1]
        rows.append(silu_half(total))
    return jnp.concatenate(rows, axis=0)


def turned(v, heads, chunk):
    turn = (128 - heads * chunk) % 128
    return pltpu.roll(v, turn, 1) if turn else v


def split2(v):
    hi = v.astype(BF16)
    return hi, (v - hi.astype(F32)).astype(BF16)


def stack_scales(source, heads, chunks, target):
    for k in range(chunks):
        hi, low = split2(turned(source, heads, k))
        target[k * CHUNK : (k + 1) * CHUNK, 0:128] = hi
        target[k * CHUNK : (k + 1) * CHUNK, 128:256] = low


def chunk_rates(ts_ref, rate_ref, chunks):
    steps = jnp.concatenate([ts_ref[:, k * CHUNK : (k + 1) * CHUNK] for k in range(chunks)], axis=0).T
    return steps, -steps * jnp.concatenate([rate_ref[...]] * chunks, axis=1)


def sum_rates(picks, rates):
    picks = picks.astype(BF16)
    r1, r2, r3 = parts3(rates)
    return mm(picks, r1) + (mm(picks, r2) + mm(picks, r3))


def spread_rows(v, e):
    n = v.shape[0]
    out = mm(jnp.concatenate(parts3(v), axis=0), e[0:128])
    return out[0:n] + (out[n : 2 * n] + out[2 * n : 3 * n])


def chunk_keeps(chunks, seq_ref, rank_ref):
    per_span = SPAN // CHUNK
    first = rank_ref[0] * (chunks // per_span)
    return [None if k % per_span else span_keep(seq_ref, first + k // per_span) for k in range(chunks)]


def fill_padded(padded_ref, src_ref, edge, k, lanes, keep):
    if k == 0:
        halo = edge
    else:
        halo = src_ref[k * CHUNK - HALO : k * CHUNK, lanes].astype(F32)[HALO - 8 :]
    padded_ref[0:8, :] = halo if keep is None else halo * keep
    padded_ref[8 : 8 + CHUNK, :] = src_ref[k * CHUNK : (k + 1) * CHUNK, lanes].astype(F32)


def tail_kernel(
    chunks, seq_ref, rank_ref, x_ref, b_ref, c_ref, b_all_ref, ts_ref, rate_ref, wx_ref, wbc_ref,
    tail_ref, b_out, ts_out, rate_out, taps_ref, keep_ref,
):
    width = x_ref.shape[1]
    tail_ref[:, 0:width] = x_ref[...]
    tail_ref[:, width : width + STATE] = b_ref[...]
    tail_ref[:, width + STATE : width + 2 * STATE] = c_ref[...]
    b_out[...] = b_all_ref[...]
    ts_out[...] = ts_ref[...]
    rate_out[...] = rate_ref[...]
    taps_ref[...] = jnp.zeros_like(taps_ref)
    taps_ref[0:CONV_K, 0:width] = wx_ref[...].astype(F32) * 0.5
    taps_ref[0:CONV_K, width : width + STATE] = wbc_ref[0].astype(F32) * 0.5
    keeps = [v for v in chunk_keeps(chunks, seq_ref, rank_ref) if v is not None]
    row = lax.broadcasted_iota(jnp.int32, (8, 128), 0)
    flags = jnp.ones((8, 128), F32)
    for i, keep in enumerate(keeps):
        flags = jnp.where(row == i, keep, flags)
    keep_ref[...] = flags


def state_kernel(
    chunks, x_hbm, b_ref, ts_ref, rate_ref, taps_ref, keep_ref,
    end_ref, head_scale_ref, chain_ref, head_ref,
    x_all, padded, order, lhsu, wide, bt, xs, x_sems,
):
    blocks = x_all.shape[0]
    width = blocks * LANES
    heads = ts_ref.shape[0]

    def x_copy(i):
        lanes = pl.ds(pl.multiple_of(i * LANES, LANES), LANES)
        return pltpu.make_async_copy(x_hbm.at[:, lanes], x_all.at[i], x_sems.at[i])

    def start(i, carry):
        x_copy(i).start()
        return carry

    lax.fori_loop(0, blocks, start, 0)
    steps, rates = chunk_rates(ts_ref, rate_ref, chunks)
    t = lax.broadcasted_iota(jnp.int32, (CHUNK + 16, CHUNK), 0)
    u = lax.broadcasted_iota(jnp.int32, (CHUNK + 16, CHUNK), 1)
    after = sum_rates(jnp.where((u > t) | (t >= CHUNK), 1.0, 0.0), rates)
    totals = after[CHUNK : CHUNK + 16]
    j = lax.broadcasted_iota(jnp.int32, (CHUNK, CHUNK), 0)
    k = lax.broadcasted_iota(jnp.int32, (CHUNK, CHUNK), 1)
    later = jnp.where((lax.rem(j, heads) == lax.rem(k, heads)) & (j > k), 1.0, 0.0).astype(BF16)
    t1, t2, t3 = parts3(totals)
    later = mm(t1, later) + (mm(t2, later) + mm(t3, later))
    lane = lax.broadcasted_iota(jnp.int32, (16, 128), 1)
    reached = jnp.ones((16, 128), F32)
    whole = jnp.exp(later + totals)
    for n in range(0, chunks, SPAN // CHUNK):
        keep = keep_ref[n * CHUNK // SPAN : n * CHUNK // SPAN + 1, :]
        reached = jnp.where(lane < n * heads, reached * keep, reached)
        whole = whole * keep
    scale = jnp.exp(after[0:CHUNK] + later[0:1]) * steps * reached[0:1]
    order[...] = scale
    per = CHUNK // 8
    stack_scales(jnp.concatenate([order[pl.ds(n, 8, stride=per), :] for n in range(per)], axis=0), heads, chunks, lhsu)
    e = one_hot(0, width)
    wide_all = mm(lhsu[...], e)
    for i in range(blocks):
        wide[i] = wide_all[:, i * LANES : (i + 1) * LANES]
    head_scale_ref[...] = mm(jnp.concatenate(split2(scale[0:HALO]), axis=1), e)
    row = lax.broadcasted_iota(jnp.int32, (16, 1), 0)
    hi, low = split2(whole)
    p = jnp.where(row == 0, hi.astype(F32), jnp.where(row == 1, low.astype(F32), 0.0))
    chain_ref[...] = mm(p.astype(BF16), e[0:128])[0:8]
    taps = taps_ref[0:CONV_K, width : width + STATE]
    none = jnp.zeros((8, 128), F32)

    per_span = SPAN // CHUNK
    keeps = [None if k % per_span else keep_ref[k // per_span : k // per_span + 1, :] for k in range(chunks)]
    for k in range(chunks):
        pad = padded.at[k % 4]
        fill_padded(pad, b_ref, none, k, slice(0, STATE), keeps[k])
        v = conv_ordered(pad, taps)
        if k == 0:
            v = jnp.where((lax.broadcasted_iota(jnp.int32, v.shape, 0) & 7) == 0, 0.0, v)
        bt[:, k * CHUNK : (k + 1) * CHUNK] = v.T.astype(BF16)
    head_ref[:, width : width + STATE] = b_ref[0:HALO, :]

    def block(i, carry):
        lane0 = pl.multiple_of(i * LANES, LANES)
        lanes = pl.ds(lane0, LANES)
        x_ref = x_all.at[i]
        weights = taps_ref[0:CONV_K, lanes]
        x_copy(i).wait()
        head_ref[:, lanes] = x_ref[0:HALO, :]

        for k in range(chunks):
            toks = slice(k * CHUNK, (k + 1) * CHUNK)
            for part in range(LANES // 128):
                cols = slice(part * 128, (part + 1) * 128)
                pad = padded.at[(2 * k + part) % 4]
                fill_padded(pad, x_ref, none, k, cols, keeps[k])
                v = conv_ordered(pad, weights[:, cols])
                xs[i, toks, cols] = (v * wide[i, toks, cols]).astype(BF16)
        return carry

    lax.fori_loop(0, blocks, block, 0)
    for i in range(blocks):
        end_ref[:, i * LANES : (i + 1) * LANES] = mm(bt[...], xs[i])


def edge_kernel(edge_ref, head_ref, taps_ref, keep_ref, scale_ref, end_ref, chain_ref, msg_ref, flat):
    width = end_ref.shape[1]
    b_cols = slice(width, width + STATE)

    def conv(cols):
        taps = taps_ref[:, cols]
        before = edge_ref[:, cols].astype(F32)[HALO - 8 :] * keep_ref[0:1, 0:1]
        joined = jnp.concatenate([before, head_ref[:, cols].astype(F32)], axis=0)
        total = joined[5 : 5 + HALO] * taps[0:1]
        for k in range(1, CONV_K):
            total = total + joined[5 + k : 5 + k + HALO] * taps[k : k + 1]
        return silu_half(total)

    bc = conv(b_cols)
    bt = jnp.concatenate([bc, jnp.zeros((STATE - HALO, STATE), F32)], axis=0).T[:, 0:HALO].astype(BF16)

    for i in range(width // LANES):
        cols = slice(i * LANES, (i + 1) * LANES)
        v = conv(cols)
        xs = (v * scale_ref[:, cols]).astype(BF16)
        state = end_ref[:, cols] + mm(bt, xs)
        decay = chain_ref[0 : MSG - 32, cols]
        for part in range(LANES // 128):
            block = slice(part * 128, (part + 1) * 128)
            for nb in range(4):
                first = MSG * ((i * (LANES // 128) + part) * 4 + nb)
                flat[first : first + 32, :] = state[nb * 32 : (nb + 1) * 32, block]
                flat[first + 32 : first + MSG, :] = decay[:, block]
    msg_ref[...] = flat[...].astype(BF16)


def scan_kernel(in_ref, after_ref, out_ref, flat):
    flat[...] = in_ref[...].astype(F32)
    carried = jnp.zeros((32, 128), F32)
    for i in range(out_ref.shape[0]):
        first = MSG * i
        out_ref[i] = carried.astype(BF16)
        decay = flat[first + 32 : first + 33, :] + flat[first + 33 : first + 34, :]
        carried = carried * decay + flat[first : first + 32, :]


def mix_first(chunks, seq_ref, rank_ref, b_ref, c_ref, edge_ref, wbc_ref, left, bt, cc_ref, padded):
    t = lax.broadcasted_iota(jnp.int32, (CHUNK, CHUNK), 0)
    u = lax.broadcasted_iota(jnp.int32, (CHUNK, CHUNK), 1)
    edges = edge_ref[...].astype(F32)[HALO - 8 :]

    keeps = chunk_keeps(chunks, seq_ref, rank_ref)
    for k in range(chunks):
        toks = slice(k * CHUNK, (k + 1) * CHUNK)
        pair = []
        for i, ref in enumerate((b_ref, c_ref)):
            pad = padded.at[(2 * k + i) % 4]
            fill_padded(pad, ref, edges[:, i * STATE : (i + 1) * STATE], k, slice(0, STATE), keeps[k])
            pair.append(conv_block(pad, wbc_ref[i].astype(F32) * 0.5))
        b, c = pair
        bt[k] = b.T.astype(BF16)
        c = c.astype(BF16)
        cc_ref[toks, :] = c
        left[toks, 128:256] = c
        g = lax.dot_general(c, b.astype(BF16), (((1,), (1,)), ((), ())), preferred_element_type=F32)
        left[toks, 0:128] = jnp.where(u <= t, g, 0.0).astype(BF16)


def mix_kernel(
    chunks, lane_first, seq_ref, rank_ref, x_ref, edge_ref, ts_ref, rate_ref, z_ref, roll_ref, wx_ref, skip_ref, *refs
):
    if lane_first == 0:
        b_ref, c_ref, bc_edge_ref, wbc_ref, a_ref, f_ref, roll_sum_ref, left, bt, cc_ref = refs[:10]
    else:
        left, bt, a_ref, f_ref, roll_sum_ref = refs[:5]
    padded, wide_u, wide_t, part, state, lhsu, lhst, ends_all, rows = refs[-9:]
    heads = skip_ref.shape[1]

    @pl.when(pl.program_id(0) == 0)
    def _():
        if lane_first == 0:
            mix_first(chunks, seq_ref, rank_ref, b_ref, c_ref, bc_edge_ref, wbc_ref, left, bt, cc_ref, padded)
        steps, rates = chunk_rates(ts_ref, rate_ref, chunks)
        t = lax.broadcasted_iota(jnp.int32, (CHUNK + 16, CHUNK), 0)
        u = lax.broadcasted_iota(jnp.int32, (CHUNK + 16, CHUNK), 1)
        half = jnp.where(u < CHUNK // 2, 1.0, 0.0)
        tri = jnp.where(u <= t, 1.0, 0.0) - half
        cum = sum_rates(jnp.where(t < CHUNK, tri, jnp.where(t == CHUNK, half, 1.0)), rates)
        rel = cum[:CHUNK]
        stack_scales(jnp.exp(-rel) * steps, heads, chunks, lhsu)
        stack_scales(jnp.exp(rel), heads, chunks, lhst)
        ends = jnp.exp(jnp.concatenate([rel[CHUNK - 8 :], cum[CHUNK : CHUNK + 8]], axis=0))
        for k in range(chunks):
            ends_all[k] = turned(ends, heads, k)
        part[...] = jnp.zeros_like(part)

    e = one_hot(lane_first + pl.program_id(0) * LANES)
    rows[...] = spread_rows(ends_all[...].reshape(16 * chunks, 128), e).reshape(chunks, 16, LANES)
    wide_u[...] = mm(lhsu[...], e)
    wide_t[...] = mm(lhst[...], e)
    s1, s2, s3 = parts3(skip_ref[...])
    skip = mm(jnp.concatenate([s1.astype(F32), s2.astype(F32), s3.astype(F32)], axis=0).astype(BF16), e[0:heads])
    skip = skip[0:1] + (skip[1:2] + skip[2:3])
    state[...] = jnp.zeros_like(state)
    edges = edge_ref[...].astype(F32)[HALO - 8 :]
    weights = wx_ref[...].astype(F32) * 0.5

    keeps = chunk_keeps(chunks, seq_ref, rank_ref)
    reach = jnp.ones((1, LANES), F32)
    for k in range(chunks):
        toks = slice(k * CHUNK, (k + 1) * CHUNK)
        to_end, to_mid, whole = rows[k, 7:8, :], rows[k, 8:9, :], rows[k, 9:10, :]
        xs, direct = [], []
        for lane in range(0, LANES, 128):
            cols = slice(lane, lane + 128)
            pad = padded.at[(2 * k + lane // 128) % 4]
            fill_padded(pad, x_ref, edges[:, cols], k, cols, keeps[k])
            v = conv_block(pad, weights[:, cols])
            xs.append((v * wide_u[toks, cols]).astype(BF16))
            direct.append(v.astype(BF16).astype(F32) * skip[:, cols])
        xs, direct = jnp.concatenate(xs, axis=1), jnp.concatenate(direct, axis=1)
        before = state[...]
        if keeps[k] is not None:
            before = before * keeps[k]
            reach = reach * keeps[k]
        state[...] = before * whole + mm(bt[k], xs) * to_end
        right = jnp.concatenate([xs, (before * to_mid).astype(BF16)], axis=0)
        inner = mm(left[toks, :], right)
        scale = wide_t[toks, :]
        gate = silu_half(z_ref[toks, :].astype(F32) * 0.5)
        a_ref[toks, :] = ((inner * scale + direct) * gate).astype(BF16)
        f_ref[toks, :] = (scale * gate * (reach * to_mid)).astype(BF16)
        r = roll_ref[toks, :].astype(F32)
        r = r * r
        part[toks, :] += r[:, 0:128] + r[:, 128:256]
        reach = reach * whole

    @pl.when(pl.program_id(0) == pl.num_programs(0) - 1)
    def _():
        for k in range(chunks):
            roll_sum_ref[k : k + 1, :] = jnp.sum(part[k * CHUNK : (k + 1) * CHUNK, :].T, axis=0, keepdims=True)


def norm_kernel(
    in_ref, a1_all, f1_all, cc_ref, a0_hbm, f0_hbm, roll_hbm, gain_hbm, roll0_hbm, roll1_hbm, out_hbm, sums_ref,
    gated, a0_all, f0_all, roll_all, out_all, gain_ref, roll0_ref, roll1_ref, parts,
    in_sems, out_sems, small_sems,
):
    width = out_all.shape[1]
    chunks, half = out_all.shape[0] // CHUNK, a0_all.shape[1]
    pairs = [(a0_hbm, a0_all), (f0_hbm, f0_all), (roll_hbm, roll_all)]
    smalls = [(gain_hbm, gain_ref), (roll0_hbm, roll0_ref), (roll1_hbm, roll1_ref)]
    size = 2 * CHUNK

    def copy_in(i, m):
        here = pl.ds(pl.multiple_of(m * size, size), size)
        return pltpu.make_async_copy(pairs[i][0].at[here], pairs[i][1].at[here], in_sems.at[i, m])

    def copy_out(m):
        here = pl.ds(pl.multiple_of(m * size, size), size)
        return pltpu.make_async_copy(out_all.at[here], out_hbm.at[here], out_sems.at[m])

    def copy_small(i):
        return pltpu.make_async_copy(*smalls[i], small_sems.at[i])

    for m in range(chunks // 2):
        for i in range(len(pairs)):
            copy_in(i, m).start()
        if m == 0:
            for i in range(len(smalls)):
                copy_small(i).start()
    for i in range(len(smalls)):
        copy_small(i).wait()

    def two(m, carry):
        for i in range(len(pairs)):
            copy_in(i, m).wait()
        scales = []
        for n in range(2):
            toks = pl.ds(pl.multiple_of(m * size + n * CHUNK, CHUNK), CHUNK)
            squares = jnp.zeros((CHUNK, 128), F32)
            for lane in range(0, width, LANES):
                a_ref, f_ref = (a0_all, f0_all) if lane < half else (a1_all, f1_all)
                own = [in_ref[lb * 4 : lb * 4 + 4].reshape(STATE, 128) for lb in range(lane // 128, (lane + LANES) // 128)]
                q = mm(cc_ref[toks, :], jnp.concatenate(own, axis=1))
                for part in range(0, LANES, 128):
                    own = slice(lane % half + part, lane % half + part + 128)
                    g = a_ref[toks, own].astype(F32) + f_ref[toks, own].astype(F32) * q[:, part : part + 128]
                    gated[n, :, lane + part : lane + part + 128] = g
                    squares = squares + g * g
            mean = jnp.sum(squares, axis=1, keepdims=True) * (1.0 / width)
            scales.append(lax.rsqrt(mean + 1e-05))
        for n in range(2):
            k = 2 * m + n
            toks = pl.ds(pl.multiple_of(k * CHUNK, CHUNK), CHUNK)
            squares = jnp.zeros((CHUNK, 128), F32)
            for lane in range(0, width, 128):
                cols = slice(lane, lane + 128)
                v = (gated[n, :, cols] * scales[n] * gain_ref[:, cols]).astype(BF16)
                out_all[toks, cols] = v
                d = v.astype(F32) - roll_all[toks, cols].astype(F32)
                squares = squares + d * d
            parts[k] = squares
        copy_out(m).start()
        return carry

    lax.fori_loop(0, chunks // 2, two, 0)
    sums = [jnp.sum(parts[k].T, axis=0, keepdims=True) for k in range(chunks)]
    both = jnp.concatenate(sums + [roll0_ref[...] + roll1_ref[...]], axis=0)
    for i in range(sums_ref.shape[0]):
        sums_ref[i] = both
    for m in range(chunks // 2):
        copy_out(m).wait()


def shards(
    x_values, b_values, c_values, z_values, time_steps, decay_rate, skip_gain,
    conv_x, conv_bc, norm_gain, rollout, seq_spans,
):
    ring = lax.axis_size("seq")
    rows, width = x_values.shape
    heads = decay_rate.shape[0]
    chunks = rows // CHUNK
    blocks = width // LANES
    rank = lax.axis_index("seq").astype(jnp.int32).reshape(1)

    ends = width + 2 * STATE
    smem = pl.BlockSpec(memory_space=pltpu.SMEM)

    def whole(*shape):
        return pl.BlockSpec(shape, lambda i: (0,) * len(shape))

    def lane_block(r, first=0):
        return pl.BlockSpec((r, LANES), lambda i: (0, first + i))

    def grant(mib):
        return pltpu.CompilerParams(vmem_limit_bytes=mib * 1024 * 1024)

    def in_hbm(*arrays):
        return [pltpu.with_memory_space_constraint(v, pltpu.HBM) for v in arrays]

    x_values, b_values, c_values, z_values, rollout = in_hbm(x_values, b_values, c_values, z_values, rollout)
    (seq_spans,) = in_hbm(seq_spans)
    steps_row, rate_row, skip_row, gain_row, conv_x, conv_bc = in_hbm(
        time_steps.T, decay_rate.reshape(1, heads), skip_gain.reshape(1, heads), norm_gain.reshape(1, width), conv_x, conv_bc
    )
    last = rows // HALO - 1
    vmem = pl.BlockSpec(memory_space=pltpu.VMEM)
    hbm = pl.BlockSpec(memory_space=pl.ANY)
    edge, b_near, steps_near, rate_near, taps, keeps = pl.pallas_call(
        functools.partial(tail_kernel, chunks),
        grid=(1,),
        in_specs=[smem, smem]
        + [pl.BlockSpec((HALO, n), lambda i: (last, 0)) for n in (width, STATE, STATE)]
        + [whole(rows, STATE), whole(heads, rows), whole(1, heads), whole(CONV_K, width), whole(2, CONV_K, STATE)],
        out_specs=[
            whole(HALO, ends), whole(rows, STATE), whole(heads, rows), whole(1, heads), whole(8, width + STATE), whole(8, 128),
        ],
        out_shape=[
            jax.ShapeDtypeStruct((HALO, ends), BF16),
            pltpu.VMEM((rows, STATE), BF16),
            pltpu.VMEM((heads, rows), F32),
            pltpu.VMEM((1, heads), F32),
            pltpu.VMEM((8, width + STATE), F32),
            pltpu.VMEM((8, 128), F32),
        ],
        compiler_params=grant(8),
        name="tails",
    )(seq_spans, rank, x_values, b_values, c_values, b_values, steps_row, rate_row, conv_x, conv_bc)
    edge = lax.ppermute(edge, "seq", [(i, i + 1) for i in range(ring - 1)])
    conv_scratch = pltpu.VMEM((4, 8 + CHUNK, 128), F32)
    wide_scratch = pltpu.VMEM((rows, LANES), F32)

    end, head_scale, chain, head = pl.pallas_call(
        functools.partial(state_kernel, chunks),
        in_specs=[hbm] + [vmem] * 5,
        out_specs=[vmem] * 4,
        out_shape=[
            jax.ShapeDtypeStruct((STATE, width), F32),
            jax.ShapeDtypeStruct((HALO, width), F32),
            jax.ShapeDtypeStruct((8, width), F32),
            jax.ShapeDtypeStruct((HALO, width + STATE), BF16),
        ],
        scratch_shapes=[
            pltpu.VMEM((blocks, rows, LANES), BF16),
            conv_scratch,
            pltpu.VMEM((CHUNK, 128), F32),
            pltpu.VMEM((rows, 256), BF16),
            pltpu.VMEM((blocks, rows, LANES), F32),
            pltpu.VMEM((STATE, rows), BF16),
            pltpu.VMEM((blocks, rows, LANES), BF16),
            pltpu.SemaphoreType.DMA((blocks,)),
        ],
        compiler_params=grant(16),
        cost_estimate=pl.CostEstimate(flops=1 << 29, bytes_accessed=4 << 20, transcendentals=1 << 20),
        name="states",
    )(x_values, b_near, steps_near, rate_near, taps, keeps)

    msg = pl.pallas_call(
        edge_kernel,
        out_shape=jax.ShapeDtypeStruct((ring * MSG, 128), BF16),
        scratch_shapes=[pltpu.VMEM((ring * MSG, 128), F32)],
        compiler_params=grant(8),
        name="edge_states",
    )(edge, head, taps, keeps, head_scale, end, chain)
    edge = pltpu.with_memory_space_constraint(edge, pltpu.VMEM)

    msg = msg.reshape(ring, MSG // 2, 2, 128)
    spread = lax.all_to_all(msg, "seq", split_axis=0, concat_axis=0, tiled=True).reshape(ring * MSG, 128)

    def mix(first, specs, operands, more_specs, more_shapes):
        half = blocks // 2
        place = pltpu.HBM if first == 0 else pltpu.VMEM
        return pl.pallas_call(
            functools.partial(mix_kernel, chunks, first * LANES),
            grid=(half,),
            in_specs=[
                smem, smem, lane_block(rows, first), lane_block(HALO, first), whole(heads, rows), whole(1, heads),
                lane_block(rows, first), lane_block(rows, first), lane_block(CONV_K, first), whole(1, heads),
            ]
            + specs,
            out_specs=[lane_block(rows), lane_block(rows), whole(chunks, CHUNK)] + more_specs,
            out_shape=[
                place((rows, half * LANES), BF16),
                place((rows, half * LANES), BF16),
                pltpu.HBM((chunks, CHUNK), F32),
            ]
            + more_shapes,
            scratch_shapes=[
                conv_scratch, wide_scratch, wide_scratch, pltpu.VMEM((rows, 128), F32), pltpu.VMEM((STATE, LANES), F32),
                pltpu.VMEM((rows, 256), BF16), pltpu.VMEM((rows, 256), BF16), pltpu.VMEM((chunks, 16, 128), F32),
                pltpu.VMEM((chunks, 16, LANES), F32),
            ],
            compiler_params=grant(32),
            cost_estimate=pl.CostEstimate(flops=1 << 30, bytes_accessed=9 << 20, transcendentals=1 << 20),
            name="mix_first" if first == 0 else "mix_second",
        )(
            seq_spans, rank, x_values, edge, steps_row, rate_row, z_values, rollout, conv_x,
            skip_row, *operands,
        )

    shared_specs = [whole(rows, 256), whole(chunks, STATE, CHUNK)]
    a0, f0, roll0, left, bt, cc = mix(
        0,
        [
            whole(rows, STATE), whole(rows, STATE), pl.BlockSpec((HALO, 2 * STATE), lambda i: (0, width // (2 * STATE))),
            whole(2, CONV_K, STATE),
        ],
        [b_values, c_values, edge, conv_bc],
        shared_specs + [whole(rows, STATE)],
        [
            pltpu.HBM((rows, 256), BF16),
            pltpu.HBM((chunks, STATE, CHUNK), BF16),
            pltpu.VMEM((rows, STATE), BF16),
        ],
    )
    a0, f0, roll0, left, bt = in_hbm(a0, f0, roll0, left, bt)
    cc = pltpu.with_memory_space_constraint(cc, pltpu.VMEM)
    a1, f1, roll1 = mix(blocks // 2, shared_specs, [left, bt], [], [])
    a1, f1 = (pltpu.with_memory_space_constraint(v, pltpu.VMEM) for v in (a1, f1))
    (roll1,) = in_hbm(roll1)

    entering = pl.pallas_call(
        scan_kernel,
        in_specs=[pl.BlockSpec(memory_space=pltpu.VMEM), pl.BlockSpec(memory_space=pl.ANY)],
        out_shape=jax.ShapeDtypeStruct((ring, 32, 128), BF16),
        scratch_shapes=[pltpu.VMEM((ring * MSG, 128), F32)],
        compiler_params=grant(8),
        name="scan",
    )(spread, roll0)
    entering = lax.all_to_all(entering, "seq", split_axis=0, concat_axis=0, tiled=True)

    group = lax.axis_size("head")
    normed, sums = pl.pallas_call(
        norm_kernel,
        in_specs=[vmem] * 4 + [hbm] * 6,
        out_specs=[hbm, vmem],
        out_shape=[pltpu.HBM((rows, width), BF16), jax.ShapeDtypeStruct((group, 2 * chunks, CHUNK), F32)],
        scratch_shapes=[pltpu.VMEM((2, CHUNK, width), F32)]
        + [pltpu.VMEM((rows, width // 2), BF16)] * 2
        + [pltpu.VMEM((rows, width), BF16)] * 2
        + [pltpu.VMEM((1, width), F32)]
        + [pltpu.VMEM((chunks, CHUNK), F32)] * 2
        + [pltpu.VMEM((chunks, CHUNK, 128), F32)]
        + [pltpu.SemaphoreType.DMA((3, chunks // 2))]
        + [pltpu.SemaphoreType.DMA((chunks // 2,)), pltpu.SemaphoreType.DMA((3,))],
        compiler_params=grant(24),
        cost_estimate=pl.CostEstimate(flops=1 << 28, bytes_accessed=8 << 20, transcendentals=1 << 10),
        name="norms",
    )(entering, a1, f1, cc, a0, f0, rollout, gain_row, roll0, roll1)

    sums = jnp.sum(lax.all_to_all(sums, "head", split_axis=0, concat_axis=0, tiled=True), axis=0)
    relative = jnp.sqrt(sums[:chunks] / (sums[chunks:] + 1e-06))
    return normed, relative.reshape(rows)


def solution(mesh):
    placed = (
        P("seq", "head"), P("seq", "head"), P("seq", "head"), P("seq", "head"), P("seq", "head"),
        P("head"), P("head"), P(None, "head"), P(None, None, "head"), P("head"), P("seq", "head"), P(),
    )
    return jax.shard_map(
        shards, mesh=mesh, in_specs=placed, out_specs=(P("seq", "head"), P("seq")), check_vma=False
    )
```

```python
import functools

import jax
import jax.numpy as jnp
from jax import lax
from jax.experimental import pallas as pl
from jax.experimental.pallas import tpu as pltpu
from jax.sharding import PartitionSpec as P

HEADS = 128
HEAD_DIM = 64
STATE = 128
GROUPS = 8
CONV_K = 4
SPAN = 256
CHUNK = 128
LANES = 256
HALO = 16
MSG = 34

F32 = jnp.float32
BF16 = jnp.bfloat16


def parts3(v):
    hi = v.astype(BF16)
    rest = v - hi.astype(F32)
    mid = rest.astype(BF16)
    low = (rest - mid.astype(F32)).astype(BF16)
    return hi, mid, low


def silu_half(h):
    return h + h * jnp.tanh(h)


def mm(a, b):
    return jnp.dot(a, b, preferred_element_type=F32)


def one_hot(lane0, width=LANES):
    r = lax.broadcasted_iota(jnp.int32, (256, width), 0)
    c = lax.broadcasted_iota(jnp.int32, (256, width), 1)
    return jnp.where((r & 127) == (c + lane0) // HEAD_DIM, 1.0, 0.0).astype(BF16)


def span_keep(seq_ref, span):
    start = seq_ref[0] * 0
    fresh = span == start
    for i in range(seq_ref.shape[0] - 1):
        start = start + seq_ref[i]
        fresh = fresh | (span == start)
    return jnp.where(fresh, 0.0, 1.0).astype(F32)


def conv_block(padded_ref, taps):
    rows = padded_ref.shape[0] - 8
    total = padded_ref[pl.ds(5, rows), :] * taps[0:1]
    for k in range(1, CONV_K):
        total = total + padded_ref[pl.ds(5 + k, rows), :] * taps[k : k + 1]
    return silu_half(total)


def conv_ordered(padded_ref, taps):
    per = CHUNK // 8
    shifted = {m: padded_ref[pl.ds(8 + m, 8, stride=per), :] for m in range(1 - CONV_K, per)}
    rows = []
    for j in range(per):
        total = shifted[j + 1 - CONV_K] * taps[0:1]
        for k in range(1, CONV_K):
            total = total + shifted[j + 1 - CONV_K + k] * taps[k : k + 1]
        rows.append(silu_half(total))
    return jnp.concatenate(rows, axis=0)


def turned(v, heads, chunk):
    turn = (128 - heads * chunk) % 128
    return pltpu.roll(v, turn, 1) if turn else v


def split2(v):
    hi = v.astype(BF16)
    return hi, (v - hi.astype(F32)).astype(BF16)


def stack_scales(source, heads, chunks, target):
    for k in range(chunks):
        hi, low = split2(turned(source, heads, k))
        target[k * CHUNK : (k + 1) * CHUNK, 0:128] = hi
        target[k * CHUNK : (k + 1) * CHUNK, 128:256] = low


def chunk_rates(ts_ref, rate_ref, chunks):
    steps = jnp.concatenate([ts_ref[:, k * CHUNK : (k + 1) * CHUNK] for k in range(chunks)], axis=0).T
    return steps, -steps * jnp.concatenate([rate_ref[...]] * chunks, axis=1)


def sum_rates(picks, rates):
    picks = picks.astype(BF16)
    r1, r2, r3 = parts3(rates)
    return mm(picks, r1) + (mm(picks, r2) + mm(picks, r3))


def spread_rows(v, e):
    n = v.shape[0]
    out = mm(jnp.concatenate(parts3(v), axis=0), e[0:128])
    return out[0:n] + (out[n : 2 * n] + out[2 * n : 3 * n])


def chunk_keeps(chunks, seq_ref, rank_ref):
    per_span = SPAN // CHUNK
    first = rank_ref[0] * (chunks // per_span)
    return [None if k % per_span else span_keep(seq_ref, first + k // per_span) for k in range(chunks)]


def fill_padded(padded_ref, src_ref, edge, k, lanes, keep):
    if k == 0:
        halo = edge
    else:
        halo = src_ref[k * CHUNK - HALO : k * CHUNK, lanes].astype(F32)[HALO - 8 :]
    padded_ref[0:8, :] = halo if keep is None else halo * keep
    padded_ref[8 : 8 + CHUNK, :] = src_ref[k * CHUNK : (k + 1) * CHUNK, lanes].astype(F32)


def tail_kernel(
    chunks, seq_ref, rank_ref, x_ref, b_ref, c_ref, b_all_ref, ts_ref, rate_ref, wx_ref, wbc_ref,
    tail_ref, b_out, ts_out, rate_out, taps_ref, keep_ref,
):
    width = x_ref.shape[1]
    tail_ref[:, 0:width] = x_ref[...]
    tail_ref[:, width : width + STATE] = b_ref[...]
    tail_ref[:, width + STATE : width + 2 * STATE] = c_ref[...]
    b_out[...] = b_all_ref[...]
    ts_out[...] = ts_ref[...]
    rate_out[...] = rate_ref[...]
    taps_ref[...] = jnp.zeros_like(taps_ref)
    taps_ref[0:CONV_K, 0:width] = wx_ref[...].astype(F32) * 0.5
    taps_ref[0:CONV_K, width : width + STATE] = wbc_ref[0].astype(F32) * 0.5
    keeps = [v for v in chunk_keeps(chunks, seq_ref, rank_ref) if v is not None]
    row = lax.broadcasted_iota(jnp.int32, (8, 128), 0)
    flags = jnp.ones((8, 128), F32)
    for i, keep in enumerate(keeps):
        flags = jnp.where(row == i, keep, flags)
    keep_ref[...] = flags


def state_kernel(
    chunks, x_hbm, b_ref, ts_ref, rate_ref, taps_ref, keep_ref,
    end_ref, head_scale_ref, chain_ref, head_ref,
    x_all, padded, order, lhsu, wide, bt, xs, x_sems,
):
    blocks = x_all.shape[0]
    width = blocks * LANES
    heads = ts_ref.shape[0]

    def x_copy(i):
        lanes = pl.ds(pl.multiple_of(i * LANES, LANES), LANES)
        return pltpu.make_async_copy(x_hbm.at[:, lanes], x_all.at[i], x_sems.at[i])

    def start(i, carry):
        x_copy(i).start()
        return carry

    lax.fori_loop(0, blocks, start, 0)
    steps, rates = chunk_rates(ts_ref, rate_ref, chunks)
    t = lax.broadcasted_iota(jnp.int32, (CHUNK + 16, CHUNK), 0)
    u = lax.broadcasted_iota(jnp.int32, (CHUNK + 16, CHUNK), 1)
    after = sum_rates(jnp.where((u > t) | (t >= CHUNK), 1.0, 0.0), rates)
    totals = after[CHUNK : CHUNK + 16]
    j = lax.broadcasted_iota(jnp.int32, (CHUNK, CHUNK), 0)
    k = lax.broadcasted_iota(jnp.int32, (CHUNK, CHUNK), 1)
    later = jnp.where((lax.rem(j, heads) == lax.rem(k, heads)) & (j > k), 1.0, 0.0).astype(BF16)
    t1, t2, t3 = parts3(totals)
    later = mm(t1, later) + (mm(t2, later) + mm(t3, later))
    lane = lax.broadcasted_iota(jnp.int32, (16, 128), 1)
    reached = jnp.ones((16, 128), F32)
    whole = jnp.exp(later + totals)
    for n in range(0, chunks, SPAN // CHUNK):
        keep = keep_ref[n * CHUNK // SPAN : n * CHUNK // SPAN + 1, :]
        reached = jnp.where(lane < n * heads, reached * keep, reached)
        whole = whole * keep
    scale = jnp.exp(after[0:CHUNK] + later[0:1]) * steps * reached[0:1]
    order[...] = scale
    per = CHUNK // 8
    stack_scales(jnp.concatenate([order[pl.ds(n, 8, stride=per), :] for n in range(per)], axis=0), heads, chunks, lhsu)
    e = one_hot(0, width)
    wide_all = mm(lhsu[...], e)
    for i in range(blocks):
        wide[i] = wide_all[:, i * LANES : (i + 1) * LANES]
    head_scale_ref[...] = mm(jnp.concatenate(split2(scale[0:HALO]), axis=1), e)
    row = lax.broadcasted_iota(jnp.int32, (16, 1), 0)
    hi, low = split2(whole)
    p = jnp.where(row == 0, hi.astype(F32), jnp.where(row == 1, low.astype(F32), 0.0))
    chain_ref[...] = mm(p.astype(BF16), e[0:128])[0:8]
    taps = taps_ref[0:CONV_K, width : width + STATE]
    none = jnp.zeros((8, 128), F32)

    per_span = SPAN // CHUNK
    keeps = [None if k % per_span else keep_ref[k // per_span : k // per_span + 1, :] for k in range(chunks)]
    for k in range(chunks):
        pad = padded.at[k % 4]
        fill_padded(pad, b_ref, none, k, slice(0, STATE), keeps[k])
        v = conv_ordered(pad, taps)
        if k == 0:
            v = jnp.where((lax.broadcasted_iota(jnp.int32, v.shape, 0) & 7) == 0, 0.0, v)
        bt[:, k * CHUNK : (k + 1) * CHUNK] = v.T.astype(BF16)
    head_ref[:, width : width + STATE] = b_ref[0:HALO, :]

    def block(i, carry):
        lane0 = pl.multiple_of(i * LANES, LANES)
        lanes = pl.ds(lane0, LANES)
        x_ref = x_all.at[i]
        weights = taps_ref[0:CONV_K, lanes]
        x_copy(i).wait()
        head_ref[:, lanes] = x_ref[0:HALO, :]

        for k in range(chunks):
            toks = slice(k * CHUNK, (k + 1) * CHUNK)
            for part in range(LANES // 128):
                cols = slice(part * 128, (part + 1) * 128)
                pad = padded.at[(2 * k + part) % 4]
                fill_padded(pad, x_ref, none, k, cols, keeps[k])
                v = conv_ordered(pad, weights[:, cols])
                xs[i, toks, cols] = (v * wide[i, toks, cols]).astype(BF16)
        return carry

    lax.fori_loop(0, blocks, block, 0)
    for i in range(blocks):
        end_ref[:, i * LANES : (i + 1) * LANES] = mm(bt[...], xs[i])


def edge_kernel(edge_ref, head_ref, taps_ref, keep_ref, scale_ref, end_ref, chain_ref, msg_ref, flat):
    width = end_ref.shape[1]
    b_cols = slice(width, width + STATE)

    def conv(cols):
        taps = taps_ref[:, cols]
        before = edge_ref[:, cols].astype(F32)[HALO - 8 :] * keep_ref[0:1, 0:1]
        joined = jnp.concatenate([before, head_ref[:, cols].astype(F32)], axis=0)
        total = joined[5 : 5 + HALO] * taps[0:1]
        for k in range(1, CONV_K):
            total = total + joined[5 + k : 5 + k + HALO] * taps[k : k + 1]
        return silu_half(total)

    bc = conv(b_cols)
    bt = jnp.concatenate([bc, jnp.zeros((STATE - HALO, STATE), F32)], axis=0).T[:, 0:HALO].astype(BF16)

    for i in range(width // LANES):
        cols = slice(i * LANES, (i + 1) * LANES)
        v = conv(cols)
        xs = (v * scale_ref[:, cols]).astype(BF16)
        state = end_ref[:, cols] + mm(bt, xs)
        decay = chain_ref[0 : MSG - 32, cols]
        for part in range(LANES // 128):
            block = slice(part * 128, (part + 1) * 128)
            for nb in range(4):
                first = MSG * ((i * (LANES // 128) + part) * 4 + nb)
                flat[first : first + 32, :] = state[nb * 32 : (nb + 1) * 32, block]
                flat[first + 32 : first + MSG, :] = decay[:, block]
    msg_ref[...] = flat[...].astype(BF16)


def scan_kernel(in_ref, after_ref, out_ref, flat):
    flat[...] = in_ref[...].astype(F32)
    carried = jnp.zeros((32, 128), F32)
    for i in range(out_ref.shape[0]):
        first = MSG * i
        out_ref[i] = carried.astype(BF16)
        decay = flat[first + 32 : first + 33, :] + flat[first + 33 : first + 34, :]
        carried = carried * decay + flat[first : first + 32, :]


def mix_first(chunks, seq_ref, rank_ref, b_ref, c_ref, edge_ref, wbc_ref, left, bt, cc_ref, padded):
    t = lax.broadcasted_iota(jnp.int32, (CHUNK, CHUNK), 0)
    u = lax.broadcasted_iota(jnp.int32, (CHUNK, CHUNK), 1)
    edges = edge_ref[...].astype(F32)[HALO - 8 :]

    keeps = chunk_keeps(chunks, seq_ref, rank_ref)
    for k in range(chunks):
        toks = slice(k * CHUNK, (k + 1) * CHUNK)
        pair = []
        for i, ref in enumerate((b_ref, c_ref)):
            pad = padded.at[(2 * k + i) % 4]
            fill_padded(pad, ref, edges[:, i * STATE : (i + 1) * STATE], k, slice(0, STATE), keeps[k])
            pair.append(conv_block(pad, wbc_ref[i].astype(F32) * 0.5))
        b, c = pair
        bt[k] = b.T.astype(BF16)
        c = c.astype(BF16)
        cc_ref[toks, :] = c
        left[toks, 128:256] = c
        g = lax.dot_general(c, b.astype(BF16), (((1,), (1,)), ((), ())), preferred_element_type=F32)
        left[toks, 0:128] = jnp.where(u <= t, g, 0.0).astype(BF16)


def mix_kernel(
    chunks, lane_first, seq_ref, rank_ref, x_ref, edge_ref, ts_ref, rate_ref, z_ref, roll_ref, wx_ref, skip_ref, *refs
):
    if lane_first == 0:
        b_ref, c_ref, bc_edge_ref, wbc_ref, a_ref, f_ref, roll_sum_ref, left, bt, cc_ref = refs[:10]
    else:
        left, bt, a_ref, f_ref, roll_sum_ref = refs[:5]
    padded, wide_u, wide_t, part, state, lhsu, lhst, ends_all, rows = refs[-9:]
    heads = skip_ref.shape[1]

    @pl.when(pl.program_id(0) == 0)
    def _():
        if lane_first == 0:
            mix_first(chunks, seq_ref, rank_ref, b_ref, c_ref, bc_edge_ref, wbc_ref, left, bt, cc_ref, padded)
        steps, rates = chunk_rates(ts_ref, rate_ref, chunks)
        t = lax.broadcasted_iota(jnp.int32, (CHUNK + 16, CHUNK), 0)
        u = lax.broadcasted_iota(jnp.int32, (CHUNK + 16, CHUNK), 1)
        half = jnp.where(u < CHUNK // 2, 1.0, 0.0)
        tri = jnp.where(u <= t, 1.0, 0.0) - half
        cum = sum_rates(jnp.where(t < CHUNK, tri, jnp.where(t == CHUNK, half, 1.0)), rates)
        rel = cum[:CHUNK]
        stack_scales(jnp.exp(-rel) * steps, heads, chunks, lhsu)
        stack_scales(jnp.exp(rel), heads, chunks, lhst)
        ends = jnp.exp(jnp.concatenate([rel[CHUNK - 8 :], cum[CHUNK : CHUNK + 8]], axis=0))
        for k in range(chunks):
            ends_all[k] = turned(ends, heads, k)
        part[...] = jnp.zeros_like(part)

    e = one_hot(lane_first + pl.program_id(0) * LANES)
    rows[...] = spread_rows(ends_all[...].reshape(16 * chunks, 128), e).reshape(chunks, 16, LANES)
    wide_u[...] = mm(lhsu[...], e)
    wide_t[...] = mm(lhst[...], e)
    s1, s2, s3 = parts3(skip_ref[...])
    skip = mm(jnp.concatenate([s1.astype(F32), s2.astype(F32), s3.astype(F32)], axis=0).astype(BF16), e[0:heads])
    skip = skip[0:1] + (skip[1:2] + skip[2:3])
    state[...] = jnp.zeros_like(state)
    edges = edge_ref[...].astype(F32)[HALO - 8 :]
    weights = wx_ref[...].astype(F32) * 0.5

    keeps = chunk_keeps(chunks, seq_ref, rank_ref)
    reach = jnp.ones((1, LANES), F32)
    for k in range(chunks):
        toks = slice(k * CHUNK, (k + 1) * CHUNK)
        to_end, to_mid, whole = rows[k, 7:8, :], rows[k, 8:9, :], rows[k, 9:10, :]
        xs, direct = [], []
        for lane in range(0, LANES, 128):
            cols = slice(lane, lane + 128)
            pad = padded.at[(2 * k + lane // 128) % 4]
            fill_padded(pad, x_ref, edges[:, cols], k, cols, keeps[k])
            v = conv_block(pad, weights[:, cols])
            xs.append((v * wide_u[toks, cols]).astype(BF16))
            direct.append(v.astype(BF16).astype(F32) * skip[:, cols])
        xs, direct = jnp.concatenate(xs, axis=1), jnp.concatenate(direct, axis=1)
        before = state[...]
        if keeps[k] is not None:
            before = before * keeps[k]
            reach = reach * keeps[k]
        state[...] = before * whole + mm(bt[k], xs) * to_end
        right = jnp.concatenate([xs, (before * to_mid).astype(BF16)], axis=0)
        inner = mm(left[toks, :], right)
        scale = wide_t[toks, :]
        gate = silu_half(z_ref[toks, :].astype(F32) * 0.5)
        a_ref[toks, :] = ((inner * scale + direct) * gate).astype(BF16)
        f_ref[toks, :] = (scale * gate * (reach * to_mid)).astype(BF16)
        r = roll_ref[toks, :].astype(F32)
        r = r * r
        part[toks, :] += r[:, 0:128] + r[:, 128:256]
        reach = reach * whole

    @pl.when(pl.program_id(0) == pl.num_programs(0) - 1)
    def _():
        for k in range(chunks):
            roll_sum_ref[k : k + 1, :] = jnp.sum(part[k * CHUNK : (k + 1) * CHUNK, :].T, axis=0, keepdims=True)


def norm_kernel(
    in_ref, a1_all, f1_all, cc_ref, a0_hbm, f0_hbm, roll_hbm, gain_hbm, roll0_hbm, roll1_hbm, out_hbm, sums_ref,
    gated, gated_near, a0_all, f0_all, roll_all, out_all, gain_ref, roll0_ref, roll1_ref, parts,
    in_sems, out_sems, small_sems,
):
    width = out_all.shape[1]
    chunks, half = out_all.shape[0] // CHUNK, a0_all.shape[1]
    pairs = [(a0_hbm, a0_all), (f0_hbm, f0_all), (roll_hbm, roll_all)]
    smalls = [(gain_hbm, gain_ref), (roll0_hbm, roll0_ref), (roll1_hbm, roll1_ref)]
    size = 2 * CHUNK

    def copy_in(i, m):
        here = pl.ds(pl.multiple_of(m * size, size), size)
        return pltpu.make_async_copy(pairs[i][0].at[here], pairs[i][1].at[here], in_sems.at[i, m])

    def copy_out(m):
        here = pl.ds(pl.multiple_of(m * size, size), size)
        return pltpu.make_async_copy(out_all.at[here], out_hbm.at[here], out_sems.at[m])

    def copy_small(i):
        return pltpu.make_async_copy(*smalls[i], small_sems.at[i])

    for m in range(chunks // 2):
        for i in range(len(pairs)):
            copy_in(i, m).start()
        if m == 0:
            for i in range(len(smalls)):
                copy_small(i).start()
    def gate(k, lanes, a_ref, f_ref, put, squares):
        toks = pl.ds(pl.multiple_of(k * CHUNK, CHUNK), CHUNK)
        first = lanes[0]
        for lane in lanes:
            own = [in_ref[lb * 4 : lb * 4 + 4].reshape(STATE, 128) for lb in range(lane // 128, (lane + LANES) // 128)]
            q = mm(cc_ref[toks, :], jnp.concatenate(own, axis=1))
            for part in range(0, LANES, 128):
                cols = slice(lane - first + part, lane - first + part + 128)
                g = a_ref[toks, cols].astype(F32) + f_ref[toks, cols].astype(F32) * q[:, part : part + 128]
                put(cols, g)
                squares = squares + g * g
        return squares

    def near(m, carry):
        for n in range(2):
            k = 2 * m + n
            toks = pl.ds(pl.multiple_of(k * CHUNK, CHUNK), CHUNK)

            def put(cols, g):
                gated_near[toks, cols] = g

            parts[k] = gate(k, range(half, width, LANES), a1_all, f1_all, put, jnp.zeros((CHUNK, 128), F32))
        return carry

    lax.fori_loop(0, chunks // 2, near, 0)
    for i in range(len(smalls)):
        copy_small(i).wait()

    def two(m, carry):
        for i in range(len(pairs)):
            copy_in(i, m).wait()
        scales = []
        for n in range(2):

            def put(cols, g):
                gated[n, :, cols] = g

            squares = gate(2 * m + n, range(0, half, LANES), a0_all, f0_all, put, parts[2 * m + n])
            mean = jnp.sum(squares, axis=1, keepdims=True) * (1.0 / width)
            scales.append(lax.rsqrt(mean + 1e-05))
        for n in range(2):
            k = 2 * m + n
            toks = pl.ds(pl.multiple_of(k * CHUNK, CHUNK), CHUNK)
            squares = jnp.zeros((CHUNK, 128), F32)
            for lane in range(0, width, 128):
                cols = slice(lane, lane + 128)
                g = gated[n, :, cols] if lane < half else gated_near[toks, lane - half : lane - half + 128]
                v = (g * scales[n] * gain_ref[:, cols]).astype(BF16)
                out_all[toks, cols] = v
                d = v.astype(F32) - roll_all[toks, cols].astype(F32)
                squares = squares + d * d
            parts[k] = squares
        copy_out(m).start()
        return carry

    lax.fori_loop(0, chunks // 2, two, 0)
    sums = [jnp.sum(parts[k].T, axis=0, keepdims=True) for k in range(chunks)]
    both = jnp.concatenate(sums + [roll0_ref[...] + roll1_ref[...]], axis=0)
    for i in range(sums_ref.shape[0]):
        sums_ref[i] = both
    for m in range(chunks // 2):
        copy_out(m).wait()


def shards(
    x_values, b_values, c_values, z_values, time_steps, decay_rate, skip_gain,
    conv_x, conv_bc, norm_gain, rollout, seq_spans,
):
    ring = lax.axis_size("seq")
    rows, width = x_values.shape
    heads = decay_rate.shape[0]
    chunks = rows // CHUNK
    blocks = width // LANES
    rank = lax.axis_index("seq").astype(jnp.int32).reshape(1)

    ends = width + 2 * STATE
    smem = pl.BlockSpec(memory_space=pltpu.SMEM)

    def whole(*shape):
        return pl.BlockSpec(shape, lambda i: (0,) * len(shape))

    def lane_block(r, first=0):
        return pl.BlockSpec((r, LANES), lambda i: (0, first + i))

    def grant(mib):
        return pltpu.CompilerParams(vmem_limit_bytes=mib * 1024 * 1024)

    def in_hbm(*arrays):
        return [pltpu.with_memory_space_constraint(v, pltpu.HBM) for v in arrays]

    x_values, b_values, c_values, z_values, rollout = in_hbm(x_values, b_values, c_values, z_values, rollout)
    (seq_spans,) = in_hbm(seq_spans)
    steps_row, rate_row, skip_row, gain_row, conv_x, conv_bc = in_hbm(
        time_steps.T, decay_rate.reshape(1, heads), skip_gain.reshape(1, heads), norm_gain.reshape(1, width), conv_x, conv_bc
    )
    last = rows // HALO - 1
    vmem = pl.BlockSpec(memory_space=pltpu.VMEM)
    hbm = pl.BlockSpec(memory_space=pl.ANY)
    edge, b_near, steps_near, rate_near, taps, keeps = pl.pallas_call(
        functools.partial(tail_kernel, chunks),
        grid=(1,),
        in_specs=[smem, smem]
        + [pl.BlockSpec((HALO, n), lambda i: (last, 0)) for n in (width, STATE, STATE)]
        + [whole(rows, STATE), whole(heads, rows), whole(1, heads), whole(CONV_K, width), whole(2, CONV_K, STATE)],
        out_specs=[
            whole(HALO, ends), whole(rows, STATE), whole(heads, rows), whole(1, heads), whole(8, width + STATE), whole(8, 128),
        ],
        out_shape=[
            jax.ShapeDtypeStruct((HALO, ends), BF16),
            pltpu.VMEM((rows, STATE), BF16),
            pltpu.VMEM((heads, rows), F32),
            pltpu.VMEM((1, heads), F32),
            pltpu.VMEM((8, width + STATE), F32),
            pltpu.VMEM((8, 128), F32),
        ],
        compiler_params=grant(8),
        name="tails",
    )(seq_spans, rank, x_values, b_values, c_values, b_values, steps_row, rate_row, conv_x, conv_bc)
    edge = lax.ppermute(edge, "seq", [(i, i + 1) for i in range(ring - 1)])
    conv_scratch = pltpu.VMEM((4, 8 + CHUNK, 128), F32)
    wide_scratch = pltpu.VMEM((rows, LANES), F32)

    end, head_scale, chain, head = pl.pallas_call(
        functools.partial(state_kernel, chunks),
        in_specs=[hbm] + [vmem] * 5,
        out_specs=[vmem] * 4,
        out_shape=[
            jax.ShapeDtypeStruct((STATE, width), F32),
            jax.ShapeDtypeStruct((HALO, width), F32),
            jax.ShapeDtypeStruct((8, width), F32),
            jax.ShapeDtypeStruct((HALO, width + STATE), BF16),
        ],
        scratch_shapes=[
            pltpu.VMEM((blocks, rows, LANES), BF16),
            conv_scratch,
            pltpu.VMEM((CHUNK, 128), F32),
            pltpu.VMEM((rows, 256), BF16),
            pltpu.VMEM((blocks, rows, LANES), F32),
            pltpu.VMEM((STATE, rows), BF16),
            pltpu.VMEM((blocks, rows, LANES), BF16),
            pltpu.SemaphoreType.DMA((blocks,)),
        ],
        compiler_params=grant(16),
        cost_estimate=pl.CostEstimate(flops=1 << 29, bytes_accessed=4 << 20, transcendentals=1 << 20),
        name="states",
    )(x_values, b_near, steps_near, rate_near, taps, keeps)

    msg = pl.pallas_call(
        edge_kernel,
        out_shape=jax.ShapeDtypeStruct((ring * MSG, 128), BF16),
        scratch_shapes=[pltpu.VMEM((ring * MSG, 128), F32)],
        compiler_params=grant(8),
        name="edge_states",
    )(edge, head, taps, keeps, head_scale, end, chain)
    edge = pltpu.with_memory_space_constraint(edge, pltpu.VMEM)

    msg = msg.reshape(ring, MSG // 2, 2, 128)
    spread = lax.all_to_all(msg, "seq", split_axis=0, concat_axis=0, tiled=True).reshape(ring * MSG, 128)

    def mix(first, specs, operands, more_specs, more_shapes):
        half = blocks // 2
        place = pltpu.HBM if first == 0 else pltpu.VMEM
        return pl.pallas_call(
            functools.partial(mix_kernel, chunks, first * LANES),
            grid=(half,),
            in_specs=[
                smem, smem, lane_block(rows, first), lane_block(HALO, first), whole(heads, rows), whole(1, heads),
                lane_block(rows, first), lane_block(rows, first), lane_block(CONV_K, first), whole(1, heads),
            ]
            + specs,
            out_specs=[lane_block(rows), lane_block(rows), whole(chunks, CHUNK)] + more_specs,
            out_shape=[
                place((rows, half * LANES), BF16),
                place((rows, half * LANES), BF16),
                pltpu.HBM((chunks, CHUNK), F32),
            ]
            + more_shapes,
            scratch_shapes=[
                conv_scratch, wide_scratch, wide_scratch, pltpu.VMEM((rows, 128), F32), pltpu.VMEM((STATE, LANES), F32),
                pltpu.VMEM((rows, 256), BF16), pltpu.VMEM((rows, 256), BF16), pltpu.VMEM((chunks, 16, 128), F32),
                pltpu.VMEM((chunks, 16, LANES), F32),
            ],
            compiler_params=grant(32),
            cost_estimate=pl.CostEstimate(flops=1 << 30, bytes_accessed=9 << 20, transcendentals=1 << 20),
            name="mix_first" if first == 0 else "mix_second",
        )(
            seq_spans, rank, x_values, edge, steps_row, rate_row, z_values, rollout, conv_x,
            skip_row, *operands,
        )

    shared_specs = [whole(rows, 256), whole(chunks, STATE, CHUNK)]
    a0, f0, roll0, left, bt, cc = mix(
        0,
        [
            whole(rows, STATE), whole(rows, STATE), pl.BlockSpec((HALO, 2 * STATE), lambda i: (0, width // (2 * STATE))),
            whole(2, CONV_K, STATE),
        ],
        [b_values, c_values, edge, conv_bc],
        shared_specs + [whole(rows, STATE)],
        [
            pltpu.HBM((rows, 256), BF16),
            pltpu.HBM((chunks, STATE, CHUNK), BF16),
            pltpu.VMEM((rows, STATE), BF16),
        ],
    )
    a0, f0, roll0, left, bt = in_hbm(a0, f0, roll0, left, bt)
    cc = pltpu.with_memory_space_constraint(cc, pltpu.VMEM)
    a1, f1, roll1 = mix(blocks // 2, shared_specs, [left, bt], [], [])
    a1, f1 = (pltpu.with_memory_space_constraint(v, pltpu.VMEM) for v in (a1, f1))
    (roll1,) = in_hbm(roll1)

    entering = pl.pallas_call(
        scan_kernel,
        in_specs=[pl.BlockSpec(memory_space=pltpu.VMEM), pl.BlockSpec(memory_space=pl.ANY)],
        out_shape=jax.ShapeDtypeStruct((ring, 32, 128), BF16),
        scratch_shapes=[pltpu.VMEM((ring * MSG, 128), F32)],
        compiler_params=grant(8),
        name="scan",
    )(spread, roll0)
    entering = lax.all_to_all(entering, "seq", split_axis=0, concat_axis=0, tiled=True)

    group = lax.axis_size("head")
    normed, sums = pl.pallas_call(
        norm_kernel,
        in_specs=[vmem] * 4 + [hbm] * 6,
        out_specs=[hbm, vmem],
        out_shape=[pltpu.HBM((rows, width), BF16), jax.ShapeDtypeStruct((group, 2 * chunks, CHUNK), F32)],
        scratch_shapes=[pltpu.VMEM((2, CHUNK, width // 2), F32), pltpu.VMEM((rows, width // 2), F32)]
        + [pltpu.VMEM((rows, width // 2), BF16)] * 2
        + [pltpu.VMEM((rows, width), BF16)] * 2
        + [pltpu.VMEM((1, width), F32)]
        + [pltpu.VMEM((chunks, CHUNK), F32)] * 2
        + [pltpu.VMEM((chunks, CHUNK, 128), F32)]
        + [pltpu.SemaphoreType.DMA((3, chunks // 2))]
        + [pltpu.SemaphoreType.DMA((chunks // 2,)), pltpu.SemaphoreType.DMA((3,))],
        compiler_params=grant(24),
        cost_estimate=pl.CostEstimate(flops=1 << 28, bytes_accessed=8 << 20, transcendentals=1 << 10),
        name="norms",
    )(entering, a1, f1, cc, a0, f0, rollout, gain_row, roll0, roll1)

    sums = jnp.sum(lax.all_to_all(sums, "head", split_axis=0, concat_axis=0, tiled=True), axis=0)
    relative = jnp.sqrt(sums[:chunks] / (sums[chunks:] + 1e-06))
    return normed, relative.reshape(rows)


def solution(mesh):
    placed = (
        P("seq", "head"), P("seq", "head"), P("seq", "head"), P("seq", "head"), P("seq", "head"),
        P("head"), P("head"), P(None, "head"), P(None, None, "head"), P("head"), P("seq", "head"), P(),
    )
    return jax.shard_map(
        shards, mesh=mesh, in_specs=placed, out_specs=(P("seq", "head"), P("seq")), check_vma=False
    )
```

```python
import functools

import jax
import jax.numpy as jnp
from jax import lax
from jax.experimental import pallas as pl
from jax.experimental.pallas import tpu as pltpu
from jax.sharding import PartitionSpec as P

HEADS = 128
HEAD_DIM = 64
STATE = 128
GROUPS = 8
CONV_K = 4
SPAN = 256
CHUNK = 128
LANES = 256
HALO = 16
MSG = 34

F32 = jnp.float32
BF16 = jnp.bfloat16


def parts3(v):
    hi = v.astype(BF16)
    rest = v - hi.astype(F32)
    mid = rest.astype(BF16)
    low = (rest - mid.astype(F32)).astype(BF16)
    return hi, mid, low


def silu_half(h):
    return h + h * jnp.tanh(h)


def mm(a, b):
    return jnp.dot(a, b, preferred_element_type=F32)


def one_hot(lane0, width=LANES):
    r = lax.broadcasted_iota(jnp.int32, (256, width), 0)
    c = lax.broadcasted_iota(jnp.int32, (256, width), 1)
    return jnp.where((r & 127) == (c + lane0) // HEAD_DIM, 1.0, 0.0).astype(BF16)


def span_keep(seq_ref, span):
    start = seq_ref[0] * 0
    fresh = span == start
    for i in range(seq_ref.shape[0] - 1):
        start = start + seq_ref[i]
        fresh = fresh | (span == start)
    return jnp.where(fresh, 0.0, 1.0).astype(F32)


def conv_block(padded_ref, taps):
    rows = padded_ref.shape[0] - 8
    total = padded_ref[pl.ds(5, rows), :] * taps[0:1]
    for k in range(1, CONV_K):
        total = total + padded_ref[pl.ds(5 + k, rows), :] * taps[k : k + 1]
    return silu_half(total)


def conv_ordered(padded_ref, taps):
    per = CHUNK // 8
    shifted = {m: padded_ref[pl.ds(8 + m, 8, stride=per), :] for m in range(1 - CONV_K, per)}
    rows = []
    for j in range(per):
        total = shifted[j + 1 - CONV_K] * taps[0:1]
        for k in range(1, CONV_K):
            total = total + shifted[j + 1 - CONV_K + k] * taps[k : k + 1]
        rows.append(silu_half(total))
    return jnp.concatenate(rows, axis=0)


def turned(v, heads, chunk):
    turn = (128 - heads * chunk) % 128
    return pltpu.roll(v, turn, 1) if turn else v


def split2(v):
    hi = v.astype(BF16)
    return hi, (v - hi.astype(F32)).astype(BF16)


def stack_scales(source, heads, chunks, target):
    for k in range(chunks):
        hi, low = split2(turned(source, heads, k))
        target[k * CHUNK : (k + 1) * CHUNK, 0:128] = hi
        target[k * CHUNK : (k + 1) * CHUNK, 128:256] = low


def chunk_rates(ts_ref, rate_ref, chunks):
    steps = jnp.concatenate([ts_ref[:, k * CHUNK : (k + 1) * CHUNK] for k in range(chunks)], axis=0).T
    return steps, -steps * jnp.concatenate([rate_ref[...]] * chunks, axis=1)


def sum_rates(picks, rates):
    picks = picks.astype(BF16)
    r1, r2, r3 = parts3(rates)
    return mm(picks, r1) + (mm(picks, r2) + mm(picks, r3))


def spread_rows(v, e):
    n = v.shape[0]
    out = mm(jnp.concatenate(parts3(v), axis=0), e[0:128])
    return out[0:n] + (out[n : 2 * n] + out[2 * n : 3 * n])


def chunk_keeps(chunks, seq_ref, rank_ref):
    per_span = SPAN // CHUNK
    first = rank_ref[0] * (chunks // per_span)
    return [None if k % per_span else span_keep(seq_ref, first + k // per_span) for k in range(chunks)]


def fill_padded(padded_ref, src_ref, edge, k, lanes, keep):
    if k == 0:
        halo = edge
    else:
        halo = src_ref[k * CHUNK - HALO : k * CHUNK, lanes].astype(F32)[HALO - 8 :]
    padded_ref[0:8, :] = halo if keep is None else halo * keep
    padded_ref[8 : 8 + CHUNK, :] = src_ref[k * CHUNK : (k + 1) * CHUNK, lanes].astype(F32)


def tail_kernel(
    chunks, seq_ref, rank_ref, x_ref, b_ref, c_ref, b_all_ref, ts_ref, rate_ref, wx_ref, wbc_ref,
    tail_ref, b_out, ts_out, rate_out, taps_ref, keep_ref,
):
    width = x_ref.shape[1]
    tail_ref[:, 0:width] = x_ref[...]
    tail_ref[:, width : width + STATE] = b_ref[...]
    tail_ref[:, width + STATE : width + 2 * STATE] = c_ref[...]
    b_out[...] = b_all_ref[...]
    ts_out[...] = ts_ref[...]
    rate_out[...] = rate_ref[...]
    taps_ref[...] = jnp.zeros_like(taps_ref)
    taps_ref[0:CONV_K, 0:width] = wx_ref[...].astype(F32) * 0.5
    taps_ref[0:CONV_K, width : width + STATE] = wbc_ref[0].astype(F32) * 0.5
    keeps = [v for v in chunk_keeps(chunks, seq_ref, rank_ref) if v is not None]
    row = lax.broadcasted_iota(jnp.int32, (8, 128), 0)
    flags = jnp.ones((8, 128), F32)
    for i, keep in enumerate(keeps):
        flags = jnp.where(row == i, keep, flags)
    keep_ref[...] = flags


def state_kernel(
    chunks, x_hbm, b_ref, ts_ref, rate_ref, taps_ref, keep_ref,
    end_ref, head_scale_ref, chain_ref, head_ref,
    x_all, padded, order, lhsu, wide, bt, xs, x_sems,
):
    blocks = x_all.shape[0]
    width = blocks * LANES
    heads = ts_ref.shape[0]

    def x_copy(i):
        lanes = pl.ds(pl.multiple_of(i * LANES, LANES), LANES)
        return pltpu.make_async_copy(x_hbm.at[:, lanes], x_all.at[i], x_sems.at[i])

    def start(i, carry):
        x_copy(i).start()
        return carry

    lax.fori_loop(0, blocks, start, 0)
    steps, rates = chunk_rates(ts_ref, rate_ref, chunks)
    t = lax.broadcasted_iota(jnp.int32, (CHUNK + 16, CHUNK), 0)
    u = lax.broadcasted_iota(jnp.int32, (CHUNK + 16, CHUNK), 1)
    after = sum_rates(jnp.where((u > t) | (t >= CHUNK), 1.0, 0.0), rates)
    totals = after[CHUNK : CHUNK + 16]
    j = lax.broadcasted_iota(jnp.int32, (CHUNK, CHUNK), 0)
    k = lax.broadcasted_iota(jnp.int32, (CHUNK, CHUNK), 1)
    later = jnp.where((lax.rem(j, heads) == lax.rem(k, heads)) & (j > k), 1.0, 0.0).astype(BF16)
    t1, t2, t3 = parts3(totals)
    later = mm(t1, later) + (mm(t2, later) + mm(t3, later))
    lane = lax.broadcasted_iota(jnp.int32, (16, 128), 1)
    reached = jnp.ones((16, 128), F32)
    whole = jnp.exp(later + totals)
    for n in range(0, chunks, SPAN // CHUNK):
        keep = keep_ref[n * CHUNK // SPAN : n * CHUNK // SPAN + 1, :]
        reached = jnp.where(lane < n * heads, reached * keep, reached)
        whole = whole * keep
    scale = jnp.exp(after[0:CHUNK] + later[0:1]) * steps * reached[0:1]
    order[...] = scale
    per = CHUNK // 8
    stack_scales(jnp.concatenate([order[pl.ds(n, 8, stride=per), :] for n in range(per)], axis=0), heads, chunks, lhsu)
    e = one_hot(0, width)
    wide_all = mm(lhsu[...], e)
    for i in range(blocks):
        wide[i] = wide_all[:, i * LANES : (i + 1) * LANES]
    head_scale_ref[...] = mm(jnp.concatenate(split2(scale[0:HALO]), axis=1), e)
    row = lax.broadcasted_iota(jnp.int32, (16, 1), 0)
    hi, low = split2(whole)
    p = jnp.where(row == 0, hi.astype(F32), jnp.where(row == 1, low.astype(F32), 0.0))
    chain_ref[...] = mm(p.astype(BF16), e[0:128])[0:8]
    taps = taps_ref[0:CONV_K, width : width + STATE]
    none = jnp.zeros((8, 128), F32)

    per_span = SPAN // CHUNK
    keeps = [None if k % per_span else keep_ref[k // per_span : k // per_span + 1, :] for k in range(chunks)]
    for k in range(chunks):
        pad = padded.at[k % 8]
        fill_padded(pad, b_ref, none, k, slice(0, STATE), keeps[k])
        v = conv_ordered(pad, taps)
        if k == 0:
            v = jnp.where((lax.broadcasted_iota(jnp.int32, v.shape, 0) & 7) == 0, 0.0, v)
        bt[:, k * CHUNK : (k + 1) * CHUNK] = v.T.astype(BF16)
    head_ref[:, width : width + STATE] = b_ref[0:HALO, :]

    def block(i, carry):
        lane0 = pl.multiple_of(i * LANES, LANES)
        lanes = pl.ds(lane0, LANES)
        x_ref = x_all.at[i]
        weights = taps_ref[0:CONV_K, lanes]
        x_copy(i).wait()
        head_ref[:, lanes] = x_ref[0:HALO, :]

        for k in range(chunks):
            toks = slice(k * CHUNK, (k + 1) * CHUNK)
            for part in range(LANES // 128):
                cols = slice(part * 128, (part + 1) * 128)
                pad = padded.at[(2 * k + part) % 8]
                fill_padded(pad, x_ref, none, k, cols, keeps[k])
                v = conv_ordered(pad, weights[:, cols])
                xs[i, toks, cols] = (v * wide[i, toks, cols]).astype(BF16)
        return carry

    lax.fori_loop(0, blocks, block, 0)
    for i in range(blocks):
        end_ref[:, i * LANES : (i + 1) * LANES] = mm(bt[...], xs[i])


def edge_kernel(edge_ref, head_ref, taps_ref, keep_ref, scale_ref, end_ref, chain_ref, msg_ref, flat):
    width = end_ref.shape[1]
    b_cols = slice(width, width + STATE)

    def conv(cols):
        taps = taps_ref[:, cols]
        before = edge_ref[:, cols].astype(F32)[HALO - 8 :] * keep_ref[0:1, 0:1]
        joined = jnp.concatenate([before, head_ref[:, cols].astype(F32)], axis=0)
        total = joined[5 : 5 + HALO] * taps[0:1]
        for k in range(1, CONV_K):
            total = total + joined[5 + k : 5 + k + HALO] * taps[k : k + 1]
        return silu_half(total)

    bc = conv(b_cols)
    bt = jnp.concatenate([bc, jnp.zeros((STATE - HALO, STATE), F32)], axis=0).T[:, 0:HALO].astype(BF16)

    for i in range(width // LANES):
        cols = slice(i * LANES, (i + 1) * LANES)
        v = conv(cols)
        xs = (v * scale_ref[:, cols]).astype(BF16)
        state = end_ref[:, cols] + mm(bt, xs)
        decay = chain_ref[0 : MSG - 32, cols]
        for part in range(LANES // 128):
            block = slice(part * 128, (part + 1) * 128)
            for nb in range(4):
                first = MSG * ((i * (LANES // 128) + part) * 4 + nb)
                flat[first : first + 32, :] = state[nb * 32 : (nb + 1) * 32, block]
                flat[first + 32 : first + MSG, :] = decay[:, block]
    msg_ref[...] = flat[...].astype(BF16)


def scan_kernel(in_ref, after_ref, out_ref, flat):
    flat[...] = in_ref[...].astype(F32)
    carried = jnp.zeros((32, 128), F32)
    for i in range(out_ref.shape[0]):
        first = MSG * i
        out_ref[i] = carried.astype(BF16)
        decay = flat[first + 32 : first + 33, :] + flat[first + 33 : first + 34, :]
        carried = carried * decay + flat[first : first + 32, :]


def mix_first(chunks, seq_ref, rank_ref, b_ref, c_ref, edge_ref, wbc_ref, left, bt, cc_ref, padded):
    t = lax.broadcasted_iota(jnp.int32, (CHUNK, CHUNK), 0)
    u = lax.broadcasted_iota(jnp.int32, (CHUNK, CHUNK), 1)
    edges = edge_ref[...].astype(F32)[HALO - 8 :]

    keeps = chunk_keeps(chunks, seq_ref, rank_ref)
    for k in range(chunks):
        toks = slice(k * CHUNK, (k + 1) * CHUNK)
        pair = []
        for i, ref in enumerate((b_ref, c_ref)):
            pad = padded.at[(2 * k + i) % 8]
            fill_padded(pad, ref, edges[:, i * STATE : (i + 1) * STATE], k, slice(0, STATE), keeps[k])
            pair.append(conv_block(pad, wbc_ref[i].astype(F32) * 0.5))
        b, c = pair
        bt[k] = b.T.astype(BF16)
        c = c.astype(BF16)
        cc_ref[toks, :] = c
        left[toks, 128:256] = c
        g = lax.dot_general(c, b.astype(BF16), (((1,), (1,)), ((), ())), preferred_element_type=F32)
        left[toks, 0:128] = jnp.where(u <= t, g, 0.0).astype(BF16)


def mix_kernel(
    chunks, lane_first, seq_ref, rank_ref, x_ref, edge_ref, ts_ref, rate_ref, z_ref, roll_ref, wx_ref, skip_ref, *refs
):
    if lane_first == 0:
        b_ref, c_ref, bc_edge_ref, wbc_ref, a_ref, f_ref, roll_sum_ref, left, bt, cc_ref = refs[:10]
    else:
        left, bt, a_ref, f_ref, roll_sum_ref = refs[:5]
    padded, wide_u, wide_t, part, state, lhsu, lhst, ends_all, rows = refs[-9:]
    heads = skip_ref.shape[1]

    @pl.when(pl.program_id(0) == 0)
    def _():
        if lane_first == 0:
            mix_first(chunks, seq_ref, rank_ref, b_ref, c_ref, bc_edge_ref, wbc_ref, left, bt, cc_ref, padded)
        steps, rates = chunk_rates(ts_ref, rate_ref, chunks)
        t = lax.broadcasted_iota(jnp.int32, (CHUNK + 16, CHUNK), 0)
        u = lax.broadcasted_iota(jnp.int32, (CHUNK + 16, CHUNK), 1)
        half = jnp.where(u < CHUNK // 2, 1.0, 0.0)
        tri = jnp.where(u <= t, 1.0, 0.0) - half
        cum = sum_rates(jnp.where(t < CHUNK, tri, jnp.where(t == CHUNK, half, 1.0)), rates)
        rel = cum[:CHUNK]
        stack_scales(jnp.exp(-rel) * steps, heads, chunks, lhsu)
        stack_scales(jnp.exp(rel), heads, chunks, lhst)
        ends = jnp.exp(jnp.concatenate([rel[CHUNK - 8 :], cum[CHUNK : CHUNK + 8]], axis=0))
        for k in range(chunks):
            ends_all[k] = turned(ends, heads, k)
        part[...] = jnp.zeros_like(part)

    e = one_hot(lane_first + pl.program_id(0) * LANES)
    rows[...] = spread_rows(ends_all[...].reshape(16 * chunks, 128), e).reshape(chunks, 16, LANES)
    wide_u[...] = mm(lhsu[...], e)
    wide_t[...] = mm(lhst[...], e)
    s1, s2, s3 = parts3(skip_ref[...])
    skip = mm(jnp.concatenate([s1.astype(F32), s2.astype(F32), s3.astype(F32)], axis=0).astype(BF16), e[0:heads])
    skip = skip[0:1] + (skip[1:2] + skip[2:3])
    state[...] = jnp.zeros_like(state)
    edges = edge_ref[...].astype(F32)[HALO - 8 :]
    weights = wx_ref[...].astype(F32) * 0.5

    keeps = chunk_keeps(chunks, seq_ref, rank_ref)
    reach = jnp.ones((1, LANES), F32)
    for k in range(chunks):
        toks = slice(k * CHUNK, (k + 1) * CHUNK)
        to_end, to_mid, whole = rows[k, 7:8, :], rows[k, 8:9, :], rows[k, 9:10, :]
        xs, direct = [], []
        for lane in range(0, LANES, 128):
            cols = slice(lane, lane + 128)
            pad = padded.at[(2 * k + lane // 128) % 8]
            fill_padded(pad, x_ref, edges[:, cols], k, cols, keeps[k])
            v = conv_block(pad, weights[:, cols])
            xs.append((v * wide_u[toks, cols]).astype(BF16))
            direct.append(v.astype(BF16).astype(F32) * skip[:, cols])
        xs, direct = jnp.concatenate(xs, axis=1), jnp.concatenate(direct, axis=1)
        before = state[...]
        if keeps[k] is not None:
            before = before * keeps[k]
            reach = reach * keeps[k]
        state[...] = before * whole + mm(bt[k], xs) * to_end
        right = jnp.concatenate([xs, (before * to_mid).astype(BF16)], axis=0)
        inner = mm(left[toks, :], right)
        scale = wide_t[toks, :]
        gate = silu_half(z_ref[toks, :].astype(F32) * 0.5)
        a_ref[toks, :] = ((inner * scale + direct) * gate).astype(BF16)
        f_ref[toks, :] = (scale * gate * (reach * to_mid)).astype(BF16)
        r = roll_ref[toks, :].astype(F32)
        r = r * r
        part[toks, :] += r[:, 0:128] + r[:, 128:256]
        reach = reach * whole

    @pl.when(pl.program_id(0) == pl.num_programs(0) - 1)
    def _():
        for k in range(chunks):
            roll_sum_ref[k : k + 1, :] = jnp.sum(part[k * CHUNK : (k + 1) * CHUNK, :].T, axis=0, keepdims=True)


def norm_kernel(
    in_ref, a1_all, f1_all, cc_ref, a0_hbm, f0_hbm, roll_hbm, gain_hbm, roll0_hbm, roll1_hbm, out_hbm, sums_ref,
    gated, gated_near, a0_all, f0_all, roll_all, out_all, gain_ref, roll0_ref, roll1_ref, parts,
    in_sems, out_sems, small_sems,
):
    width = out_all.shape[1]
    chunks, half = out_all.shape[0] // CHUNK, a0_all.shape[1]
    pairs = [(a0_hbm, a0_all), (f0_hbm, f0_all), (roll_hbm, roll_all)]
    smalls = [(gain_hbm, gain_ref), (roll0_hbm, roll0_ref), (roll1_hbm, roll1_ref)]
    size = 2 * CHUNK

    rows = out_all.shape[0] // 2

    def copy_in(i, m):
        here = pl.ds(pl.multiple_of(m * rows, rows), rows)
        return pltpu.make_async_copy(pairs[i][0].at[here], pairs[i][1].at[here], in_sems.at[i, m])

    def copy_out(m):
        here = pl.ds(pl.multiple_of(m * size, size), size)
        return pltpu.make_async_copy(out_all.at[here], out_hbm.at[here], out_sems.at[m])

    def copy_small(i):
        return pltpu.make_async_copy(*smalls[i], small_sems.at[i])

    for m in range(2):
        for i in range(len(pairs)):
            copy_in(i, m).start()
        if m == 0:
            for i in range(len(smalls)):
                copy_small(i).start()
    def gate(k, lanes, a_ref, f_ref, put, squares):
        toks = pl.ds(pl.multiple_of(k * CHUNK, CHUNK), CHUNK)
        first = lanes[0]
        for lane in lanes:
            own = [in_ref[lb * 4 : lb * 4 + 4].reshape(STATE, 128) for lb in range(lane // 128, (lane + LANES) // 128)]
            q = mm(cc_ref[toks, :], jnp.concatenate(own, axis=1))
            for part in range(0, LANES, 128):
                cols = slice(lane - first + part, lane - first + part + 128)
                g = a_ref[toks, cols].astype(F32) + f_ref[toks, cols].astype(F32) * q[:, part : part + 128]
                put(cols, g)
                squares = squares + g * g
        return squares

    def near(m, carry):
        for n in range(2):
            k = 2 * m + n
            toks = pl.ds(pl.multiple_of(k * CHUNK, CHUNK), CHUNK)

            def put(cols, g):
                gated_near[toks, cols] = g

            parts[k] = gate(k, range(half, width, LANES), a1_all, f1_all, put, jnp.zeros((CHUNK, 128), F32))
        return carry

    lax.fori_loop(0, chunks // 2, near, 0)
    for i in range(len(smalls)):
        copy_small(i).wait()

    def two(m, carry):
        scales = []
        for n in range(2):

            def put(cols, g):
                gated[n, :, cols] = g

            squares = gate(2 * m + n, range(0, half, LANES), a0_all, f0_all, put, parts[2 * m + n])
            mean = jnp.sum(squares, axis=1, keepdims=True) * (1.0 / width)
            scales.append(lax.rsqrt(mean + 1e-05))
        for n in range(2):
            k = 2 * m + n
            toks = pl.ds(pl.multiple_of(k * CHUNK, CHUNK), CHUNK)
            squares = jnp.zeros((CHUNK, 128), F32)
            for lane in range(0, width, 128):
                cols = slice(lane, lane + 128)
                g = gated[n, :, cols] if lane < half else gated_near[toks, lane - half : lane - half + 128]
                v = (g * scales[n] * gain_ref[:, cols]).astype(BF16)
                out_all[toks, cols] = v
                d = v.astype(F32) - roll_all[toks, cols].astype(F32)
                squares = squares + d * d
            parts[k] = squares
        copy_out(m).start()
        return carry

    def block(h, carry):
        for i in range(len(pairs)):
            copy_in(i, h).wait()
        return lax.fori_loop(h * (chunks // 4), (h + 1) * (chunks // 4), two, carry)

    lax.fori_loop(0, 2, block, 0)
    sums = [jnp.sum(parts[k].T, axis=0, keepdims=True) for k in range(chunks)]
    both = jnp.concatenate(sums + [roll0_ref[...] + roll1_ref[...]], axis=0)
    for i in range(sums_ref.shape[0]):
        sums_ref[i] = both
    for m in range(chunks // 2):
        copy_out(m).wait()


def shards(
    x_values, b_values, c_values, z_values, time_steps, decay_rate, skip_gain,
    conv_x, conv_bc, norm_gain, rollout, seq_spans,
):
    ring = lax.axis_size("seq")
    rows, width = x_values.shape
    heads = decay_rate.shape[0]
    chunks = rows // CHUNK
    blocks = width // LANES
    rank = lax.axis_index("seq").astype(jnp.int32).reshape(1)

    ends = width + 2 * STATE
    smem = pl.BlockSpec(memory_space=pltpu.SMEM)

    def whole(*shape):
        return pl.BlockSpec(shape, lambda i: (0,) * len(shape))

    def lane_block(r, first=0):
        return pl.BlockSpec((r, LANES), lambda i: (0, first + i))

    def grant(mib):
        return pltpu.CompilerParams(vmem_limit_bytes=mib * 1024 * 1024)

    def in_hbm(*arrays):
        return [pltpu.with_memory_space_constraint(v, pltpu.HBM) for v in arrays]

    x_values, b_values, c_values, z_values, rollout = in_hbm(x_values, b_values, c_values, z_values, rollout)
    (seq_spans,) = in_hbm(seq_spans)
    steps_row, rate_row, skip_row, gain_row, conv_x, conv_bc = in_hbm(
        time_steps.T, decay_rate.reshape(1, heads), skip_gain.reshape(1, heads), norm_gain.reshape(1, width), conv_x, conv_bc
    )
    last = rows // HALO - 1
    vmem = pl.BlockSpec(memory_space=pltpu.VMEM)
    hbm = pl.BlockSpec(memory_space=pl.ANY)
    edge, b_near, steps_near, rate_near, taps, keeps = pl.pallas_call(
        functools.partial(tail_kernel, chunks),
        grid=(1,),
        in_specs=[smem, smem]
        + [pl.BlockSpec((HALO, n), lambda i: (last, 0)) for n in (width, STATE, STATE)]
        + [whole(rows, STATE), whole(heads, rows), whole(1, heads), whole(CONV_K, width), whole(2, CONV_K, STATE)],
        out_specs=[
            whole(HALO, ends), whole(rows, STATE), whole(heads, rows), whole(1, heads), whole(8, width + STATE), whole(8, 128),
        ],
        out_shape=[
            jax.ShapeDtypeStruct((HALO, ends), BF16),
            pltpu.VMEM((rows, STATE), BF16),
            pltpu.VMEM((heads, rows), F32),
            pltpu.VMEM((1, heads), F32),
            pltpu.VMEM((8, width + STATE), F32),
            pltpu.VMEM((8, 128), F32),
        ],
        compiler_params=grant(8),
        name="tails",
    )(seq_spans, rank, x_values, b_values, c_values, b_values, steps_row, rate_row, conv_x, conv_bc)
    edge = lax.ppermute(edge, "seq", [(i, i + 1) for i in range(ring - 1)])
    conv_scratch = pltpu.VMEM((8, 8 + CHUNK, 128), F32)
    wide_scratch = pltpu.VMEM((rows, LANES), F32)

    end, head_scale, chain, head = pl.pallas_call(
        functools.partial(state_kernel, chunks),
        in_specs=[hbm] + [vmem] * 5,
        out_specs=[vmem] * 4,
        out_shape=[
            jax.ShapeDtypeStruct((STATE, width), F32),
            jax.ShapeDtypeStruct((HALO, width), F32),
            jax.ShapeDtypeStruct((8, width), F32),
            jax.ShapeDtypeStruct((HALO, width + STATE), BF16),
        ],
        scratch_shapes=[
            pltpu.VMEM((blocks, rows, LANES), BF16),
            conv_scratch,
            pltpu.VMEM((CHUNK, 128), F32),
            pltpu.VMEM((rows, 256), BF16),
            pltpu.VMEM((blocks, rows, LANES), F32),
            pltpu.VMEM((STATE, rows), BF16),
            pltpu.VMEM((blocks, rows, LANES), BF16),
            pltpu.SemaphoreType.DMA((blocks,)),
        ],
        compiler_params=grant(16),
        cost_estimate=pl.CostEstimate(flops=1 << 29, bytes_accessed=4 << 20, transcendentals=1 << 20),
        name="states",
    )(x_values, b_near, steps_near, rate_near, taps, keeps)

    msg = pl.pallas_call(
        edge_kernel,
        out_shape=jax.ShapeDtypeStruct((ring * MSG, 128), BF16),
        scratch_shapes=[pltpu.VMEM((ring * MSG, 128), F32)],
        compiler_params=grant(8),
        name="edge_states",
    )(edge, head, taps, keeps, head_scale, end, chain)
    edge = pltpu.with_memory_space_constraint(edge, pltpu.VMEM)

    msg = msg.reshape(ring, MSG // 2, 2, 128)
    spread = lax.all_to_all(msg, "seq", split_axis=0, concat_axis=0, tiled=True).reshape(ring * MSG, 128)

    def mix(first, specs, operands, more_specs, more_shapes):
        half = blocks // 2
        place = pltpu.HBM if first == 0 else pltpu.VMEM
        return pl.pallas_call(
            functools.partial(mix_kernel, chunks, first * LANES),
            grid=(half,),
            in_specs=[
                smem, smem, lane_block(rows, first), lane_block(HALO, first), whole(heads, rows), whole(1, heads),
                lane_block(rows, first), lane_block(rows, first), lane_block(CONV_K, first), whole(1, heads),
            ]
            + specs,
            out_specs=[lane_block(rows), lane_block(rows), whole(chunks, CHUNK)] + more_specs,
            out_shape=[
                place((rows, half * LANES), BF16),
                place((rows, half * LANES), BF16),
                pltpu.HBM((chunks, CHUNK), F32),
            ]
            + more_shapes,
            scratch_shapes=[
                conv_scratch, wide_scratch, wide_scratch, pltpu.VMEM((rows, 128), F32), pltpu.VMEM((STATE, LANES), F32),
                pltpu.VMEM((rows, 256), BF16), pltpu.VMEM((rows, 256), BF16), pltpu.VMEM((chunks, 16, 128), F32),
                pltpu.VMEM((chunks, 16, LANES), F32),
            ],
            compiler_params=grant(32),
            cost_estimate=pl.CostEstimate(flops=1 << 30, bytes_accessed=9 << 20, transcendentals=1 << 20),
            name="mix_first" if first == 0 else "mix_second",
        )(
            seq_spans, rank, x_values, edge, steps_row, rate_row, z_values, rollout, conv_x,
            skip_row, *operands,
        )

    shared_specs = [whole(rows, 256), whole(chunks, STATE, CHUNK)]
    a0, f0, roll0, left, bt, cc = mix(
        0,
        [
            whole(rows, STATE), whole(rows, STATE), pl.BlockSpec((HALO, 2 * STATE), lambda i: (0, width // (2 * STATE))),
            whole(2, CONV_K, STATE),
        ],
        [b_values, c_values, edge, conv_bc],
        shared_specs + [whole(rows, STATE)],
        [
            pltpu.HBM((rows, 256), BF16),
            pltpu.HBM((chunks, STATE, CHUNK), BF16),
            pltpu.VMEM((rows, STATE), BF16),
        ],
    )
    a0, f0, roll0, left, bt = in_hbm(a0, f0, roll0, left, bt)
    cc = pltpu.with_memory_space_constraint(cc, pltpu.VMEM)
    a1, f1, roll1 = mix(blocks // 2, shared_specs, [left, bt], [], [])
    a1, f1 = (pltpu.with_memory_space_constraint(v, pltpu.VMEM) for v in (a1, f1))
    (roll1,) = in_hbm(roll1)

    entering = pl.pallas_call(
        scan_kernel,
        in_specs=[pl.BlockSpec(memory_space=pltpu.VMEM), pl.BlockSpec(memory_space=pl.ANY)],
        out_shape=jax.ShapeDtypeStruct((ring, 32, 128), BF16),
        scratch_shapes=[pltpu.VMEM((ring * MSG, 128), F32)],
        compiler_params=grant(8),
        name="scan",
    )(spread, roll0)
    entering = lax.all_to_all(entering, "seq", split_axis=0, concat_axis=0, tiled=True)

    group = lax.axis_size("head")
    normed, sums = pl.pallas_call(
        norm_kernel,
        in_specs=[vmem] * 4 + [hbm] * 6,
        out_specs=[hbm, vmem],
        out_shape=[pltpu.HBM((rows, width), BF16), jax.ShapeDtypeStruct((group, 2 * chunks, CHUNK), F32)],
        scratch_shapes=[pltpu.VMEM((2, CHUNK, width // 2), F32), pltpu.VMEM((rows, width // 2), F32)]
        + [pltpu.VMEM((rows, width // 2), BF16)] * 2
        + [pltpu.VMEM((rows, width), BF16)] * 2
        + [pltpu.VMEM((1, width), F32)]
        + [pltpu.VMEM((chunks, CHUNK), F32)] * 2
        + [pltpu.VMEM((chunks, CHUNK, 128), F32)]
        + [pltpu.SemaphoreType.DMA((3, 2))]
        + [pltpu.SemaphoreType.DMA((chunks // 2,)), pltpu.SemaphoreType.DMA((3,))],
        compiler_params=grant(24),
        cost_estimate=pl.CostEstimate(flops=1 << 28, bytes_accessed=8 << 20, transcendentals=1 << 10),
        name="norms",
    )(entering, a1, f1, cc, a0, f0, rollout, gain_row, roll0, roll1)

    sums = jnp.sum(lax.all_to_all(sums, "head", split_axis=0, concat_axis=0, tiled=True), axis=0)
    relative = jnp.sqrt(sums[:chunks] / (sums[chunks:] + 1e-06))
    return normed, relative.reshape(rows)


def solution(mesh):
    placed = (
        P("seq", "head"), P("seq", "head"), P("seq", "head"), P("seq", "head"), P("seq", "head"),
        P("head"), P("head"), P(None, "head"), P(None, None, "head"), P("head"), P("seq", "head"), P(),
    )
    return jax.shard_map(
        shards, mesh=mesh, in_specs=placed, out_specs=(P("seq", "head"), P("seq")), check_vma=False
    )
```

```python
import functools

import jax
import jax.numpy as jnp
from jax import lax
from jax.experimental import pallas as pl
from jax.experimental.pallas import tpu as pltpu
from jax.sharding import PartitionSpec as P

HEADS = 128
HEAD_DIM = 64
STATE = 128
GROUPS = 8
CONV_K = 4
SPAN = 256
CHUNK = 128
LANES = 256
HALO = 16
MSG = 34

F32 = jnp.float32
BF16 = jnp.bfloat16


def parts3(v):
    hi = v.astype(BF16)
    rest = v - hi.astype(F32)
    mid = rest.astype(BF16)
    low = (rest - mid.astype(F32)).astype(BF16)
    return hi, mid, low


def silu_half(h):
    return h + h * jnp.tanh(h)


def mm(a, b):
    return jnp.dot(a, b, preferred_element_type=F32)


def one_hot(lane0, width=LANES):
    r = lax.broadcasted_iota(jnp.int32, (256, width), 0)
    c = lax.broadcasted_iota(jnp.int32, (256, width), 1)
    return jnp.where((r & 127) == (c + lane0) // HEAD_DIM, 1.0, 0.0).astype(BF16)


def span_keep(seq_ref, span):
    start = seq_ref[0] * 0
    fresh = span == start
    for i in range(seq_ref.shape[0] - 1):
        start = start + seq_ref[i]
        fresh = fresh | (span == start)
    return jnp.where(fresh, 0.0, 1.0).astype(F32)


def conv_block(padded_ref, taps):
    rows = padded_ref.shape[0] - 8
    total = padded_ref[pl.ds(5, rows), :] * taps[0:1]
    for k in range(1, CONV_K):
        total = total + padded_ref[pl.ds(5 + k, rows), :] * taps[k : k + 1]
    return silu_half(total)


def conv_ordered(padded_ref, taps):
    per = CHUNK // 8
    shifted = {m: padded_ref[pl.ds(8 + m, 8, stride=per), :] for m in range(1 - CONV_K, per)}
    rows = []
    for j in range(per):
        total = shifted[j + 1 - CONV_K] * taps[0:1]
        for k in range(1, CONV_K):
            total = total + shifted[j + 1 - CONV_K + k] * taps[k : k + 1]
        rows.append(silu_half(total))
    return jnp.concatenate(rows, axis=0)


def turned(v, heads, chunk):
    turn = (128 - heads * chunk) % 128
    return pltpu.roll(v, turn, 1) if turn else v


def split2(v):
    hi = v.astype(BF16)
    return hi, (v - hi.astype(F32)).astype(BF16)


def stack_scales(source, heads, chunks, target):
    for k in range(chunks):
        hi, low = split2(turned(source, heads, k))
        target[k * CHUNK : (k + 1) * CHUNK, 0:128] = hi
        target[k * CHUNK : (k + 1) * CHUNK, 128:256] = low


def chunk_rates(ts_ref, rate_ref, chunks):
    steps = jnp.concatenate([ts_ref[:, k * CHUNK : (k + 1) * CHUNK] for k in range(chunks)], axis=0).T
    return steps, -steps * jnp.concatenate([rate_ref[...]] * chunks, axis=1)


def sum_rates(picks, rates):
    picks = picks.astype(BF16)
    r1, r2, r3 = parts3(rates)
    return mm(picks, r1) + (mm(picks, r2) + mm(picks, r3))


def spread_rows(v, e):
    n = v.shape[0]
    out = mm(jnp.concatenate(parts3(v), axis=0), e[0:128])
    return out[0:n] + (out[n : 2 * n] + out[2 * n : 3 * n])


def chunk_keeps(chunks, seq_ref, rank_ref):
    per_span = SPAN // CHUNK
    first = rank_ref[0] * (chunks // per_span)
    return [None if k % per_span else span_keep(seq_ref, first + k // per_span) for k in range(chunks)]


def fill_padded(padded_ref, src_ref, edge, k, lanes, keep):
    if k == 0:
        halo = edge
    else:
        halo = src_ref[k * CHUNK - HALO : k * CHUNK, lanes].astype(F32)[HALO - 8 :]
    padded_ref[0:8, :] = halo if keep is None else halo * keep
    padded_ref[8 : 8 + CHUNK, :] = src_ref[k * CHUNK : (k + 1) * CHUNK, lanes].astype(F32)


def tail_kernel(
    chunks, seq_ref, rank_ref, x_ref, b_ref, c_ref, b_all_ref, ts_ref, rate_ref, wx_ref, wbc_ref,
    tail_ref, b_out, ts_out, rate_out, taps_ref, keep_ref,
):
    width = x_ref.shape[1]
    tail_ref[:, 0:width] = x_ref[...]
    tail_ref[:, width : width + STATE] = b_ref[...]
    tail_ref[:, width + STATE : width + 2 * STATE] = c_ref[...]
    b_out[...] = b_all_ref[...]
    ts_out[...] = ts_ref[...]
    rate_out[...] = rate_ref[...]
    taps_ref[...] = jnp.zeros_like(taps_ref)
    taps_ref[0:CONV_K, 0:width] = wx_ref[...].astype(F32) * 0.5
    taps_ref[0:CONV_K, width : width + STATE] = wbc_ref[0].astype(F32) * 0.5
    keeps = [v for v in chunk_keeps(chunks, seq_ref, rank_ref) if v is not None]
    row = lax.broadcasted_iota(jnp.int32, (8, 128), 0)
    flags = jnp.ones((8, 128), F32)
    for i, keep in enumerate(keeps):
        flags = jnp.where(row == i, keep, flags)
    keep_ref[...] = flags


def state_kernel(
    chunks, x_hbm, b_ref, ts_ref, rate_ref, taps_ref, keep_ref,
    end_ref, head_scale_ref, chain_ref, head_ref,
    x_all, padded, order, lhsu, wide, bt, xs, x_sems,
):
    blocks = x_all.shape[0]
    width = blocks * LANES
    heads = ts_ref.shape[0]

    def x_copy(i):
        lanes = pl.ds(pl.multiple_of(i * LANES, LANES), LANES)
        return pltpu.make_async_copy(x_hbm.at[:, lanes], x_all.at[i], x_sems.at[i])

    def start(i, carry):
        x_copy(i).start()
        return carry

    lax.fori_loop(0, blocks, start, 0)
    steps, rates = chunk_rates(ts_ref, rate_ref, chunks)
    t = lax.broadcasted_iota(jnp.int32, (CHUNK + 16, CHUNK), 0)
    u = lax.broadcasted_iota(jnp.int32, (CHUNK + 16, CHUNK), 1)
    after = sum_rates(jnp.where((u > t) | (t >= CHUNK), 1.0, 0.0), rates)
    totals = after[CHUNK : CHUNK + 16]
    j = lax.broadcasted_iota(jnp.int32, (CHUNK, CHUNK), 0)
    k = lax.broadcasted_iota(jnp.int32, (CHUNK, CHUNK), 1)
    later = jnp.where((lax.rem(j, heads) == lax.rem(k, heads)) & (j > k), 1.0, 0.0).astype(BF16)
    t1, t2, t3 = parts3(totals)
    later = mm(t1, later) + (mm(t2, later) + mm(t3, later))
    lane = lax.broadcasted_iota(jnp.int32, (16, 128), 1)
    reached = jnp.ones((16, 128), F32)
    whole = jnp.exp(later + totals)
    for n in range(0, chunks, SPAN // CHUNK):
        keep = keep_ref[n * CHUNK // SPAN : n * CHUNK // SPAN + 1, :]
        reached = jnp.where(lane < n * heads, reached * keep, reached)
        whole = whole * keep
    scale = jnp.exp(after[0:CHUNK] + later[0:1]) * steps * reached[0:1]
    order[...] = scale
    per = CHUNK // 8
    stack_scales(jnp.concatenate([order[pl.ds(n, 8, stride=per), :] for n in range(per)], axis=0), heads, chunks, lhsu)
    e = one_hot(0, width)
    wide_all = mm(lhsu[...], e)
    for i in range(blocks):
        wide[i] = wide_all[:, i * LANES : (i + 1) * LANES]
    head_scale_ref[...] = mm(jnp.concatenate(split2(scale[0:HALO]), axis=1), e)
    row = lax.broadcasted_iota(jnp.int32, (16, 1), 0)
    hi, low = split2(whole)
    p = jnp.where(row == 0, hi.astype(F32), jnp.where(row == 1, low.astype(F32), 0.0))
    chain_ref[...] = mm(p.astype(BF16), e[0:128])[0:8]
    taps = taps_ref[0:CONV_K, width : width + STATE]
    none = jnp.zeros((8, 128), F32)

    per_span = SPAN // CHUNK
    keeps = [None if k % per_span else keep_ref[k // per_span : k // per_span + 1, :] for k in range(chunks)]
    for k in range(chunks):
        pad = padded.at[k % 8]
        fill_padded(pad, b_ref, none, k, slice(0, STATE), keeps[k])
        v = conv_ordered(pad, taps)
        if k == 0:
            v = jnp.where((lax.broadcasted_iota(jnp.int32, v.shape, 0) & 7) == 0, 0.0, v)
        bt[:, k * CHUNK : (k + 1) * CHUNK] = v.T.astype(BF16)
    head_ref[:, width : width + STATE] = b_ref[0:HALO, :]

    def block(i, carry):
        lane0 = pl.multiple_of(i * LANES, LANES)
        lanes = pl.ds(lane0, LANES)
        x_ref = x_all.at[i]
        weights = taps_ref[0:CONV_K, lanes]
        x_copy(i).wait()
        head_ref[:, lanes] = x_ref[0:HALO, :]

        for k in range(chunks):
            toks = slice(k * CHUNK, (k + 1) * CHUNK)
            for part in range(LANES // 128):
                cols = slice(part * 128, (part + 1) * 128)
                pad = padded.at[(2 * k + part) % 8]
                fill_padded(pad, x_ref, none, k, cols, keeps[k])
                v = conv_ordered(pad, weights[:, cols])
                xs[i, toks, cols] = (v * wide[i, toks, cols]).astype(BF16)
        return carry

    lax.fori_loop(0, blocks, block, 0)
    for i in range(blocks):
        end_ref[:, i * LANES : (i + 1) * LANES] = mm(bt[...], xs[i])


def edge_kernel(edge_ref, head_ref, taps_ref, keep_ref, scale_ref, end_ref, chain_ref, msg_ref, flat):
    width = end_ref.shape[1]
    b_cols = slice(width, width + STATE)

    def conv(cols):
        taps = taps_ref[:, cols]
        before = edge_ref[:, cols].astype(F32)[HALO - 8 :] * keep_ref[0:1, 0:1]
        joined = jnp.concatenate([before, head_ref[:, cols].astype(F32)], axis=0)
        total = joined[5 : 5 + HALO] * taps[0:1]
        for k in range(1, CONV_K):
            total = total + joined[5 + k : 5 + k + HALO] * taps[k : k + 1]
        return silu_half(total)

    bc = conv(b_cols)
    bt = jnp.concatenate([bc, jnp.zeros((STATE - HALO, STATE), F32)], axis=0).T[:, 0:HALO].astype(BF16)

    for i in range(width // LANES):
        cols = slice(i * LANES, (i + 1) * LANES)
        v = conv(cols)
        xs = (v * scale_ref[:, cols]).astype(BF16)
        state = end_ref[:, cols] + mm(bt, xs)
        decay = chain_ref[0 : MSG - 32, cols]
        for part in range(LANES // 128):
            block = slice(part * 128, (part + 1) * 128)
            for nb in range(4):
                first = MSG * ((i * (LANES // 128) + part) * 4 + nb)
                flat[first : first + 32, :] = state[nb * 32 : (nb + 1) * 32, block]
                flat[first + 32 : first + MSG, :] = decay[:, block]
    msg_ref[...] = flat[...].astype(BF16)


def scan_kernel(in_ref, after_ref, out_ref, flat):
    flat[...] = in_ref[...].astype(F32)
    carried = jnp.zeros((32, 128), F32)
    for i in range(out_ref.shape[0]):
        first = MSG * i
        out_ref[i] = carried.astype(BF16)
        decay = flat[first + 32 : first + 33, :] + flat[first + 33 : first + 34, :]
        carried = carried * decay + flat[first : first + 32, :]


def mix_first(chunks, seq_ref, rank_ref, b_ref, c_ref, edge_ref, wbc_ref, left, bt, cc_ref, padded):
    t = lax.broadcasted_iota(jnp.int32, (CHUNK, CHUNK), 0)
    u = lax.broadcasted_iota(jnp.int32, (CHUNK, CHUNK), 1)
    edges = edge_ref[...].astype(F32)[HALO - 8 :]

    keeps = chunk_keeps(chunks, seq_ref, rank_ref)
    for k in range(chunks):
        toks = slice(k * CHUNK, (k + 1) * CHUNK)
        pair = []
        for i, ref in enumerate((b_ref, c_ref)):
            pad = padded.at[(2 * k + i) % 8]
            fill_padded(pad, ref, edges[:, i * STATE : (i + 1) * STATE], k, slice(0, STATE), keeps[k])
            pair.append(conv_block(pad, wbc_ref[i].astype(F32) * 0.5))
        b, c = pair
        bt[k] = b.T.astype(BF16)
        c = c.astype(BF16)
        cc_ref[toks, :] = c
        left[toks, 128:256] = c
        g = lax.dot_general(c, b.astype(BF16), (((1,), (1,)), ((), ())), preferred_element_type=F32)
        left[toks, 0:128] = jnp.where(u <= t, g, 0.0).astype(BF16)


def mix_kernel(
    chunks, lane_first, seq_ref, rank_ref, x_ref, edge_ref, ts_ref, rate_ref, z_ref, roll_ref, wx_ref, skip_ref, *refs
):
    if lane_first == 0:
        b_ref, c_ref, bc_edge_ref, wbc_ref, a_ref, f_ref, roll_sum_ref, left, bt, cc_ref = refs[:10]
    else:
        left, bt, a_ref, f_ref, roll_sum_ref = refs[:5]
    padded, wide_u, wide_t, part, state, lhsu, lhst, ends_all, rows = refs[-9:]
    heads = skip_ref.shape[1]

    @pl.when(pl.program_id(0) == 0)
    def _():
        if lane_first == 0:
            mix_first(chunks, seq_ref, rank_ref, b_ref, c_ref, bc_edge_ref, wbc_ref, left, bt, cc_ref, padded)
        steps, rates = chunk_rates(ts_ref, rate_ref, chunks)
        t = lax.broadcasted_iota(jnp.int32, (CHUNK + 16, CHUNK), 0)
        u = lax.broadcasted_iota(jnp.int32, (CHUNK + 16, CHUNK), 1)
        half = jnp.where(u < CHUNK // 2, 1.0, 0.0)
        tri = jnp.where(u <= t, 1.0, 0.0) - half
        cum = sum_rates(jnp.where(t < CHUNK, tri, jnp.where(t == CHUNK, half, 1.0)), rates)
        rel = cum[:CHUNK]
        stack_scales(jnp.exp(-rel) * steps, heads, chunks, lhsu)
        stack_scales(jnp.exp(rel), heads, chunks, lhst)
        ends = jnp.exp(jnp.concatenate([rel[CHUNK - 8 :], cum[CHUNK : CHUNK + 8]], axis=0))
        for k in range(chunks):
            ends_all[k] = turned(ends, heads, k)
        part[...] = jnp.zeros_like(part)

    e = one_hot(lane_first + pl.program_id(0) * LANES)
    rows[...] = spread_rows(ends_all[...].reshape(16 * chunks, 128), e).reshape(chunks, 16, LANES)
    wide_u[...] = mm(lhsu[...], e)
    wide_t[...] = mm(lhst[...], e)
    s1, s2, s3 = parts3(skip_ref[...])
    skip = mm(jnp.concatenate([s1.astype(F32), s2.astype(F32), s3.astype(F32)], axis=0).astype(BF16), e[0:heads])
    skip = skip[0:1] + (skip[1:2] + skip[2:3])
    state[...] = jnp.zeros_like(state)
    edges = edge_ref[...].astype(F32)[HALO - 8 :]
    weights = wx_ref[...].astype(F32) * 0.5

    keeps = chunk_keeps(chunks, seq_ref, rank_ref)
    reach = jnp.ones((1, LANES), F32)
    for k in range(chunks):
        toks = slice(k * CHUNK, (k + 1) * CHUNK)
        to_end, to_mid, whole = rows[k, 7:8, :], rows[k, 8:9, :], rows[k, 9:10, :]
        xs, direct = [], []
        for lane in range(0, LANES, 128):
            cols = slice(lane, lane + 128)
            pad = padded.at[(2 * k + lane // 128) % 8]
            fill_padded(pad, x_ref, edges[:, cols], k, cols, keeps[k])
            v = conv_block(pad, weights[:, cols])
            xs.append((v * wide_u[toks, cols]).astype(BF16))
            direct.append(v.astype(BF16).astype(F32) * skip[:, cols])
        xs, direct = jnp.concatenate(xs, axis=1), jnp.concatenate(direct, axis=1)
        before = state[...]
        if keeps[k] is not None:
            before = before * keeps[k]
            reach = reach * keeps[k]
        state[...] = before * whole + mm(bt[k], xs) * to_end
        right = jnp.concatenate([xs, (before * to_mid).astype(BF16)], axis=0)
        inner = mm(left[toks, :], right)
        scale = wide_t[toks, :]
        gate = silu_half(z_ref[toks, :].astype(F32) * 0.5)
        a_ref[toks, :] = ((inner * scale + direct) * gate).astype(BF16)
        f_ref[toks, :] = (scale * gate * (reach * to_mid)).astype(BF16)
        r = roll_ref[toks, :].astype(F32)
        r = r * r
        part[toks, :] += r[:, 0:128] + r[:, 128:256]
        reach = reach * whole

    @pl.when(pl.program_id(0) == pl.num_programs(0) - 1)
    def _():
        for k in range(chunks):
            roll_sum_ref[k : k + 1, :] = jnp.sum(part[k * CHUNK : (k + 1) * CHUNK, :].T, axis=0, keepdims=True)


def norm_kernel(
    in_ref, a1_all, f1_all, cc_ref, a0_hbm, f0_hbm, roll_hbm, gain_hbm, roll0_hbm, roll1_hbm, out_hbm, sums_ref,
    gated, gated_near, a0_all, f0_all, roll_all, out_all, gain_ref, roll0_ref, roll1_ref, parts,
    in_sems, out_sems, small_sems,
):
    width = out_all.shape[1]
    chunks, half = out_all.shape[0] // CHUNK, a0_all.shape[1]
    pairs = [(a0_hbm, a0_all), (f0_hbm, f0_all), (roll_hbm, roll_all)]
    smalls = [(gain_hbm, gain_ref), (roll0_hbm, roll0_ref), (roll1_hbm, roll1_ref)]
    size = 2 * CHUNK

    rows = out_all.shape[0] // 2

    def copy_in(i, m):
        here = pl.ds(pl.multiple_of(m * rows, rows), rows)
        return pltpu.make_async_copy(pairs[i][0].at[here], pairs[i][1].at[here], in_sems.at[i, m])

    def copy_out(m):
        here = pl.ds(pl.multiple_of(m * size, size), size)
        return pltpu.make_async_copy(out_all.at[here], out_hbm.at[here], out_sems.at[m])

    def copy_small(i):
        return pltpu.make_async_copy(*smalls[i], small_sems.at[i])

    for m in range(2):
        for i in range(len(pairs)):
            copy_in(i, m).start()
        if m == 0:
            for i in range(len(smalls)):
                copy_small(i).start()
    def gate(k, lanes, a_ref, f_ref, put, squares):
        toks = pl.ds(pl.multiple_of(k * CHUNK, CHUNK), CHUNK)
        first = lanes[0]
        for lane in lanes:
            own = [in_ref[lb * 4 : lb * 4 + 4].reshape(STATE, 128) for lb in range(lane // 128, (lane + LANES) // 128)]
            q = mm(cc_ref[toks, :], jnp.concatenate(own, axis=1))
            for part in range(0, LANES, 128):
                cols = slice(lane - first + part, lane - first + part + 128)
                g = a_ref[toks, cols].astype(F32) + f_ref[toks, cols].astype(F32) * q[:, part : part + 128]
                put(cols, g)
                squares = squares + g * g
        return squares

    def near(m, carry):
        for n in range(4):
            k = 4 * m + n
            toks = pl.ds(pl.multiple_of(k * CHUNK, CHUNK), CHUNK)

            def put(cols, g):
                gated_near[toks, cols] = g

            parts[k] = gate(k, range(half, width, LANES), a1_all, f1_all, put, jnp.zeros((CHUNK, 128), F32))
        return carry

    lax.fori_loop(0, chunks // 4, near, 0)
    for i in range(len(smalls)):
        copy_small(i).wait()

    def two(m, carry):
        scales = []
        for n in range(2):

            def put(cols, g):
                gated[n, :, cols] = g

            squares = gate(2 * m + n, range(0, half, LANES), a0_all, f0_all, put, parts[2 * m + n])
            mean = jnp.sum(squares, axis=1, keepdims=True) * (1.0 / width)
            scales.append(lax.rsqrt(mean + 1e-05))
        for n in range(2):
            k = 2 * m + n
            toks = pl.ds(pl.multiple_of(k * CHUNK, CHUNK), CHUNK)
            squares = jnp.zeros((CHUNK, 128), F32)
            for lane in range(0, width, 128):
                cols = slice(lane, lane + 128)
                g = gated[n, :, cols] if lane < half else gated_near[toks, lane - half : lane - half + 128]
                v = (g * scales[n] * gain_ref[:, cols]).astype(BF16)
                out_all[toks, cols] = v
                d = v.astype(F32) - roll_all[toks, cols].astype(F32)
                squares = squares + d * d
            parts[k] = squares
        copy_out(m).start()
        return carry

    def block(h, carry):
        for i in range(len(pairs)):
            copy_in(i, h).wait()
        return lax.fori_loop(h * (chunks // 4), (h + 1) * (chunks // 4), two, carry)

    lax.fori_loop(0, 2, block, 0)
    sums = [jnp.sum(parts[k].T, axis=0, keepdims=True) for k in range(chunks)]
    both = jnp.concatenate(sums + [roll0_ref[...] + roll1_ref[...]], axis=0)
    for i in range(sums_ref.shape[0]):
        sums_ref[i] = both
    for m in range(chunks // 2):
        copy_out(m).wait()


def shards(
    x_values, b_values, c_values, z_values, time_steps, decay_rate, skip_gain,
    conv_x, conv_bc, norm_gain, rollout, seq_spans,
):
    ring = lax.axis_size("seq")
    rows, width = x_values.shape
    heads = decay_rate.shape[0]
    chunks = rows // CHUNK
    blocks = width // LANES
    rank = lax.axis_index("seq").astype(jnp.int32).reshape(1)

    ends = width + 2 * STATE
    smem = pl.BlockSpec(memory_space=pltpu.SMEM)

    def whole(*shape):
        return pl.BlockSpec(shape, lambda i: (0,) * len(shape))

    def lane_block(r, first=0):
        return pl.BlockSpec((r, LANES), lambda i: (0, first + i))

    def grant(mib):
        return pltpu.CompilerParams(vmem_limit_bytes=mib * 1024 * 1024)

    def in_hbm(*arrays):
        return [pltpu.with_memory_space_constraint(v, pltpu.HBM) for v in arrays]

    x_values, b_values, c_values, z_values, rollout = in_hbm(x_values, b_values, c_values, z_values, rollout)
    (seq_spans,) = in_hbm(seq_spans)
    steps_row, rate_row, skip_row, gain_row, conv_x, conv_bc = in_hbm(
        time_steps.T, decay_rate.reshape(1, heads), skip_gain.reshape(1, heads), norm_gain.reshape(1, width), conv_x, conv_bc
    )
    last = rows // HALO - 1
    vmem = pl.BlockSpec(memory_space=pltpu.VMEM)
    hbm = pl.BlockSpec(memory_space=pl.ANY)
    edge, b_near, steps_near, rate_near, taps, keeps = pl.pallas_call(
        functools.partial(tail_kernel, chunks),
        grid=(1,),
        in_specs=[smem, smem]
        + [pl.BlockSpec((HALO, n), lambda i: (last, 0)) for n in (width, STATE, STATE)]
        + [whole(rows, STATE), whole(heads, rows), whole(1, heads), whole(CONV_K, width), whole(2, CONV_K, STATE)],
        out_specs=[
            whole(HALO, ends), whole(rows, STATE), whole(heads, rows), whole(1, heads), whole(8, width + STATE), whole(8, 128),
        ],
        out_shape=[
            jax.ShapeDtypeStruct((HALO, ends), BF16),
            pltpu.VMEM((rows, STATE), BF16),
            pltpu.VMEM((heads, rows), F32),
            pltpu.VMEM((1, heads), F32),
            pltpu.VMEM((8, width + STATE), F32),
            pltpu.VMEM((8, 128), F32),
        ],
        compiler_params=grant(8),
        name="tails",
    )(seq_spans, rank, x_values, b_values, c_values, b_values, steps_row, rate_row, conv_x, conv_bc)
    edge = lax.ppermute(edge, "seq", [(i, i + 1) for i in range(ring - 1)])
    conv_scratch = pltpu.VMEM((8, 8 + CHUNK, 128), F32)
    wide_scratch = pltpu.VMEM((rows, LANES), F32)

    end, head_scale, chain, head = pl.pallas_call(
        functools.partial(state_kernel, chunks),
        in_specs=[hbm] + [vmem] * 5,
        out_specs=[vmem] * 4,
        out_shape=[
            jax.ShapeDtypeStruct((STATE, width), F32),
            jax.ShapeDtypeStruct((HALO, width), F32),
            jax.ShapeDtypeStruct((8, width), F32),
            jax.ShapeDtypeStruct((HALO, width + STATE), BF16),
        ],
        scratch_shapes=[
            pltpu.VMEM((blocks, rows, LANES), BF16),
            conv_scratch,
            pltpu.VMEM((CHUNK, 128), F32),
            pltpu.VMEM((rows, 256), BF16),
            pltpu.VMEM((blocks, rows, LANES), F32),
            pltpu.VMEM((STATE, rows), BF16),
            pltpu.VMEM((blocks, rows, LANES), BF16),
            pltpu.SemaphoreType.DMA((blocks,)),
        ],
        compiler_params=grant(16),
        cost_estimate=pl.CostEstimate(flops=1 << 29, bytes_accessed=4 << 20, transcendentals=1 << 20),
        name="states",
    )(x_values, b_near, steps_near, rate_near, taps, keeps)

    msg = pl.pallas_call(
        edge_kernel,
        out_shape=jax.ShapeDtypeStruct((ring * MSG, 128), BF16),
        scratch_shapes=[pltpu.VMEM((ring * MSG, 128), F32)],
        compiler_params=grant(8),
        name="edge_states",
    )(edge, head, taps, keeps, head_scale, end, chain)
    edge = pltpu.with_memory_space_constraint(edge, pltpu.VMEM)

    msg = msg.reshape(ring, MSG // 2, 2, 128)
    spread = lax.all_to_all(msg, "seq", split_axis=0, concat_axis=0, tiled=True).reshape(ring * MSG, 128)

    def mix(first, specs, operands, more_specs, more_shapes):
        half = blocks // 2
        place = pltpu.HBM if first == 0 else pltpu.VMEM
        return pl.pallas_call(
            functools.partial(mix_kernel, chunks, first * LANES),
            grid=(half,),
            in_specs=[
                smem, smem, lane_block(rows, first), lane_block(HALO, first), whole(heads, rows), whole(1, heads),
                lane_block(rows, first), lane_block(rows, first), lane_block(CONV_K, first), whole(1, heads),
            ]
            + specs,
            out_specs=[lane_block(rows), lane_block(rows), whole(chunks, CHUNK)] + more_specs,
            out_shape=[
                place((rows, half * LANES), BF16),
                place((rows, half * LANES), BF16),
                pltpu.HBM((chunks, CHUNK), F32),
            ]
            + more_shapes,
            scratch_shapes=[
                conv_scratch, wide_scratch, wide_scratch, pltpu.VMEM((rows, 128), F32), pltpu.VMEM((STATE, LANES), F32),
                pltpu.VMEM((rows, 256), BF16), pltpu.VMEM((rows, 256), BF16), pltpu.VMEM((chunks, 16, 128), F32),
                pltpu.VMEM((chunks, 16, LANES), F32),
            ],
            compiler_params=grant(32),
            cost_estimate=pl.CostEstimate(flops=1 << 30, bytes_accessed=9 << 20, transcendentals=1 << 20),
            name="mix_first" if first == 0 else "mix_second",
        )(
            seq_spans, rank, x_values, edge, steps_row, rate_row, z_values, rollout, conv_x,
            skip_row, *operands,
        )

    shared_specs = [whole(rows, 256), whole(chunks, STATE, CHUNK)]
    a0, f0, roll0, left, bt, cc = mix(
        0,
        [
            whole(rows, STATE), whole(rows, STATE), pl.BlockSpec((HALO, 2 * STATE), lambda i: (0, width // (2 * STATE))),
            whole(2, CONV_K, STATE),
        ],
        [b_values, c_values, edge, conv_bc],
        shared_specs + [whole(rows, STATE)],
        [
            pltpu.HBM((rows, 256), BF16),
            pltpu.HBM((chunks, STATE, CHUNK), BF16),
            pltpu.VMEM((rows, STATE), BF16),
        ],
    )
    a0, f0, roll0, left, bt = in_hbm(a0, f0, roll0, left, bt)
    cc = pltpu.with_memory_space_constraint(cc, pltpu.VMEM)
    a1, f1, roll1 = mix(blocks // 2, shared_specs, [left, bt], [], [])
    a1, f1 = (pltpu.with_memory_space_constraint(v, pltpu.VMEM) for v in (a1, f1))
    (roll1,) = in_hbm(roll1)

    entering = pl.pallas_call(
        scan_kernel,
        in_specs=[pl.BlockSpec(memory_space=pltpu.VMEM), pl.BlockSpec(memory_space=pl.ANY)],
        out_shape=jax.ShapeDtypeStruct((ring, 32, 128), BF16),
        scratch_shapes=[pltpu.VMEM((ring * MSG, 128), F32)],
        compiler_params=grant(8),
        name="scan",
    )(spread, roll0)
    entering = lax.all_to_all(entering, "seq", split_axis=0, concat_axis=0, tiled=True)

    group = lax.axis_size("head")
    normed, sums = pl.pallas_call(
        norm_kernel,
        in_specs=[vmem] * 4 + [hbm] * 6,
        out_specs=[hbm, vmem],
        out_shape=[pltpu.HBM((rows, width), BF16), jax.ShapeDtypeStruct((group, 2 * chunks, CHUNK), F32)],
        scratch_shapes=[pltpu.VMEM((2, CHUNK, width // 2), F32), pltpu.VMEM((rows, width // 2), F32)]
        + [pltpu.VMEM((rows, width // 2), BF16)] * 2
        + [pltpu.VMEM((rows, width), BF16)] * 2
        + [pltpu.VMEM((1, width), F32)]
        + [pltpu.VMEM((chunks, CHUNK), F32)] * 2
        + [pltpu.VMEM((chunks, CHUNK, 128), F32)]
        + [pltpu.SemaphoreType.DMA((3, 2))]
        + [pltpu.SemaphoreType.DMA((chunks // 2,)), pltpu.SemaphoreType.DMA((3,))],
        compiler_params=grant(24),
        cost_estimate=pl.CostEstimate(flops=1 << 28, bytes_accessed=8 << 20, transcendentals=1 << 10),
        name="norms",
    )(entering, a1, f1, cc, a0, f0, rollout, gain_row, roll0, roll1)

    sums = jnp.sum(lax.all_to_all(sums, "head", split_axis=0, concat_axis=0, tiled=True), axis=0)
    relative = jnp.sqrt(sums[:chunks] / (sums[chunks:] + 1e-06))
    return normed, relative.reshape(rows)


def solution(mesh):
    placed = (
        P("seq", "head"), P("seq", "head"), P("seq", "head"), P("seq", "head"), P("seq", "head"),
        P("head"), P("head"), P(None, "head"), P(None, None, "head"), P("head"), P("seq", "head"), P(),
    )
    return jax.shard_map(
        shards, mesh=mesh, in_specs=placed, out_specs=(P("seq", "head"), P("seq")), check_vma=False
    )
```
